32 devices in a mesh: groups: 2 (over x), role: 2 (over core), seq: 8 (over z, y).
Axes of the slice: x: 2, y: 2, z: 4, core: 2. Of those that a mesh axis runs over, the one named last changes fastest.
Arguments:
- kv_store: bfloat16 [2, 8192, 1024], P('role', ('groups', 'seq')), parts along dimension 1, may hold values from -6 to 6
- queries: bfloat16 [2, 256, 2, 4096], P('role', ('groups', 'seq')), parts along dimension 1, may hold values from -100 to 100
- step_kv: bfloat16 [256, 2, 1024], P(('groups', 'seq')), parts along dimension 0, may hold values from -6 to 6
- suffix_pages: int32 [256, 2], P(('groups', 'seq')), parts along dimension 0, may hold values from 0 to 31, as said below
- suffix_len: int32 [256], P(('groups', 'seq')), parts along dimension 0, may hold values from 2 to 32, as said below
- owner: int32 [256, 1], P(('groups', 'seq')), parts along dimension 0, may hold values from 0 to 7; in each aligned block of 16 rows (0 to 15, 16 to 31, ...) at most 4 rows name the same one
- parent_id: int32 [256], P(('groups', 'seq')), parts along dimension 0, may hold values from 0 to 1
- parent_pages: int32 [32, 16], P(('groups', 'seq')), parts along dimension 0, may hold values from 0 to 31, as said below
- parent_len: int32 [32], P(('groups', 'seq')), parts along dimension 0, may hold values from 1 to 256, as said below
Outputs:
- served: bfloat16 [2, 256, 2, 4096], P('role', ('groups', 'seq')), parts along dimension 1
The draws below stay inside these ranges and needn't reach their ends.
There are 2 independent parts, one for each index of `groups`. The reference program is written for one: setup_inputs(seed, part) draws one part's arguments, and reference() takes and returns one part's arrays. A program takes and returns all parts, laid end to end along the dimension named above; each array names one. Nothing has to cross between parts.
Inputs may be any that keep to these rules, and one draw needn't show every extreme that they name: `suffix_pages`: on each device the page lists of its 16 requests are disjoint and together name every page of its store once. `suffix_len`: the first request of every device has the full 32 tokens. Of the requests of one device at most 4 go to one owner, and some device sends 4 to one owner. `parent_pages`: on each device the page tables of its 2 parent slots are disjoint and together name every page of its store once. `parent_len`: the first parent slot of every device has the full 256 tokens.
All inputs are finite; a program needn't handle non-finite values.
Results may differ from the reference program's by a relative error of at most 0.0025.
Values may be sent and summed in bfloat16 or wider, within the bound.
No kernel may reach another device: no remote copies, remote signals or barrier semaphores. Data moves between devices by JAX's collectives and lax.ppermute only.
A program may use at most 128 MiB of HBM per device.

```python
import math
import jax
import jax.numpy as jnp
import numpy as np
from jax import lax

HEAD_DIM = 128
KV_HEADS = 4
GROUP = 8
PAGE = 16
SUF_PAGES = 2
REQ_DEV = 16
PARENTS = 2
QW = 4096
KVW = 1024
SUF = 32
STORE_PAGES = 32
PAR_PAGES = 16
PCTX = 256
CAP = 4
REQUESTS = 128
PAR_ALL = 16
N_SEQ = 8


def shared_draws(key):
    key_store = jax.random.fold_in(key, 101)
    key_query = jax.random.fold_in(key, 102)
    key_step = jax.random.fold_in(key, 103)
    key_pages = jax.random.fold_in(key, 104)
    devices = REQUESTS // REQ_DEV
    page_store = jnp.clip(jax.random.normal(key_store, (2, devices * STORE_PAGES * PAGE, KVW), jnp.float32), -6.0, 6.0)
    query_rows = jnp.clip(2.5 * jax.random.normal(key_query, (2, REQUESTS, 2, QW), jnp.float32), -15.0, 15.0)
    step_rows = jnp.clip(jax.random.normal(key_step, (REQUESTS, 2, KVW), jnp.float32), -6.0, 6.0)
    page_keys = jax.random.split(key_pages, devices)
    page_lists = jax.vmap(lambda subkey: jax.random.permutation(subkey, STORE_PAGES))(page_keys)
    page_lists = page_lists.reshape(REQUESTS, SUF_PAGES).astype(jnp.int32)
    return (page_store, query_rows, step_rows, page_lists)


def draw_kv_store(key, part):
    return shared_draws(key)[0].astype(jnp.bfloat16)


def draw_queries(key, part):
    return shared_draws(key)[1].astype(jnp.bfloat16)


def draw_step_kv(key, part):
    return shared_draws(key)[2].astype(jnp.bfloat16)


def draw_suffix_pages(key, part):
    return shared_draws(key)[3]


def draw_suffix_len(key, part):
    lengths = jax.random.randint(jax.random.fold_in(key, 201), (REQUESTS,), 2, SUF + 1, jnp.int32)
    return lengths.at[::REQ_DEV].set(SUF)


def draw_parent_pages(key, part):
    devices = REQUESTS // REQ_DEV
    page_keys = jax.random.split(jax.random.fold_in(key, 202), devices)
    page_lists = jax.vmap(lambda subkey: jax.random.permutation(subkey, STORE_PAGES))(page_keys)
    return page_lists.reshape(devices * PARENTS, PAR_PAGES).astype(jnp.int32)


def draw_parent_len(key, part):
    lengths = jax.random.randint(jax.random.fold_in(key, 203), (PAR_ALL,), 1, PCTX + 1, jnp.int32)
    return lengths.at[::PARENTS].set(PCTX)


def plant(values, stream_key, least, top_value):
    place = [jax.random.randint(jax.random.fold_in(stream_key, axis), (), 0, length) for axis, length in enumerate(values.shape)]
    longest = values.shape.index(max(values.shape))
    beside = place[:longest] + [(place[longest] + 1) % values.shape[longest]] + place[longest + 1:]
    return values.at[tuple(place)].set(least).at[tuple(beside)].set(top_value)


def routed_block(key, own, number, rows, number_of, top, reach, slope):
    sequence = jax.random.permutation(key, number_of)
    heavy_load, common = portions_of(number_of, rows * top, reach, slope, True), portions_of(number_of, rows * top, reach, slope, False)
    places = jnp.arange(number_of)

    def named(tallies, offset_by):
        used = int((tallies > 0).sum())
        fixed = max(1, used // 4)
        moved = fixed + (places - fixed + offset_by * (used - fixed)) % max(1, number_of - fixed)
        return jnp.zeros((number_of,), jnp.int32).at[sequence[jnp.where(places < fixed, places, moved)]].set(jnp.asarray(tallies, jnp.int32))

    tallies = jnp.where(number % 4 == 0, named(heavy_load, number // 4), named(common, number - number // 4 - 1))
    mixed = jax.random.permutation(jax.random.fold_in(own, 3), number_of)
    source_of, taker = mixed[0:number_of // 2 * 2:2], mixed[1:number_of // 2 * 2:2]
    room = jnp.minimum(tallies[source_of] - 1, reach - tallies[taker]) // 2
    room = jnp.where((source_of == sequence[0]) | (taker == sequence[0]) | (tallies[taker] == 0), 0, jnp.maximum(room, 0))
    moved = jax.random.randint(jax.random.fold_in(own, 4), (number_of // 2,), 0, 1 << 20) % (room + 1)
    tallies = tallies.at[source_of].add(-moved).at[taker].add(moved)
    members = jnp.searchsorted(jnp.cumsum(tallies), jnp.arange(rows * top), side="right").astype(jnp.int32)
    table = members.reshape(top, rows).T
    table = table[jax.random.permutation(jax.random.fold_in(own, 1), rows)]
    offset_by = jax.random.randint(jax.random.fold_in(own, 2), (rows, 1), 0, top)
    return jnp.take_along_axis(table, (jnp.arange(top)[None, :] + offset_by) % top, axis=1)


def portions_of(number_of, total, most, skew, full):
    portions = [(1 << 20) // math.isqrt(grade ** skew) + 1 for grade in range(1, number_of + 1)]
    largest = most if full else min(most, max(-(-total // number_of), total * portions[0] // sum(portions)))
    least = 1 if total - largest >= number_of - 1 else 0
    given, surplus = [largest] + [least] * (number_of - 1), total - largest - least * (number_of - 1)
    while surplus > 0:
        free = [i for i in range(1, number_of) if given[i] < largest] or [i for i in range(1, number_of) if given[i] < most]
        pool, budget = sum([portions[i] for i in free]), surplus
        for i in free:
            more = min(most - given[i], max(1, budget * portions[i] // pool), surplus)
            given[i] = given[i] + more
            surplus = surplus - more
    return np.array(given)


def setup_inputs(seed: int = 0, part: int = 0) -> dict:
    key_of = jax.random.split(jax.random.key(seed), 10)
    own_keys = jax.random.split(jax.random.fold_in(key_of[9], part), 10)
    kv_store = draw_kv_store(jax.random.fold_in(jax.random.fold_in(key_of[9], part), 71), part)
    queries = draw_queries(jax.random.fold_in(jax.random.fold_in(key_of[9], part), 71), part)
    step_kv = draw_step_kv(jax.random.fold_in(jax.random.fold_in(key_of[9], part), 71), part)
    suffix_pages = draw_suffix_pages(jax.random.fold_in(jax.random.fold_in(key_of[9], part), 71), part)
    suffix_len = draw_suffix_len(jax.random.fold_in(jax.random.fold_in(key_of[9], part), 71), part)
    owner_keys = jax.random.split(jax.random.fold_in(own_keys[5], 1), REQUESTS // REQ_DEV)
    owner_turns = jax.random.permutation(jax.random.fold_in(own_keys[5], 3), REQUESTS // REQ_DEV)
    owner = jax.vmap(lambda own, number: routed_block(jax.random.fold_in(own_keys[5], 2), own, number, REQ_DEV, N_SEQ, 1, CAP, 2))(owner_keys, owner_turns).reshape((REQUESTS, 1))
    parent_id = plant(jax.random.randint(own_keys[6], (REQUESTS,), 0, PARENTS), jax.random.fold_in(own_keys[6], 1), 0, PARENTS - 1).astype(jnp.int32)
    parent_pages = draw_parent_pages(jax.random.fold_in(jax.random.fold_in(key_of[9], part), 71), part)
    parent_len = draw_parent_len(jax.random.fold_in(jax.random.fold_in(key_of[9], part), 71), part)
    return dict(kv_store=kv_store, queries=queries, step_kv=step_kv, suffix_pages=suffix_pages, suffix_len=suffix_len, owner=owner, parent_id=parent_id, parent_pages=parent_pages, parent_len=parent_len)


MASKED_SCORE = -1e30


def heads_of(kv_rows):
    key_width = KV_HEADS * HEAD_DIM
    shape_head = kv_rows.shape[:-1] + (KV_HEADS, HEAD_DIM)
    return kv_rows[..., :key_width].reshape(shape_head), kv_rows[..., key_width:].reshape(shape_head)


def attend(query_rows, kv_rows, keep_mask):
    request_count = query_rows.shape[0]
    query_heads = query_rows.astype(jnp.float32).reshape(request_count, 2, KV_HEADS, GROUP, HEAD_DIM)
    key_rows, value_rows = heads_of(kv_rows.astype(jnp.float32))
    scores = jnp.einsum("rtgqh,rugh->rtgqu", query_heads, key_rows, precision=lax.Precision.HIGHEST) * HEAD_DIM ** -0.5
    scores = jnp.where(keep_mask[:, :, None, None, :], scores, MASKED_SCORE)
    row_max = jnp.max(scores, axis=-1, keepdims=True)
    exp_terms = jnp.exp(scores - row_max)
    row_total = jnp.sum(exp_terms, axis=-1)
    weights = lax.optimization_barrier(exp_terms.astype(jnp.bfloat16)).astype(jnp.float32)
    blended = jnp.einsum("rtgqu,rugh->rtgqh", weights, value_rows, precision=lax.Precision.HIGHEST)
    blended = blended / row_total[..., None]
    return blended.reshape(request_count, 2, -1).astype(jnp.bfloat16)


def reference(kv_store, queries, step_kv, suffix_pages, suffix_len, owner, parent_id, parent_pages, parent_len):
    page_span = PAGE * KVW
    fresh_store = kv_store[0].reshape(N_SEQ, STORE_PAGES, page_span)
    parent_store = kv_store[1].reshape(N_SEQ, STORE_PAGES, page_span)
    device = (jnp.arange(REQUESTS, dtype=jnp.int32) // REQ_DEV).astype(jnp.int32)
    suffix = fresh_store[device[:, None], suffix_pages].reshape(REQUESTS, SUF, KVW)
    positions = jnp.arange(SUF, dtype=jnp.int32)
    last_seen = suffix_len[:, None] - 2 + jnp.arange(2, dtype=jnp.int32)[None, :]
    keep_prefill = positions[None, None, :] <= last_seen[:, :, None]
    prefilled = attend(queries[0], suffix, keep_prefill)

    def one_device(device_index):
        first_row = (device_index * REQ_DEV).astype(jnp.int32)

        def take_rows(array):
            return lax.dynamic_slice_in_dim(array, first_row, REQ_DEV, 0)

        owner_seq = take_rows(owner)[:, 0]
        parent_slot = owner_seq * PARENTS + take_rows(parent_id)
        page_table = parent_pages[parent_slot]
        context = parent_store[owner_seq[:, None], page_table].reshape(REQ_DEV, PCTX, KVW)
        key_rows = jnp.concatenate([context, take_rows(suffix), take_rows(step_kv)], axis=1)
        keep_parent = jnp.arange(PCTX, dtype=jnp.int32)[None, :] < parent_len[parent_slot][:, None]
        keep_suffix = positions[None, :] < take_rows(suffix_len)[:, None]
        keep_step = jnp.arange(2, dtype=jnp.int32)[None, :] <= jnp.arange(2, dtype=jnp.int32)[:, None]
        keep_mask = jnp.concatenate([
            jnp.broadcast_to(keep_parent[:, None, :], (REQ_DEV, 2, PCTX)),
            jnp.broadcast_to(keep_suffix[:, None, :], (REQ_DEV, 2, SUF)),
            jnp.broadcast_to(keep_step[None, :, :], (REQ_DEV, 2, 2))], axis=2)
        return attend(take_rows(queries[1]), key_rows, keep_mask)

    decoded = lax.map(one_device, jnp.arange(N_SEQ, dtype=jnp.int32)).reshape(REQUESTS, 2, QW)
    return jnp.stack([prefilled, decoded])
```

```python
import functools

import jax
import jax.numpy as jnp
from jax import lax
from jax.experimental import pallas as pl
from jax.experimental.pallas import tpu as pltpu
from jax.sharding import PartitionSpec as P

HEAD_DIM = 128
KV_HEADS = 4
GROUP = 8
PAGE = 16
HEAD_ROWS = 2 * GROUP
KEY_WIDTH = KV_HEADS * HEAD_DIM
SCALE = HEAD_DIM ** (-0.5)
MASKED = -1e30
STAT_ROWS = 8
VMEM_BYTES = 48 * 1024 * 1024

NT = (((1,), (1,)), ((), ()))


def iota(shape, dim):
    return lax.broadcasted_iota(jnp.int32, shape, dim)


def slot_ranks(owner_ref, count):
    names = [owner_ref[r] for r in range(count)]
    ranks = []
    for r in range(count):
        rank = jnp.int32(0)
        for earlier in range(r):
            rank = rank + jnp.where(names[earlier] == names[r], 1, 0)
        ranks.append(rank)
    return names, ranks


def pack_kernel(cap, owner_ref, parent_ref, query_ref, out_ref, meta_ref):
    count = query_ref.shape[0]
    head_span = cap * HEAD_ROWS
    out_ref[...] = jnp.zeros_like(out_ref)
    meta_ref[...] = jnp.zeros_like(meta_ref)
    names, ranks = slot_ranks(owner_ref, count)
    row, lane = iota((16, HEAD_DIM), 0), iota((16, HEAD_DIM), 1)
    for r in range(count):
        d, rank = names[r], ranks[r]
        for g in range(KV_HEADS):
            start = pl.multiple_of(g * head_span + rank * HEAD_ROWS, HEAD_ROWS)
            out_ref[d, pl.ds(start, HEAD_ROWS), :] = query_ref[r, pl.ds(g * HEAD_ROWS, HEAD_ROWS), :]
        hit = (row == rank) & (lane == parent_ref[r])
        meta_ref[d] = jnp.where(hit, 1.0, meta_ref[d])
    out_ref[:, pl.ds(KV_HEADS * head_span, 16), :] = meta_ref[...].astype(jnp.bfloat16)


def parent_kernel(
    cap, chunk, pages_ref, len_ref, recv_ref, store_ref, out_ref, bias_ref
):
    parents, page_count = pages_ref.shape
    sources = recv_ref.shape[0]
    head_span = cap * HEAD_ROWS
    row, lane = iota((PAGE, HEAD_DIM), 0), iota((PAGE, HEAD_DIM), 1)
    for p in range(parents):
        for i in range(page_count):
            keep = (lane == p) & (row + i * PAGE < len_ref[p])
            start = pl.multiple_of(pages_ref[p, i] * PAGE, PAGE)
            bias_ref[pl.ds(start, PAGE), :] = jnp.where(keep, 0.0, MASKED).astype(jnp.bfloat16)

    def body(c, carry):
        base = c * chunk
        rows = chunk * head_span
        meta = recv_ref[pl.ds(base, chunk), pl.ds(KV_HEADS * head_span, 16), :].astype(jnp.float32)
        picks = [
            jnp.broadcast_to(meta[:, s : s + 1, :], (chunk, HEAD_ROWS, HEAD_DIM)) for s in range(cap)
        ]
        pick = jnp.concatenate(picks, axis=1).reshape(rows, HEAD_DIM).astype(jnp.bfloat16)
        stats = jnp.zeros((rows, HEAD_DIM), jnp.float32)
        lanes = iota((rows, HEAD_DIM), 1)
        for g in range(KV_HEADS):
            query = recv_ref[pl.ds(base, chunk), pl.ds(g * head_span, head_span), :].reshape(rows, HEAD_DIM)
            keys = store_ref[:, pl.ds(g * HEAD_DIM, HEAD_DIM)]
            values = store_ref[:, pl.ds(KEY_WIDTH + g * HEAD_DIM, HEAD_DIM)]
            scores = lax.dot_general(
                jnp.concatenate([query, pick], axis=1),
                jnp.concatenate([keys, bias_ref[...]], axis=1),
                NT,
                preferred_element_type=jnp.float32,
            ) * SCALE
            top = jnp.max(scores, axis=1, keepdims=True)
            terms = jnp.exp(scores - top)
            total = jnp.sum(terms, axis=1, keepdims=True)
            blended = jnp.dot(terms.astype(jnp.bfloat16), values, preferred_element_type=jnp.float32)
            out_ref[pl.ds(base, chunk), pl.ds(g * head_span, head_span), :] = blended.reshape(
                chunk, head_span, HEAD_DIM
            )
            stats = jnp.where(lanes == g, top, stats)
            stats = jnp.where(lanes == KV_HEADS + g, total, stats)
        flat = stats.T[:STAT_ROWS, :]
        for j in range(chunk):
            piece = flat[:, j * head_span : (j + 1) * head_span]
            if head_span < HEAD_DIM:
                piece = jnp.concatenate(
                    [piece, jnp.zeros((STAT_ROWS, HEAD_DIM - head_span), jnp.float32)], axis=1
                )
            out_ref[base + j, pl.ds(KV_HEADS * head_span, STAT_ROWS), :] = piece
        return carry

    lax.fori_loop(0, sources // chunk, body, 0, unroll=min(2, sources // chunk))


def fill_suffix_bias(pages_ref, len_ref, bias_ref, last_of):
    page_count, count = pages_ref.shape
    row, lane = iota((PAGE, HEAD_DIM), 0), iota((PAGE, HEAD_DIM), 1)
    for r in range(count):
        for i in range(page_count):
            keep = (lane // 2 == r) & (row + i * PAGE <= last_of(len_ref[r], lane % 2))
            start = pl.multiple_of(pages_ref[i, r] * PAGE, PAGE)
            bias_ref[pl.ds(start, PAGE), :] = jnp.where(keep, 0.0, MASKED).astype(jnp.bfloat16)


def own_pick(count):
    rows = count * HEAD_ROWS
    row, lane = iota((rows, HEAD_DIM), 0), iota((rows, HEAD_DIM), 1)
    return jnp.where(lane == (row // HEAD_ROWS) * 2 + row % 2, 1.0, 0.0).astype(jnp.bfloat16)


def prefill_kernel(pages_ref, len_ref, query_ref, store_ref, out_ref, bias_ref):
    count = query_ref.shape[0]
    rows = count * HEAD_ROWS
    fill_suffix_bias(pages_ref, len_ref, bias_ref, lambda length, t: length - 2 + t)
    pick = own_pick(count)
    for g in range(KV_HEADS):
        query = query_ref[:, pl.ds(g * HEAD_ROWS, HEAD_ROWS), :].reshape(rows, HEAD_DIM)
        keys = store_ref[:, pl.ds(g * HEAD_DIM, HEAD_DIM)]
        values = store_ref[:, pl.ds(KEY_WIDTH + g * HEAD_DIM, HEAD_DIM)]
        scores = lax.dot_general(
            jnp.concatenate([query, pick], axis=1),
            jnp.concatenate([keys, bias_ref[...]], axis=1),
            NT,
            preferred_element_type=jnp.float32,
        ) * SCALE
        terms = jnp.exp(scores - jnp.max(scores, axis=1, keepdims=True))
        total = jnp.sum(terms, axis=1, keepdims=True)
        blended = jnp.dot(terms.astype(jnp.bfloat16), values, preferred_element_type=jnp.float32)
        out_ref[:, pl.ds(g * HEAD_ROWS, HEAD_ROWS), :] = (
            (blended / total).astype(jnp.bfloat16).reshape(count, HEAD_ROWS, HEAD_DIM)
        )


def merge_kernel(
    cap, owner_ref, pages_ref, len_ref, back_ref, query_ref, store_ref, step_ref, out_ref,
    bias_ref, part_ref, stat_ref,
):
    count = query_ref.shape[0]
    rows = count * HEAD_ROWS
    head_span = cap * HEAD_ROWS
    fill_suffix_bias(pages_ref, len_ref, bias_ref, lambda length, t: length - 1)
    steps = 2 * count
    step_pad = -steps % HEAD_DIM
    key_row, lane = iota((steps + step_pad, HEAD_DIM), 0), iota((steps + step_pad, HEAD_DIM), 1)
    seen = (key_row // 2 == lane // 2) & (key_row % 2 <= lane % 2) & (key_row < steps)
    step_bias = jnp.where(seen, 0.0, MASKED).astype(jnp.bfloat16)
    pad = jnp.zeros((step_pad, HEAD_DIM), jnp.bfloat16)

    names, ranks = slot_ranks(owner_ref, count)
    for r in range(count):
        d, rank = names[r], ranks[r]
        for g in range(KV_HEADS):
            start = pl.multiple_of(g * head_span + rank * HEAD_ROWS, HEAD_ROWS)
            part_ref[g, pl.ds(r * HEAD_ROWS, HEAD_ROWS), :] = back_ref[d, pl.ds(start, HEAD_ROWS), :]
        tile = back_ref[d, pl.ds(KV_HEADS * head_span, STAT_ROWS), :]
        shift = lax.rem(HEAD_DIM - rank * HEAD_ROWS, HEAD_DIM)
        stat_ref[pl.ds(r * STAT_ROWS, STAT_ROWS), :] = pltpu.roll(tile, shift, 1)
    columns = stat_ref[...].T[:HEAD_ROWS, :]

    def column(k):
        return jnp.concatenate(
            [columns[:, r * STAT_ROWS + k : r * STAT_ROWS + k + 1] for r in range(count)], axis=0
        )

    def step_rows(c):
        return jnp.concatenate([step_ref[r, 2 * c : 2 * c + 2, :] for r in range(count)] + [pad], axis=0)

    pick = own_pick(count)
    for g in range(KV_HEADS):
        query = query_ref[:, pl.ds(g * HEAD_ROWS, HEAD_ROWS), :].reshape(rows, HEAD_DIM)
        query = jnp.concatenate([query, pick], axis=1)
        keys = jnp.concatenate([store_ref[:, pl.ds(g * HEAD_DIM, HEAD_DIM)], bias_ref[...]], axis=1)
        step_keys = jnp.concatenate([step_rows(g), step_bias], axis=1)
        values = store_ref[:, pl.ds(KEY_WIDTH + g * HEAD_DIM, HEAD_DIM)]
        step_values = step_rows(KV_HEADS + g)
        scores = lax.dot_general(query, keys, NT, preferred_element_type=jnp.float32) * SCALE
        step_scores = lax.dot_general(query, step_keys, NT, preferred_element_type=jnp.float32) * SCALE
        part_top, part_total = column(g), column(KV_HEADS + g)
        top = jnp.maximum(
            jnp.maximum(jnp.max(scores, axis=1, keepdims=True), jnp.max(step_scores, axis=1, keepdims=True)),
            part_top,
        )
        terms = jnp.exp(scores - top)
        step_terms = jnp.exp(step_scores - top)
        part_weight = jnp.exp(part_top - top)
        total = (
            jnp.sum(terms, axis=1, keepdims=True)
            + jnp.sum(step_terms, axis=1, keepdims=True)
            + part_weight * part_total
        )
        blended = jnp.dot(terms.astype(jnp.bfloat16), values, preferred_element_type=jnp.float32)
        blended = blended + jnp.dot(
            step_terms.astype(jnp.bfloat16), step_values, preferred_element_type=jnp.float32
        )
        blended = blended + part_weight * part_ref[g]
        out_ref[:, pl.ds(g * HEAD_ROWS, HEAD_ROWS), :] = (
            (blended / total).astype(jnp.bfloat16).reshape(count, HEAD_ROWS, HEAD_DIM)
        )


def call(kernel, out_shape, scalars, arrays, scratch):
    smem = pl.BlockSpec(memory_space=pltpu.SMEM)
    vmem = pl.BlockSpec(memory_space=pltpu.VMEM)
    return pl.pallas_call(
        kernel,
        out_shape=out_shape,
        in_specs=[smem] * len(scalars) + [vmem] * len(arrays),
        out_specs=vmem,
        scratch_shapes=scratch,
        compiler_params=pltpu.CompilerParams(vmem_limit_bytes=VMEM_BYTES),
    )(*scalars, *arrays)


def head_rows(tokens):
    count, pair, width = tokens.shape
    blocks = tokens.reshape(count, pair, width // HEAD_DIM, HEAD_DIM)
    return blocks.transpose(0, 2, 1, 3).reshape(count, -1, HEAD_DIM)


def local(
    kv_store, queries, step_kv, suffix_pages, suffix_len, owner, parent_id, parent_pages, parent_len
):
    decoding = lax.axis_index("role") == 1
    seq_count = lax.axis_size("seq")
    store = kv_store[0]
    count, pair, width = queries.shape[1:]
    cap = max(2, 2 * count // seq_count)
    head_span = cap * HEAD_ROWS
    chunk = max(1, 256 // head_span)
    query_rows = head_rows(queries[0])
    owner_of = owner.reshape(-1)
    suffix_table = suffix_pages.T
    token_rows = store.shape[0]

    suffix_store = lax.ppermute(store, "role", [(0, 1)])

    sent = jax.ShapeDtypeStruct((seq_count, KV_HEADS * head_span + 16, HEAD_DIM), jnp.bfloat16)
    answer = jax.ShapeDtypeStruct((seq_count, KV_HEADS * head_span + STAT_ROWS, HEAD_DIM), jnp.float32)
    result = jax.ShapeDtypeStruct(query_rows.shape, jnp.bfloat16)
    bias = pltpu.VMEM((token_rows, HEAD_DIM), jnp.bfloat16)

    def exchange(block):
        return lax.all_to_all(block, "seq", split_axis=0, concat_axis=0, tiled=True)

    def send_queries(query_rows):
        packed = call(
            functools.partial(pack_kernel, cap),
            sent,
            (owner_of, parent_id),
            (query_rows,),
            [pltpu.VMEM((seq_count, 16, HEAD_DIM), jnp.float32)],
        )
        return exchange(packed)

    received = lax.cond(
        decoding, send_queries, lambda query_rows: jnp.zeros(sent.shape, sent.dtype), query_rows
    )

    def decode(received, suffix_store, query_rows):
        parts = call(
            functools.partial(parent_kernel, cap, chunk),
            answer,
            (parent_pages, parent_len),
            (received, store),
            [bias],
        )
        back = exchange(parts)
        return call(
            functools.partial(merge_kernel, cap),
            result,
            (owner_of, suffix_table, suffix_len),
            (back, query_rows, suffix_store, head_rows(step_kv)),
            [
                bias,
                pltpu.VMEM((KV_HEADS, count * HEAD_ROWS, HEAD_DIM), jnp.float32),
                pltpu.VMEM((count * STAT_ROWS, HEAD_DIM), jnp.float32),
            ],
        )

    def prefill(received, suffix_store, query_rows):
        return call(
            prefill_kernel, result, (suffix_table, suffix_len), (query_rows, store), [bias]
        )

    served = lax.cond(decoding, decode, prefill, received, suffix_store, query_rows)
    served = served.reshape(count, width // HEAD_DIM, pair, HEAD_DIM).transpose(0, 2, 1, 3)
    return served.reshape(1, count, pair, width)


def solution(mesh):
    in_specs = (
        P("role", ("groups", "seq"), None),
        P("role", ("groups", "seq"), None, None),
        P(("groups", "seq"), None, None),
        P(("groups", "seq"), None),
        P(("groups", "seq")),
        P(("groups", "seq"), None),
        P(("groups", "seq")),
        P(("groups", "seq"), None),
        P(("groups", "seq")),
    )
    out_specs = P("role", ("groups", "seq"), None, None)
    return jax.shard_map(local, mesh=mesh, in_specs=in_specs, out_specs=out_specs, check_vma=False)
```

```python
import functools

import jax
import jax.numpy as jnp
from jax import lax
from jax.experimental import pallas as pl
from jax.experimental.pallas import tpu as pltpu
from jax.sharding import PartitionSpec as P

HEAD_DIM = 128
KV_HEADS = 4
GROUP = 8
PAGE = 16
HEAD_ROWS = 2 * GROUP
KEY_WIDTH = KV_HEADS * HEAD_DIM
SCALE = HEAD_DIM ** (-0.5)
MASKED = -1e30
STAT_ROWS = 4 * KV_HEADS
LOG_STEPS = 4.0
SCALE_STEPS = 128.0
VMEM_BYTES = 48 * 1024 * 1024

NT = (((1,), (1,)), ((), ()))


def iota(shape, dim):
    return lax.broadcasted_iota(jnp.int32, shape, dim)


def slot_ranks(owner_ref, count):
    names = [owner_ref[r] for r in range(count)]
    ranks = []
    for r in range(count):
        rank = jnp.int32(0)
        for earlier in range(r):
            rank = rank + jnp.where(names[earlier] == names[r], 1, 0)
        ranks.append(rank)
    return names, ranks


def pack_kernel(cap, owner_ref, parent_ref, query_ref, out_ref, meta_ref):
    count = query_ref.shape[0]
    head_span = cap * HEAD_ROWS
    out_ref[...] = jnp.zeros_like(out_ref)
    meta_ref[...] = jnp.zeros_like(meta_ref)
    names, ranks = slot_ranks(owner_ref, count)
    row = iota((16, HEAD_DIM), 0)
    for r in range(count):
        d, rank = names[r], ranks[r]
        for g in range(KV_HEADS):
            start = pl.multiple_of(g * head_span + rank * HEAD_ROWS, HEAD_ROWS)
            out_ref[d, pl.ds(start, HEAD_ROWS), :] = query_ref[r, pl.ds(g * HEAD_ROWS, HEAD_ROWS), :]
        meta_ref[d] = jnp.where(row == rank, parent_ref[r].astype(jnp.float32), meta_ref[d])
    out_ref[:, pl.ds(KV_HEADS * head_span, 16), :] = meta_ref[...].astype(jnp.bfloat16)


def two_codes(values, steps):
    scaled = values * steps
    whole = jnp.floor(scaled)
    rest = jnp.minimum(jnp.floor((scaled - whole) * 65536.0 + 0.5), 65535.0) - 32768.0
    return whole, rest


def from_codes(whole, rest, steps):
    return (whole + (rest + 32768.0) * (1.0 / 65536.0)) * (1.0 / steps)


def parent_kernel(cap, chunk, pages_ref, len_ref, recv_ref, store_ref, out_ref, key_ref, value_ref):
    parents, page_count = pages_ref.shape
    sources = recv_ref.shape[0]
    head_span = cap * HEAD_ROWS
    tokens = page_count * PAGE
    for p in range(parents):
        for i in range(page_count):
            start = pl.multiple_of(pages_ref[p, i] * PAGE, PAGE)
            page = store_ref[pl.ds(start, PAGE), :]
            for g in range(KV_HEADS):
                span = (g, pl.ds(i * PAGE, PAGE), pl.ds(p * HEAD_DIM, HEAD_DIM))
                key_ref[span] = page[:, g * HEAD_DIM : (g + 1) * HEAD_DIM]
                value_ref[span] = page[:, KEY_WIDTH + g * HEAD_DIM : KEY_WIDTH + (g + 1) * HEAD_DIM]

    rows = chunk * head_span
    lanes = iota((rows, HEAD_DIM), 1)
    positions = iota((rows, tokens), 1)

    def body(c, carry):
        base = c * chunk
        meta = recv_ref[pl.ds(base, chunk), pl.ds(KV_HEADS * head_span, 16), :].astype(jnp.float32)
        picks = [
            jnp.broadcast_to(meta[:, s : s + 1, :], (chunk, HEAD_ROWS, HEAD_DIM)) for s in range(cap)
        ]
        parent = jnp.concatenate(picks, axis=1).reshape(rows, HEAD_DIM)
        limit = jnp.full((rows, HEAD_DIM), len_ref[0], jnp.int32)
        for p in range(1, parents):
            limit = jnp.where(parent == p, len_ref[p], limit)
        limit = limit[:, :1]
        parent_low = parent.astype(jnp.bfloat16)
        stats = jnp.zeros((rows, HEAD_DIM), jnp.float32)
        for g in range(KV_HEADS):
            query = recv_ref[pl.ds(base, chunk), pl.ds(g * head_span, head_span), :].reshape(rows, HEAD_DIM)
            query = jnp.concatenate(
                [jnp.where(parent_low == p, query, jnp.zeros_like(query)) for p in range(parents)], axis=1
            )
            scores = lax.dot_general(query, key_ref[g], NT, preferred_element_type=jnp.float32) * SCALE
            scores = jnp.where(positions < limit, scores, MASKED)
            top = jnp.max(scores, axis=1, keepdims=True)
            terms = jnp.exp(scores - top)
            total = jnp.sum(terms, axis=1, keepdims=True)
            both = jnp.dot(terms.astype(jnp.bfloat16), value_ref[g], preferred_element_type=jnp.float32)
            blended = both[:, :HEAD_DIM]
            for p in range(1, parents):
                blended = jnp.where(parent == p, both[:, p * HEAD_DIM : (p + 1) * HEAD_DIM], blended)
            reach = jnp.maximum(jnp.max(jnp.abs(blended), axis=1, keepdims=True), 1e-30)
            coded = jnp.round(blended * (32767.0 / reach)).astype(jnp.int32).astype(jnp.int16)
            out_ref[pl.ds(base, chunk), pl.ds(g * head_span, head_span), :] = coded.reshape(
                chunk, head_span, HEAD_DIM
            )
            stats = jnp.where(lanes == g, top, stats)
            stats = jnp.where(lanes == KV_HEADS + g, total, stats)
            stats = jnp.where(lanes == 2 * KV_HEADS + g, reach, stats)
        flat = stats.T
        top, total, reach = (flat[k * KV_HEADS : (k + 1) * KV_HEADS, :] for k in range(3))
        codes = two_codes(top + jnp.log(total), LOG_STEPS) + two_codes(jnp.log2(reach / total), SCALE_STEPS)
        flat = jnp.concatenate(codes, axis=0).astype(jnp.int32).astype(jnp.int16)
        for j in range(chunk):
            piece = flat[:, j * head_span : (j + 1) * head_span]
            if head_span < HEAD_DIM:
                piece = jnp.concatenate(
                    [piece, jnp.zeros((STAT_ROWS, HEAD_DIM - head_span), jnp.int16)], axis=1
                )
            out_ref[base + j, pl.ds(KV_HEADS * head_span, STAT_ROWS), :] = piece
        return carry

    lax.fori_loop(0, sources // chunk, body, 0, unroll=min(2, sources // chunk))


def fill_suffix_bias(pages_ref, len_ref, bias_ref, last_of):
    page_count, count = pages_ref.shape
    row, lane = iota((PAGE, HEAD_DIM), 0), iota((PAGE, HEAD_DIM), 1)
    for r in range(count):
        for i in range(page_count):
            keep = (lane // 2 == r) & (row + i * PAGE <= last_of(len_ref[r], lane % 2))
            start = pl.multiple_of(pages_ref[i, r] * PAGE, PAGE)
            bias_ref[pl.ds(start, PAGE), :] = jnp.where(keep, 0.0, MASKED).astype(jnp.bfloat16)


def own_pick(count):
    rows = count * HEAD_ROWS
    row, lane = iota((rows, HEAD_DIM), 0), iota((rows, HEAD_DIM), 1)
    return jnp.where(lane == (row // HEAD_ROWS) * 2 + row % 2, 1.0, 0.0).astype(jnp.bfloat16)


def prefill_kernel(pages_ref, len_ref, query_ref, store_ref, out_ref, bias_ref):
    count = query_ref.shape[0]
    rows = count * HEAD_ROWS
    fill_suffix_bias(pages_ref, len_ref, bias_ref, lambda length, t: length - 2 + t)
    pick = own_pick(count)
    for g in range(KV_HEADS):
        query = query_ref[:, pl.ds(g * HEAD_ROWS, HEAD_ROWS), :].reshape(rows, HEAD_DIM)
        keys = store_ref[:, pl.ds(g * HEAD_DIM, HEAD_DIM)]
        values = store_ref[:, pl.ds(KEY_WIDTH + g * HEAD_DIM, HEAD_DIM)]
        scores = lax.dot_general(
            jnp.concatenate([query, pick], axis=1),
            jnp.concatenate([keys, bias_ref[...]], axis=1),
            NT,
            preferred_element_type=jnp.float32,
        ) * SCALE
        terms = jnp.exp(scores - jnp.max(scores, axis=1, keepdims=True))
        total = jnp.sum(terms, axis=1, keepdims=True)
        blended = jnp.dot(terms.astype(jnp.bfloat16), values, preferred_element_type=jnp.float32)
        out_ref[:, pl.ds(g * HEAD_ROWS, HEAD_ROWS), :] = (
            (blended / total).astype(jnp.bfloat16).reshape(count, HEAD_ROWS, HEAD_DIM)
        )


def local_kernel(pages_ref, len_ref, query_ref, store_ref, step_ref, out_ref, stat_ref, bias_ref):
    count = query_ref.shape[0]
    rows = count * HEAD_ROWS
    fill_suffix_bias(pages_ref, len_ref, bias_ref, lambda length, t: length - 1)
    steps = 2 * count
    step_pad = -steps % HEAD_DIM
    key_row, lane = iota((steps + step_pad, HEAD_DIM), 0), iota((steps + step_pad, HEAD_DIM), 1)
    seen = (key_row // 2 == lane // 2) & (key_row % 2 <= lane % 2) & (key_row < steps)
    step_bias = jnp.where(seen, 0.0, MASKED).astype(jnp.bfloat16)
    pad = jnp.zeros((step_pad, HEAD_DIM), jnp.bfloat16)

    def step_rows(c):
        return jnp.concatenate([step_ref[r, 2 * c : 2 * c + 2, :] for r in range(count)] + [pad], axis=0)

    pick = own_pick(count)
    lanes = iota((rows, HEAD_DIM), 1)
    stats = jnp.zeros((rows, HEAD_DIM), jnp.float32)
    for g in range(KV_HEADS):
        query = query_ref[:, pl.ds(g * HEAD_ROWS, HEAD_ROWS), :].reshape(rows, HEAD_DIM)
        query = jnp.concatenate([query, pick], axis=1)
        keys = jnp.concatenate([store_ref[:, pl.ds(g * HEAD_DIM, HEAD_DIM)], bias_ref[...]], axis=1)
        step_keys = jnp.concatenate([step_rows(g), step_bias], axis=1)
        values = store_ref[:, pl.ds(KEY_WIDTH + g * HEAD_DIM, HEAD_DIM)]
        step_values = step_rows(KV_HEADS + g)
        scores = lax.dot_general(query, keys, NT, preferred_element_type=jnp.float32) * SCALE
        step_scores = lax.dot_general(query, step_keys, NT, preferred_element_type=jnp.float32) * SCALE
        top = jnp.maximum(
            jnp.max(scores, axis=1, keepdims=True), jnp.max(step_scores, axis=1, keepdims=True)
        )
        terms = jnp.exp(scores - top)
        step_terms = jnp.exp(step_scores - top)
        total = jnp.sum(terms, axis=1, keepdims=True) + jnp.sum(step_terms, axis=1, keepdims=True)
        blended = jnp.dot(terms.astype(jnp.bfloat16), values, preferred_element_type=jnp.float32)
        blended = blended + jnp.dot(
            step_terms.astype(jnp.bfloat16), step_values, preferred_element_type=jnp.float32
        )
        out_ref[g] = blended
        stats = jnp.where(lanes == g, top, stats)
        stats = jnp.where(lanes == KV_HEADS + g, total, stats)
    stat_ref[...] = stats


def merge_kernel(cap, owner_ref, back_ref, own_ref, own_stat_ref, out_ref, part_ref, decoded_ref, stat_ref):
    count = out_ref.shape[0]
    head_span = cap * HEAD_ROWS
    codes = back_ref[:, pl.ds(KV_HEADS * head_span, STAT_ROWS), :].astype(jnp.int32).astype(jnp.float32)
    codes = [codes[:, k * KV_HEADS : (k + 1) * KV_HEADS, :] for k in range(4)]
    log_total = from_codes(codes[0], codes[1], LOG_STEPS)
    unit = jnp.exp2(from_codes(codes[2], codes[3], SCALE_STEPS)) * (1.0 / 32767.0)
    decoded_ref[...] = jnp.concatenate([log_total, unit], axis=1)

    names, ranks = slot_ranks(owner_ref, count)
    for r in range(count):
        d, rank = names[r], ranks[r]
        for g in range(KV_HEADS):
            start = pl.multiple_of(g * head_span + rank * HEAD_ROWS, HEAD_ROWS)
            coded = back_ref[d, pl.ds(start, HEAD_ROWS), :].astype(jnp.int32).astype(jnp.float32)
            part_ref[g, pl.ds(r * HEAD_ROWS, HEAD_ROWS), :] = coded
        shift = lax.rem(HEAD_DIM - rank * HEAD_ROWS, HEAD_DIM)
        stat_ref[pl.ds(r * 2 * KV_HEADS, 2 * KV_HEADS), :] = pltpu.roll(decoded_ref[d], shift, 1)
    columns = stat_ref[...].T[:HEAD_ROWS, :]

    def column(k):
        return jnp.concatenate(
            [columns[:, r * 2 * KV_HEADS + k : r * 2 * KV_HEADS + k + 1] for r in range(count)], axis=0
        )

    for g in range(KV_HEADS):
        part_top, unit = column(g), column(KV_HEADS + g)
        own_top = own_stat_ref[:, g : g + 1]
        own_total = own_stat_ref[:, KV_HEADS + g : KV_HEADS + g + 1]
        top = jnp.maximum(own_top, part_top)
        own_weight, part_weight = jnp.exp(own_top - top), jnp.exp(part_top - top)
        inverse = 1.0 / (own_weight * own_total + part_weight)
        merged = own_ref[g] * (own_weight * inverse) + part_ref[g] * (unit * part_weight * inverse)
        out_ref[:, pl.ds(g * HEAD_ROWS, HEAD_ROWS), :] = merged.astype(jnp.bfloat16).reshape(
            count, HEAD_ROWS, HEAD_DIM
        )


def call(kernel, out_shape, scalars, arrays, scratch, cost=None):
    smem = pl.BlockSpec(memory_space=pltpu.SMEM)
    vmem = pl.BlockSpec(memory_space=pltpu.VMEM)
    return pl.pallas_call(
        kernel,
        out_shape=out_shape,
        in_specs=[smem] * len(scalars) + [vmem] * len(arrays),
        out_specs=jax.tree.map(lambda _: vmem, out_shape),
        cost_estimate=cost,
        scratch_shapes=scratch,
        compiler_params=pltpu.CompilerParams(vmem_limit_bytes=VMEM_BYTES),
    )(*scalars, *arrays)


def head_rows(tokens):
    count, pair, width = tokens.shape
    blocks = tokens.reshape(count, pair, width // HEAD_DIM, HEAD_DIM)
    return blocks.transpose(0, 2, 1, 3).reshape(count, -1, HEAD_DIM)


def local(
    kv_store, queries, step_kv, suffix_pages, suffix_len, owner, parent_id, parent_pages, parent_len
):
    decoding = lax.axis_index("role") == 1
    seq_count = lax.axis_size("seq")
    store = kv_store[0]
    count, pair, width = queries.shape[1:]
    cap = max(2, 2 * count // seq_count)
    head_span = cap * HEAD_ROWS
    chunk = max(1, 256 // head_span)
    query_rows = head_rows(queries[0])
    owner_of = owner.reshape(-1)
    suffix_table = suffix_pages.T
    token_rows = store.shape[0]

    suffix_store = lax.ppermute(store, "role", [(0, 1), (1, 0)])

    sent = jax.ShapeDtypeStruct((seq_count, KV_HEADS * head_span + 16, HEAD_DIM), jnp.bfloat16)
    answer = jax.ShapeDtypeStruct((seq_count, KV_HEADS * head_span + STAT_ROWS, HEAD_DIM), jnp.int16)
    result = jax.ShapeDtypeStruct(query_rows.shape, jnp.bfloat16)
    bias = pltpu.VMEM((token_rows, HEAD_DIM), jnp.bfloat16)
    rows = count * HEAD_ROWS
    part = (KV_HEADS, rows, HEAD_DIM)

    def exchange(block):
        return lax.all_to_all(block, "seq", split_axis=0, concat_axis=0, tiled=True)

    def tokens_of(rows):
        return rows.reshape(count, width // HEAD_DIM, pair, HEAD_DIM).transpose(0, 2, 1, 3).reshape(
            1, count, pair, width
        )

    def send_queries(query_rows):
        packed = call(
            functools.partial(pack_kernel, cap),
            sent,
            (owner_of, parent_id),
            (query_rows,),
            [pltpu.VMEM((seq_count, 16, HEAD_DIM), jnp.float32)],
        )
        return exchange(packed)

    received = lax.cond(
        decoding, send_queries, lambda query_rows: jnp.zeros(sent.shape, sent.dtype), query_rows
    )

    def decode(received, suffix_store, query_rows):
        parents, page_count = parent_pages.shape
        beside = (KV_HEADS, page_count * PAGE, parents * HEAD_DIM)
        parts = call(
            functools.partial(parent_kernel, cap, chunk),
            answer,
            (parent_pages, parent_len),
            (received, store),
            [pltpu.VMEM(beside, jnp.bfloat16), pltpu.VMEM(beside, jnp.bfloat16)],
        )
        back = exchange(parts)
        own, own_stats = call(
            local_kernel,
            (jax.ShapeDtypeStruct(part, jnp.float32), jax.ShapeDtypeStruct((rows, HEAD_DIM), jnp.float32)),
            (suffix_table, suffix_len),
            (query_rows, suffix_store, head_rows(step_kv)),
            [bias],
            pl.CostEstimate(flops=1 << 31, bytes_accessed=1 << 22, transcendentals=1 << 20),
        )
        return tokens_of(
            call(
                functools.partial(merge_kernel, cap),
                result,
                (owner_of,),
                (back, own, own_stats),
                [
                    pltpu.VMEM(part, jnp.float32),
                    pltpu.VMEM((seq_count, 2 * KV_HEADS, HEAD_DIM), jnp.float32),
                    pltpu.VMEM((count * 2 * KV_HEADS, HEAD_DIM), jnp.float32),
                ],
            )
        )

    def prefill(received, suffix_store, query_rows):
        return tokens_of(
            call(prefill_kernel, result, (suffix_table, suffix_len), (query_rows, store), [bias])
        )

    return lax.cond(decoding, decode, prefill, received, suffix_store, query_rows)


def solution(mesh):
    in_specs = (
        P("role", ("groups", "seq"), None),
        P("role", ("groups", "seq"), None, None),
        P(("groups", "seq"), None, None),
        P(("groups", "seq"), None),
        P(("groups", "seq")),
        P(("groups", "seq"), None),
        P(("groups", "seq")),
        P(("groups", "seq"), None),
        P(("groups", "seq")),
    )
    out_specs = P("role", ("groups", "seq"), None, None)
    return jax.shard_map(local, mesh=mesh, in_specs=in_specs, out_specs=out_specs, check_vma=False)
```

```python
import functools

import jax
import jax.numpy as jnp
from jax import lax
from jax.experimental import pallas as pl
from jax.experimental.pallas import tpu as pltpu
from jax.sharding import PartitionSpec as P

HEAD_DIM = 128
KV_HEADS = 4
GROUP = 8
PAGE = 16
HEAD_ROWS = 2 * GROUP
KEY_WIDTH = KV_HEADS * HEAD_DIM
SCALE = HEAD_DIM ** (-0.5)
MASKED = -1e30
STAT_ROWS = 4 * KV_HEADS
LOG_STEPS = 4.0
SCALE_STEPS = 128.0
VMEM_BYTES = 48 * 1024 * 1024

NT = (((1,), (1,)), ((), ()))


def iota(shape, dim):
    return lax.broadcasted_iota(jnp.int32, shape, dim)


def slot_ranks(owner_ref, count):
    owner = owner_ref[...]
    names = [owner[0, r] for r in range(count)]
    ranks = []
    for r in range(count):
        rank = jnp.int32(0)
        for earlier in range(r):
            rank = rank + jnp.where(names[earlier] == names[r], 1, 0)
        ranks.append(rank)
    return names, ranks


def pack_kernel(cap, query_ref, owner_ref, parent_ref, *refs):
    tables, (out_ref, *copies), meta_ref = refs[: len(refs) // 2 - 1], refs[len(refs) // 2 - 1 : -1], refs[-1]
    for table, copy in zip((owner_ref, *tables), copies):
        copy[...] = table[...]
    parent = parent_ref[...]
    count = query_ref.shape[0]
    head_span = cap * HEAD_ROWS
    out_ref[...] = jnp.zeros_like(out_ref)
    meta_ref[...] = jnp.zeros_like(meta_ref)
    names, ranks = slot_ranks(owner_ref, count)
    row = iota((16, HEAD_DIM), 0)
    for r in range(count):
        d, rank = names[r], ranks[r]
        for g in range(KV_HEADS):
            start = pl.multiple_of(g * head_span + rank * HEAD_ROWS, HEAD_ROWS)
            out_ref[d, pl.ds(start, HEAD_ROWS), :] = query_ref[r, pl.ds(g * HEAD_ROWS, HEAD_ROWS), :]
        meta_ref[d] = jnp.where(row == rank, parent[0, r].astype(jnp.float32), meta_ref[d])
    out_ref[:, pl.ds(KV_HEADS * head_span, 16), :] = meta_ref[...].astype(jnp.bfloat16)


def idle_kernel(*refs):
    tables, (out_ref, *copies) = refs[: len(refs) // 2], refs[len(refs) // 2 :]
    out_ref[...] = jnp.zeros_like(out_ref)
    for table, copy in zip(tables, copies):
        copy[...] = table[...]


def two_codes(values, steps):
    scaled = values * steps
    whole = jnp.floor(scaled)
    rest = jnp.minimum(jnp.floor((scaled - whole) * 65536.0 + 0.5), 65535.0) - 32768.0
    return whole, rest


def from_codes(whole, rest, steps):
    return (whole + (rest + 32768.0) * (1.0 / 65536.0)) * (1.0 / steps)


def parent_kernel(cap, chunk, pages_ref, len_ref, recv_ref, store_ref, out_ref, key_ref, value_ref):
    parents, page_count = pages_ref.shape
    pages, lengths = pages_ref[...], len_ref[...]
    sources = recv_ref.shape[0]
    head_span = cap * HEAD_ROWS
    tokens = page_count * PAGE
    for p in range(parents):
        for i in range(page_count):
            start = pl.multiple_of(pages[p, i] * PAGE, PAGE)
            page = store_ref[pl.ds(start, PAGE), :]
            for g in range(KV_HEADS):
                span = (g, pl.ds(i * PAGE, PAGE), pl.ds(p * HEAD_DIM, HEAD_DIM))
                key_ref[span] = page[:, g * HEAD_DIM : (g + 1) * HEAD_DIM]
                value_ref[span] = page[:, KEY_WIDTH + g * HEAD_DIM : KEY_WIDTH + (g + 1) * HEAD_DIM]

    rows = chunk * head_span
    lanes = iota((rows, HEAD_DIM), 1)
    positions = iota((rows, tokens), 1)

    def body(c, carry):
        base = c * chunk
        meta = recv_ref[pl.ds(base, chunk), pl.ds(KV_HEADS * head_span, 16), :].astype(jnp.float32)
        picks = [
            jnp.broadcast_to(meta[:, s : s + 1, :], (chunk, HEAD_ROWS, HEAD_DIM)) for s in range(cap)
        ]
        parent = jnp.concatenate(picks, axis=1).reshape(rows, HEAD_DIM)
        limit = jnp.full((rows, HEAD_DIM), lengths[0, 0], jnp.int32)
        for p in range(1, parents):
            limit = jnp.where(parent == p, lengths[0, p], limit)
        limit = limit[:, :1]
        parent_low = parent.astype(jnp.bfloat16)
        stats = jnp.zeros((rows, HEAD_DIM), jnp.float32)
        for g in range(KV_HEADS):
            query = recv_ref[pl.ds(base, chunk), pl.ds(g * head_span, head_span), :].reshape(rows, HEAD_DIM)
            query = jnp.concatenate(
                [jnp.where(parent_low == p, query, jnp.zeros_like(query)) for p in range(parents)], axis=1
            )
            scores = lax.dot_general(query, key_ref[g], NT, preferred_element_type=jnp.float32) * SCALE
            scores = jnp.where(positions < limit, scores, MASKED)
            top = jnp.max(scores, axis=1, keepdims=True)
            terms = jnp.exp(scores - top)
            total = jnp.sum(terms, axis=1, keepdims=True)
            both = jnp.dot(terms.astype(jnp.bfloat16), value_ref[g], preferred_element_type=jnp.float32)
            blended = both[:, :HEAD_DIM]
            for p in range(1, parents):
                blended = jnp.where(parent == p, both[:, p * HEAD_DIM : (p + 1) * HEAD_DIM], blended)
            reach = jnp.maximum(jnp.max(jnp.abs(blended), axis=1, keepdims=True), 1e-30)
            coded = jnp.round(blended * (32767.0 / reach)).astype(jnp.int32).astype(jnp.int16)
            out_ref[pl.ds(base, chunk), pl.ds(g * head_span, head_span), :] = coded.reshape(
                chunk, head_span, HEAD_DIM
            )
            stats = jnp.where(lanes == g, top, stats)
            stats = jnp.where(lanes == KV_HEADS + g, total, stats)
            stats = jnp.where(lanes == 2 * KV_HEADS + g, reach, stats)
        flat = stats.T
        top, total, reach = (flat[k * KV_HEADS : (k + 1) * KV_HEADS, :] for k in range(3))
        codes = two_codes(top + jnp.log(total), LOG_STEPS) + two_codes(jnp.log2(reach / total), SCALE_STEPS)
        flat = jnp.concatenate(codes, axis=0).astype(jnp.int32).astype(jnp.int16)
        for j in range(chunk):
            piece = flat[:, j * head_span : (j + 1) * head_span]
            if head_span < HEAD_DIM:
                piece = jnp.concatenate(
                    [piece, jnp.zeros((STAT_ROWS, HEAD_DIM - head_span), jnp.int16)], axis=1
                )
            out_ref[base + j, pl.ds(KV_HEADS * head_span, STAT_ROWS), :] = piece
        return carry

    lax.fori_loop(0, sources // chunk, body, 0, unroll=min(2, sources // chunk))


def fill_suffix_bias(pages_ref, len_ref, bias_ref, last_of):
    page_count, count = pages_ref.shape
    pages, lengths = pages_ref[...], len_ref[...]
    row, lane = iota((PAGE, HEAD_DIM), 0), iota((PAGE, HEAD_DIM), 1)
    for r in range(count):
        for i in range(page_count):
            keep = (lane // 2 == r) & (row + i * PAGE <= last_of(lengths[0, r], lane % 2))
            start = pl.multiple_of(pages[i, r] * PAGE, PAGE)
            bias_ref[pl.ds(start, PAGE), :] = jnp.where(keep, 0.0, MASKED).astype(jnp.bfloat16)


def own_pick(count):
    rows = count * HEAD_ROWS
    row, lane = iota((rows, HEAD_DIM), 0), iota((rows, HEAD_DIM), 1)
    return jnp.where(lane == (row // HEAD_ROWS) * 2 + row % 2, 1.0, 0.0).astype(jnp.bfloat16)


def prefill_kernel(pages_ref, len_ref, query_ref, store_ref, out_ref, bias_ref):
    count = query_ref.shape[0]
    rows = count * HEAD_ROWS
    fill_suffix_bias(pages_ref, len_ref, bias_ref, lambda length, t: length - 2 + t)
    pick = own_pick(count)
    for g in range(KV_HEADS):
        query = query_ref[:, pl.ds(g * HEAD_ROWS, HEAD_ROWS), :].reshape(rows, HEAD_DIM)
        keys = store_ref[:, pl.ds(g * HEAD_DIM, HEAD_DIM)]
        values = store_ref[:, pl.ds(KEY_WIDTH + g * HEAD_DIM, HEAD_DIM)]
        scores = lax.dot_general(
            jnp.concatenate([query, pick], axis=1),
            jnp.concatenate([keys, bias_ref[...]], axis=1),
            NT,
            preferred_element_type=jnp.float32,
        ) * SCALE
        terms = jnp.exp(scores - jnp.max(scores, axis=1, keepdims=True))
        total = jnp.sum(terms, axis=1, keepdims=True)
        blended = jnp.dot(terms.astype(jnp.bfloat16), values, preferred_element_type=jnp.float32)
        out_ref[:, pl.ds(g * HEAD_ROWS, HEAD_ROWS), :] = (
            (blended / total).astype(jnp.bfloat16).reshape(count, HEAD_ROWS, HEAD_DIM)
        )


def local_kernel(pages_ref, len_ref, query_ref, store_ref, step_ref, out_ref, stat_ref, bias_ref):
    count = query_ref.shape[0]
    rows = count * HEAD_ROWS
    fill_suffix_bias(pages_ref, len_ref, bias_ref, lambda length, t: length - 1)
    steps = 2 * count
    step_pad = -steps % HEAD_DIM
    key_row, lane = iota((steps + step_pad, HEAD_DIM), 0), iota((steps + step_pad, HEAD_DIM), 1)
    seen = (key_row // 2 == lane // 2) & (key_row % 2 <= lane % 2) & (key_row < steps)
    step_bias = jnp.where(seen, 0.0, MASKED).astype(jnp.bfloat16)
    pad = jnp.zeros((step_pad, HEAD_DIM), jnp.bfloat16)

    def step_rows(c):
        return jnp.concatenate([step_ref[r, 2 * c : 2 * c + 2, :] for r in range(count)] + [pad], axis=0)

    pick = own_pick(count)
    lanes = iota((rows, HEAD_DIM), 1)
    stats = jnp.zeros((rows, HEAD_DIM), jnp.float32)
    for g in range(KV_HEADS):
        query = query_ref[:, pl.ds(g * HEAD_ROWS, HEAD_ROWS), :].reshape(rows, HEAD_DIM)
        query = jnp.concatenate([query, pick], axis=1)
        keys = jnp.concatenate([store_ref[:, pl.ds(g * HEAD_DIM, HEAD_DIM)], bias_ref[...]], axis=1)
        step_keys = jnp.concatenate([step_rows(g), step_bias], axis=1)
        values = store_ref[:, pl.ds(KEY_WIDTH + g * HEAD_DIM, HEAD_DIM)]
        step_values = step_rows(KV_HEADS + g)
        scores = lax.dot_general(query, keys, NT, preferred_element_type=jnp.float32) * SCALE
        step_scores = lax.dot_general(query, step_keys, NT, preferred_element_type=jnp.float32) * SCALE
        top = jnp.maximum(
            jnp.max(scores, axis=1, keepdims=True), jnp.max(step_scores, axis=1, keepdims=True)
        )
        terms = jnp.exp(scores - top)
        step_terms = jnp.exp(step_scores - top)
        total = jnp.sum(terms, axis=1, keepdims=True) + jnp.sum(step_terms, axis=1, keepdims=True)
        blended = jnp.dot(terms.astype(jnp.bfloat16), values, preferred_element_type=jnp.float32)
        blended = blended + jnp.dot(
            step_terms.astype(jnp.bfloat16), step_values, preferred_element_type=jnp.float32
        )
        out_ref[g] = blended
        stats = jnp.where(lanes == g, top, stats)
        stats = jnp.where(lanes == KV_HEADS + g, total, stats)
    stat_ref[...] = stats


def merge_kernel(cap, owner_ref, back_ref, own_ref, own_stat_ref, out_ref, part_ref, decoded_ref, stat_ref):
    count = out_ref.shape[0]
    head_span = cap * HEAD_ROWS
    codes = back_ref[:, pl.ds(KV_HEADS * head_span, STAT_ROWS), :].astype(jnp.int32).astype(jnp.float32)
    codes = [codes[:, k * KV_HEADS : (k + 1) * KV_HEADS, :] for k in range(4)]
    log_total = from_codes(codes[0], codes[1], LOG_STEPS)
    unit = jnp.exp2(from_codes(codes[2], codes[3], SCALE_STEPS)) * (1.0 / 32767.0)
    decoded_ref[...] = jnp.concatenate([log_total, unit], axis=1)

    names, ranks = slot_ranks(owner_ref, count)
    for r in range(count):
        d, rank = names[r], ranks[r]
        for g in range(KV_HEADS):
            start = pl.multiple_of(g * head_span + rank * HEAD_ROWS, HEAD_ROWS)
            coded = back_ref[d, pl.ds(start, HEAD_ROWS), :].astype(jnp.int32).astype(jnp.float32)
            part_ref[g, pl.ds(r * HEAD_ROWS, HEAD_ROWS), :] = coded
        shift = lax.rem(HEAD_DIM - rank * HEAD_ROWS, HEAD_DIM)
        stat_ref[pl.ds(r * 2 * KV_HEADS, 2 * KV_HEADS), :] = pltpu.roll(decoded_ref[d], shift, 1)
    columns = stat_ref[...].T[:HEAD_ROWS, :]

    def column(k):
        return jnp.concatenate(
            [columns[:, r * 2 * KV_HEADS + k : r * 2 * KV_HEADS + k + 1] for r in range(count)], axis=0
        )

    for g in range(KV_HEADS):
        part_top, unit = column(g), column(KV_HEADS + g)
        own_top = own_stat_ref[:, g : g + 1]
        own_total = own_stat_ref[:, KV_HEADS + g : KV_HEADS + g + 1]
        top = jnp.maximum(own_top, part_top)
        own_weight, part_weight = jnp.exp(own_top - top), jnp.exp(part_top - top)
        inverse = 1.0 / (own_weight * own_total + part_weight)
        merged = own_ref[g] * (own_weight * inverse) + part_ref[g] * (unit * part_weight * inverse)
        out_ref[:, pl.ds(g * HEAD_ROWS, HEAD_ROWS), :] = merged.astype(jnp.bfloat16).reshape(
            count, HEAD_ROWS, HEAD_DIM
        )


def call(kernel, out_shape, arrays, scratch, cost=None):
    vmem = pl.BlockSpec(memory_space=pltpu.VMEM)
    return pl.pallas_call(
        kernel,
        out_shape=out_shape,
        in_specs=[vmem] * len(arrays),
        out_specs=jax.tree.map(lambda _: vmem, out_shape),
        cost_estimate=cost,
        scratch_shapes=scratch,
        compiler_params=pltpu.CompilerParams(vmem_limit_bytes=VMEM_BYTES),
    )(*arrays)


def head_rows(tokens):
    count, pair, width = tokens.shape
    blocks = tokens.reshape(count, pair, width // HEAD_DIM, HEAD_DIM)
    return blocks.transpose(0, 2, 1, 3).reshape(count, -1, HEAD_DIM)


def local(
    kv_store, queries, step_kv, suffix_pages, suffix_len, owner, parent_id, parent_pages, parent_len
):
    decoding = lax.axis_index("role") == 1
    seq_count = lax.axis_size("seq")
    store = kv_store[0]
    count, pair, width = queries.shape[1:]
    cap = max(2, 2 * count // seq_count)
    head_span = cap * HEAD_ROWS
    chunk = max(1, 256 // head_span)
    query_rows = head_rows(queries[0])
    owner_row, parent_row = owner.reshape(1, -1), parent_id.reshape(1, -1)
    tables = (suffix_pages.T, suffix_len.reshape(1, -1), parent_pages, parent_len.reshape(1, -1))
    token_rows = store.shape[0]

    suffix_store = lax.ppermute(store, "role", [(0, 1), (1, 0)])

    sent = jax.ShapeDtypeStruct((seq_count, KV_HEADS * head_span + 16, HEAD_DIM), jnp.bfloat16)
    answer = jax.ShapeDtypeStruct((seq_count, KV_HEADS * head_span + STAT_ROWS, HEAD_DIM), jnp.int16)
    result = jax.ShapeDtypeStruct(query_rows.shape, jnp.bfloat16)
    bias = pltpu.VMEM((token_rows, HEAD_DIM), jnp.bfloat16)
    rows = count * HEAD_ROWS
    part = (KV_HEADS, rows, HEAD_DIM)

    def exchange(block):
        return lax.all_to_all(block, "seq", split_axis=0, concat_axis=0, tiled=True)

    def tokens_of(rows):
        return rows.reshape(count, width // HEAD_DIM, pair, HEAD_DIM).transpose(0, 2, 1, 3).reshape(
            1, count, pair, width
        )

    handed = (sent, *(jax.ShapeDtypeStruct(t.shape, t.dtype) for t in (owner_row, *tables)))

    def send_queries(query_rows):
        packed, *copies = call(
            functools.partial(pack_kernel, cap),
            handed,
            (query_rows, owner_row, parent_row, *tables),
            [pltpu.VMEM((seq_count, 16, HEAD_DIM), jnp.float32)],
        )
        return exchange(packed), *copies

    def idle(query_rows):
        return call(idle_kernel, handed, (owner_row, *tables), [])

    received = lax.cond(decoding, send_queries, idle, query_rows)

    def decode(received, suffix_store, query_rows):
        received, owner_row, suffix_table, suffix_lengths, parent_pages, parent_lengths = received
        parents, page_count = parent_pages.shape
        beside = (KV_HEADS, page_count * PAGE, parents * HEAD_DIM)
        parts = call(
            functools.partial(parent_kernel, cap, chunk),
            answer,
            (parent_pages, parent_lengths, received, store),
            [pltpu.VMEM(beside, jnp.bfloat16), pltpu.VMEM(beside, jnp.bfloat16)],
        )
        back = exchange(parts)
        own, own_stats = call(
            local_kernel,
            (jax.ShapeDtypeStruct(part, jnp.float32), jax.ShapeDtypeStruct((rows, HEAD_DIM), jnp.float32)),
            (suffix_table, suffix_lengths, query_rows, suffix_store, head_rows(step_kv)),
            [bias],
            pl.CostEstimate(flops=1 << 31, bytes_accessed=1 << 22, transcendentals=1 << 20),
        )
        return tokens_of(
            call(
                functools.partial(merge_kernel, cap),
                result,
                (owner_row, back, own, own_stats),
                [
                    pltpu.VMEM(part, jnp.float32),
                    pltpu.VMEM((seq_count, 2 * KV_HEADS, HEAD_DIM), jnp.float32),
                    pltpu.VMEM((count * 2 * KV_HEADS, HEAD_DIM), jnp.float32),
                ],
            )
        )

    def prefill(received, suffix_store, query_rows):
        return tokens_of(
            call(prefill_kernel, result, (*received[2:4], query_rows, store), [bias])
        )

    return lax.cond(decoding, decode, prefill, received, suffix_store, query_rows)


def solution(mesh):
    in_specs = (
        P("role", ("groups", "seq"), None),
        P("role", ("groups", "seq"), None, None),
        P(("groups", "seq"), None, None),
        P(("groups", "seq"), None),
        P(("groups", "seq")),
        P(("groups", "seq"), None),
        P(("groups", "seq")),
        P(("groups", "seq"), None),
        P(("groups", "seq")),
    )
    out_specs = P("role", ("groups", "seq"), None, None)
    return jax.shard_map(local, mesh=mesh, in_specs=in_specs, out_specs=out_specs, check_vma=False)
```

```python
import functools

import jax
import jax.numpy as jnp
from jax import lax
from jax.experimental import pallas as pl
from jax.experimental.pallas import tpu as pltpu
from jax.sharding import PartitionSpec as P

HEAD_DIM = 128
KV_HEADS = 4
GROUP = 8
PAGE = 16
HEAD_ROWS = 2 * GROUP
KEY_WIDTH = KV_HEADS * HEAD_DIM
SCALE = HEAD_DIM ** (-0.5)
MASKED = -1e30
STAT_ROWS = 4 * KV_HEADS
LOG_STEPS = 4.0
SCALE_STEPS = 128.0
CODE_TOP = 32600.0
LOG2_E = 1.4426950408889634
VMEM_BYTES = 48 * 1024 * 1024

NT = (((1,), (1,)), ((), ()))


def iota(shape, dim):
    return lax.broadcasted_iota(jnp.int32, shape, dim)


def slot_ranks(owner_ref, count):
    owner = owner_ref[...]
    names = [owner[0, r] for r in range(count)]
    ranks = []
    for r in range(count):
        rank = jnp.int32(0)
        for earlier in range(r):
            rank = rank + jnp.where(names[earlier] == names[r], 1, 0)
        ranks.append(rank)
    return names, ranks


def pack_kernel(cap, query_ref, owner_ref, parent_ref, *refs):
    tables, (out_ref, *copies), meta_ref = refs[: len(refs) // 2 - 1], refs[len(refs) // 2 - 1 : -1], refs[-1]
    for table, copy in zip((owner_ref, *tables), copies):
        copy[...] = table[...]
    parent = parent_ref[...]
    count = query_ref.shape[0]
    head_span = cap * HEAD_ROWS
    out_ref[...] = jnp.zeros_like(out_ref)
    meta_ref[...] = jnp.zeros_like(meta_ref)
    names, ranks = slot_ranks(owner_ref, count)
    row = iota((16, HEAD_DIM), 0)
    for r in range(count):
        d, rank = names[r], ranks[r]
        for g in range(KV_HEADS):
            start = pl.multiple_of(g * head_span + rank * HEAD_ROWS, HEAD_ROWS)
            out_ref[d, pl.ds(start, HEAD_ROWS), :] = query_ref[r, pl.ds(g * HEAD_ROWS, HEAD_ROWS), :]
        meta_ref[d] = jnp.where(row == rank, parent[0, r].astype(jnp.float32), meta_ref[d])
    out_ref[:, pl.ds(KV_HEADS * head_span, 16), :] = meta_ref[...].astype(jnp.bfloat16)


def idle_kernel(*refs):
    tables, (out_ref, *copies) = refs[: len(refs) // 2], refs[len(refs) // 2 :]
    out_ref[...] = jnp.zeros_like(out_ref)
    for table, copy in zip(tables, copies):
        copy[...] = table[...]


def two_codes(values, steps):
    scaled = values * steps
    whole = jnp.floor(scaled)
    rest = jnp.minimum(jnp.floor((scaled - whole) * 65536.0 + 0.5), 65535.0) - 32768.0
    return whole, rest


def from_codes(whole, rest, steps):
    return (whole + (rest + 32768.0) * (1.0 / 65536.0)) * (1.0 / steps)


def parent_kernel(
    cap, chunk, pages_ref, len_ref, recv_ref, store_ref, out_hbm, out_ref, key_ref, value_ref, sems
):
    parents, page_count = pages_ref.shape
    pages, lengths = pages_ref[...], len_ref[...]
    sources = recv_ref.shape[0]
    head_span = cap * HEAD_ROWS
    tokens = page_count * PAGE
    heads = range(KV_HEADS)
    for p in range(parents):
        for i in range(page_count):
            start = pl.multiple_of(pages[p, i] * PAGE, PAGE)
            page = store_ref[pl.ds(start, PAGE), :]
            for g in heads:
                span = (g, pl.ds(i * PAGE, PAGE), pl.ds(p * HEAD_DIM, HEAD_DIM))
                key_ref[span] = page[:, g * HEAD_DIM : (g + 1) * HEAD_DIM]
                value_ref[span] = page[:, KEY_WIDTH + g * HEAD_DIM : KEY_WIDTH + (g + 1) * HEAD_DIM]

    rows = chunk * head_span
    lanes = iota((rows, HEAD_DIM), 1)
    positions = iota((rows, tokens), 1)

    def put(c, k):
        part = (pl.ds(c * chunk, chunk), pl.ds(k * head_span, head_span if k < KV_HEADS else STAT_ROWS))
        return pltpu.make_async_copy(out_ref.at[part], out_hbm.at[part], sems.at[c, k])

    def body(c, carry):
        part = pl.ds(c * chunk, chunk)
        meta = recv_ref[part, pl.ds(KV_HEADS * head_span, 16), :].astype(jnp.float32)
        picks = [
            jnp.broadcast_to(meta[:, s : s + 1, :], (chunk, HEAD_ROWS, HEAD_DIM)) for s in range(cap)
        ]
        parent = jnp.concatenate(picks, axis=1).reshape(rows, HEAD_DIM)
        limit = jnp.full((rows, HEAD_DIM), lengths[0, 0], jnp.int32)
        for p in range(1, parents):
            limit = jnp.where(parent == p, lengths[0, p], limit)
        bias = jnp.where(positions < limit[:, :1], 0.0, MASKED)
        parent_low = parent.astype(jnp.bfloat16)

        def scores_of(g):
            query = recv_ref[part, pl.ds(g * head_span, head_span), :].reshape(rows, HEAD_DIM)
            query = jnp.concatenate(
                [jnp.where(parent_low == p, query, jnp.zeros_like(query)) for p in range(parents)], axis=1
            )
            return lax.dot_general(query, key_ref[g], NT, preferred_element_type=jnp.float32)

        def softmax_of(scores):
            scores = scores + bias
            top = jnp.max(scores, axis=1, keepdims=True)
            terms = jnp.exp2((scores - top) * (SCALE * LOG2_E))
            return terms.astype(jnp.bfloat16), top, jnp.sum(terms, axis=1, keepdims=True)

        def blended_of(g, weights):
            both = jnp.dot(weights, value_ref[g], preferred_element_type=jnp.float32)
            blended = both[:, :HEAD_DIM]
            for p in range(1, parents):
                blended = jnp.where(parent == p, both[:, p * HEAD_DIM : (p + 1) * HEAD_DIM], blended)
            return blended

        scores = [scores_of(g) for g in heads]
        softmaxes = [softmax_of(scores[g]) for g in heads]
        blends = [blended_of(g, softmaxes[g][0]) for g in heads]
        stats = jnp.zeros((rows, HEAD_DIM), jnp.float32)
        for g in heads:
            reach = jnp.maximum(jnp.max(jnp.abs(blends[g]), axis=1, keepdims=True), 1e-30)
            inverse = pltpu.reciprocal(reach, approx=True) * CODE_TOP
            coded = jnp.round(blends[g] * inverse).astype(jnp.int32).astype(jnp.int16)
            out_ref[part, pl.ds(g * head_span, head_span), :] = coded.reshape(chunk, head_span, HEAD_DIM)
            put(c, g).start()
            for k, value in enumerate((softmaxes[g][1], softmaxes[g][2], inverse)):
                stats = jnp.where(lanes == k * KV_HEADS + g, value, stats)
        flat = stats.T
        top, total, inverse = (flat[k * KV_HEADS : (k + 1) * KV_HEADS, :] for k in range(3))
        codes = two_codes(top * SCALE + jnp.log(total), LOG_STEPS)
        codes += two_codes(-jnp.log2(inverse * total), SCALE_STEPS)
        flat = jnp.concatenate(codes, axis=0).astype(jnp.int32).astype(jnp.int16)
        for j in range(chunk):
            piece = flat[:, j * head_span : (j + 1) * head_span]
            if head_span < HEAD_DIM:
                piece = jnp.concatenate(
                    [piece, jnp.zeros((STAT_ROWS, HEAD_DIM - head_span), jnp.int16)], axis=1
                )
            out_ref[c * chunk + j, pl.ds(KV_HEADS * head_span, STAT_ROWS), :] = piece
        put(c, KV_HEADS).start()
        return carry

    lax.fori_loop(0, sources // chunk, body, 0, unroll=sources == chunk)
    for c in range(sources // chunk):
        for k in range(KV_HEADS + 1):
            put(c, k).wait()


def fill_suffix_bias(pages_ref, len_ref, bias_ref, last_of):
    page_count, count = pages_ref.shape
    pages, lengths = pages_ref[...], len_ref[...]
    row, lane = iota((PAGE, HEAD_DIM), 0), iota((PAGE, HEAD_DIM), 1)
    for r in range(count):
        for i in range(page_count):
            keep = (lane // 2 == r) & (row + i * PAGE <= last_of(lengths[0, r], lane % 2))
            start = pl.multiple_of(pages[i, r] * PAGE, PAGE)
            bias_ref[pl.ds(start, PAGE), :] = jnp.where(keep, 0.0, MASKED).astype(jnp.bfloat16)


def own_pick(count):
    rows = count * HEAD_ROWS
    row, lane = iota((rows, HEAD_DIM), 0), iota((rows, HEAD_DIM), 1)
    return jnp.where(lane == (row // HEAD_ROWS) * 2 + row % 2, 1.0, 0.0).astype(jnp.bfloat16)


def prefill_kernel(pages_ref, len_ref, query_ref, store_ref, out_ref, bias_ref):
    count = query_ref.shape[0]
    rows = count * HEAD_ROWS
    fill_suffix_bias(pages_ref, len_ref, bias_ref, lambda length, t: length - 2 + t)
    pick = own_pick(count)
    for g in range(KV_HEADS):
        query = query_ref[:, pl.ds(g * HEAD_ROWS, HEAD_ROWS), :].reshape(rows, HEAD_DIM)
        keys = store_ref[:, pl.ds(g * HEAD_DIM, HEAD_DIM)]
        values = store_ref[:, pl.ds(KEY_WIDTH + g * HEAD_DIM, HEAD_DIM)]
        scores = lax.dot_general(
            jnp.concatenate([query, pick], axis=1),
            jnp.concatenate([keys, bias_ref[...]], axis=1),
            NT,
            preferred_element_type=jnp.float32,
        ) * SCALE
        terms = jnp.exp(scores - jnp.max(scores, axis=1, keepdims=True))
        total = jnp.sum(terms, axis=1, keepdims=True)
        blended = jnp.dot(terms.astype(jnp.bfloat16), values, preferred_element_type=jnp.float32)
        out_ref[:, pl.ds(g * HEAD_ROWS, HEAD_ROWS), :] = (
            (blended / total).astype(jnp.bfloat16).reshape(count, HEAD_ROWS, HEAD_DIM)
        )


def local_kernel(pages_ref, len_ref, query_ref, store_ref, step_ref, out_ref, stat_ref, bias_ref):
    count = query_ref.shape[0]
    rows = count * HEAD_ROWS
    fill_suffix_bias(pages_ref, len_ref, bias_ref, lambda length, t: length - 1)
    steps = 2 * count
    step_pad = -steps % HEAD_DIM
    key_row, lane = iota((steps + step_pad, HEAD_DIM), 0), iota((steps + step_pad, HEAD_DIM), 1)
    seen = (key_row // 2 == lane // 2) & (key_row % 2 <= lane % 2) & (key_row < steps)
    step_bias = jnp.where(seen, 0.0, MASKED).astype(jnp.bfloat16)
    pad = jnp.zeros((step_pad, HEAD_DIM), jnp.bfloat16)

    def step_rows(c):
        return jnp.concatenate([step_ref[r, 2 * c : 2 * c + 2, :] for r in range(count)] + [pad], axis=0)

    pick = own_pick(count)
    lanes = iota((rows, HEAD_DIM), 1)
    stats = jnp.zeros((rows, HEAD_DIM), jnp.float32)
    for g in range(KV_HEADS):
        query = query_ref[:, pl.ds(g * HEAD_ROWS, HEAD_ROWS), :].reshape(rows, HEAD_DIM)
        query = jnp.concatenate([query, pick], axis=1)
        keys = jnp.concatenate([store_ref[:, pl.ds(g * HEAD_DIM, HEAD_DIM)], bias_ref[...]], axis=1)
        step_keys = jnp.concatenate([step_rows(g), step_bias], axis=1)
        values = store_ref[:, pl.ds(KEY_WIDTH + g * HEAD_DIM, HEAD_DIM)]
        step_values = step_rows(KV_HEADS + g)
        scores = lax.dot_general(query, keys, NT, preferred_element_type=jnp.float32) * SCALE
        step_scores = lax.dot_general(query, step_keys, NT, preferred_element_type=jnp.float32) * SCALE
        top = jnp.maximum(
            jnp.max(scores, axis=1, keepdims=True), jnp.max(step_scores, axis=1, keepdims=True)
        )
        terms = jnp.exp(scores - top)
        step_terms = jnp.exp(step_scores - top)
        total = jnp.sum(terms, axis=1, keepdims=True) + jnp.sum(step_terms, axis=1, keepdims=True)
        blended = jnp.dot(terms.astype(jnp.bfloat16), values, preferred_element_type=jnp.float32)
        blended = blended + jnp.dot(
            step_terms.astype(jnp.bfloat16), step_values, preferred_element_type=jnp.float32
        )
        out_ref[g] = blended
        stats = jnp.where(lanes == g, top, stats)
        stats = jnp.where(lanes == KV_HEADS + g, total, stats)
    stat_ref[...] = stats.T[: 2 * KV_HEADS, :]


def merge_kernel(cap, owner_ref, back_ref, own_ref, own_stat_ref, out_ref, decoded_ref):
    count = out_ref.shape[0]
    rows = count * HEAD_ROWS
    head_span = cap * HEAD_ROWS
    codes = back_ref[:, pl.ds(KV_HEADS * head_span, STAT_ROWS), :].astype(jnp.int32).astype(jnp.float32)
    codes = [codes[:, k * KV_HEADS : (k + 1) * KV_HEADS, :] for k in range(4)]
    log_total = from_codes(codes[0], codes[1], LOG_STEPS)
    unit = jnp.exp2(from_codes(codes[2], codes[3], SCALE_STEPS))
    decoded_ref[...] = jnp.concatenate([log_total, unit], axis=1)

    names, ranks = slot_ranks(owner_ref, count)
    per_tile = HEAD_DIM // HEAD_ROWS
    place = iota((2 * KV_HEADS, HEAD_DIM), 1) // HEAD_ROWS
    tiles = []
    for first in range(0, count, per_tile):
        tile = jnp.zeros((2 * KV_HEADS, HEAD_DIM), jnp.float32)
        for r in range(first, min(first + per_tile, count)):
            shift = lax.rem((r - first) * HEAD_ROWS - ranks[r] * HEAD_ROWS + HEAD_DIM, HEAD_DIM)
            tile = jnp.where(place == r - first, pltpu.roll(decoded_ref[names[r]], shift, 1), tile)
        tiles.append(tile)
    flat = jnp.concatenate(tiles, axis=1)[:, :rows]
    part_top, unit = flat[:KV_HEADS], flat[KV_HEADS:]
    own_top, own_total = own_stat_ref[:KV_HEADS, :], own_stat_ref[KV_HEADS:, :]
    top = jnp.maximum(own_top, part_top)
    own_weight, part_weight = jnp.exp(own_top - top), jnp.exp(part_top - top)
    inverse = 1.0 / (own_weight * own_total + part_weight)
    weights = [own_weight * inverse, unit * part_weight * inverse]
    weights.append(jnp.zeros((HEAD_DIM - 2 * KV_HEADS, rows), jnp.float32))
    weights = jnp.concatenate(weights, axis=0).T
    for r in range(count):
        span = slice(r * HEAD_ROWS, (r + 1) * HEAD_ROWS)
        for g in range(KV_HEADS):
            start = pl.multiple_of(g * head_span + ranks[r] * HEAD_ROWS, HEAD_ROWS)
            part = back_ref[names[r], pl.ds(start, HEAD_ROWS), :].astype(jnp.int32).astype(jnp.float32)
            merged = own_ref[g, span, :] * weights[span, g : g + 1]
            merged = merged + part * weights[span, KV_HEADS + g : KV_HEADS + g + 1]
            out_ref[r, pl.ds(g * HEAD_ROWS, HEAD_ROWS), :] = merged.astype(jnp.bfloat16)


def call(kernel, out_shape, arrays, scratch, cost=None, out_space=pltpu.VMEM):
    vmem = pl.BlockSpec(memory_space=pltpu.VMEM)
    put = pl.BlockSpec(memory_space=out_space)
    return pl.pallas_call(
        kernel,
        out_shape=out_shape,
        in_specs=[vmem] * len(arrays),
        out_specs=jax.tree.map(lambda _: put, out_shape),
        cost_estimate=cost,
        scratch_shapes=scratch,
        compiler_params=pltpu.CompilerParams(vmem_limit_bytes=VMEM_BYTES),
    )(*arrays)


def head_rows(tokens):
    count, pair, width = tokens.shape
    blocks = tokens.reshape(count, pair, width // HEAD_DIM, HEAD_DIM)
    return blocks.transpose(0, 2, 1, 3).reshape(count, -1, HEAD_DIM)


def local(
    kv_store, queries, step_kv, suffix_pages, suffix_len, owner, parent_id, parent_pages, parent_len
):
    decoding = lax.axis_index("role") == 1
    seq_count = lax.axis_size("seq")
    store = kv_store[0]
    count, pair, width = queries.shape[1:]
    cap = max(2, 2 * count // seq_count)
    head_span = cap * HEAD_ROWS
    chunk = max(1, min(seq_count, 512 // head_span))
    query_rows = head_rows(queries[0])
    owner_row, parent_row = owner.reshape(1, -1), parent_id.reshape(1, -1)
    tables = (suffix_pages.T, suffix_len.reshape(1, -1), parent_pages, parent_len.reshape(1, -1))
    token_rows = store.shape[0]

    suffix_store = lax.ppermute(store, "role", [(0, 1), (1, 0)])

    sent = jax.ShapeDtypeStruct((seq_count, KV_HEADS * head_span + 16, HEAD_DIM), jnp.bfloat16)
    answer = jax.ShapeDtypeStruct((seq_count, KV_HEADS * head_span + STAT_ROWS, HEAD_DIM), jnp.int16)
    result = jax.ShapeDtypeStruct(query_rows.shape, jnp.bfloat16)
    bias = pltpu.VMEM((token_rows, HEAD_DIM), jnp.bfloat16)
    rows = count * HEAD_ROWS
    part = (KV_HEADS, rows, HEAD_DIM)

    def exchange(block):
        return lax.all_to_all(block, "seq", split_axis=0, concat_axis=0, tiled=True)

    def tokens_of(rows):
        return rows.reshape(count, width // HEAD_DIM, pair, HEAD_DIM).transpose(0, 2, 1, 3).reshape(
            1, count, pair, width
        )

    handed = (sent, *(jax.ShapeDtypeStruct(t.shape, t.dtype) for t in (owner_row, *tables)))

    def send_queries(query_rows):
        packed, *copies = call(
            functools.partial(pack_kernel, cap),
            handed,
            (query_rows, owner_row, parent_row, *tables),
            [pltpu.VMEM((seq_count, 16, HEAD_DIM), jnp.float32)],
        )
        return exchange(packed), *copies

    def idle(query_rows):
        return call(idle_kernel, handed, (owner_row, *tables), [])

    received = lax.cond(decoding, send_queries, idle, query_rows)

    def decode(received, suffix_store, query_rows):
        received, owner_row, suffix_table, suffix_lengths, parent_pages, parent_lengths = received
        parents, page_count = parent_pages.shape
        beside = (KV_HEADS, page_count * PAGE, parents * HEAD_DIM)
        parts = call(
            functools.partial(parent_kernel, cap, chunk),
            answer,
            (parent_pages, parent_lengths, received, store),
            [
                pltpu.VMEM(answer.shape, jnp.int16),
                pltpu.VMEM(beside, jnp.bfloat16),
                pltpu.VMEM(beside, jnp.bfloat16),
                pltpu.SemaphoreType.DMA((seq_count // chunk, KV_HEADS + 1)),
            ],
            out_space=pl.ANY,
        )
        back = exchange(parts)
        own, own_stats = call(
            local_kernel,
            (jax.ShapeDtypeStruct(part, jnp.float32), jax.ShapeDtypeStruct((2 * KV_HEADS, rows), jnp.float32)),
            (suffix_table, suffix_lengths, query_rows, suffix_store, head_rows(step_kv)),
            [bias],
            pl.CostEstimate(flops=1 << 31, bytes_accessed=1 << 22, transcendentals=1 << 20),
        )
        return tokens_of(
            call(
                functools.partial(merge_kernel, cap),
                result,
                (owner_row, back, own, own_stats),
                [pltpu.VMEM((seq_count, 2 * KV_HEADS, HEAD_DIM), jnp.float32)],
            )
        )

    def prefill(received, suffix_store, query_rows):
        return tokens_of(
            call(prefill_kernel, result, (*received[2:4], query_rows, store), [bias])
        )

    return lax.cond(decoding, decode, prefill, received, suffix_store, query_rows)


def solution(mesh):
    in_specs = (
        P("role", ("groups", "seq"), None),
        P("role", ("groups", "seq"), None, None),
        P(("groups", "seq"), None, None),
        P(("groups", "seq"), None),
        P(("groups", "seq")),
        P(("groups", "seq"), None),
        P(("groups", "seq")),
        P(("groups", "seq"), None),
        P(("groups", "seq")),
    )
    out_specs = P("role", ("groups", "seq"), None, None)
    return jax.shard_map(local, mesh=mesh, in_specs=in_specs, out_specs=out_specs, check_vma=False)
```

```python
import functools

import jax
import jax.numpy as jnp
from jax import lax
from jax.experimental import pallas as pl
from jax.experimental.pallas import tpu as pltpu
from jax.sharding import PartitionSpec as P

HEAD_DIM = 128
KV_HEADS = 4
GROUP = 8
PAGE = 16
HEAD_ROWS = 2 * GROUP
KEY_WIDTH = KV_HEADS * HEAD_DIM
SCALE = HEAD_DIM ** (-0.5)
MASKED = -1e30
STAT_ROWS = 4 * KV_HEADS
LOG_STEPS = 4.0
SCALE_STEPS = 128.0
CODE_TOP = 32600.0
LOG2_E = 1.4426950408889634
VMEM_BYTES = 48 * 1024 * 1024

NT = (((1,), (1,)), ((), ()))


def iota(shape, dim):
    return lax.broadcasted_iota(jnp.int32, shape, dim)


def slot_ranks(owner_ref, cap, owners):
    owner = owner_ref[...]
    bits = cap.bit_length()
    per_word = 30 // bits
    words = [jnp.int32(0)] * -(-owners // per_word)
    names, ranks = [], []
    for r in range(owner.shape[1]):
        name = owner[0, r]
        word, rank = name // per_word if len(words) > 1 else 0, jnp.int32(0)
        shift = (name - word * per_word) * bits
        for k, counts in enumerate(words):
            here = (word == k) if len(words) > 1 else True
            count = (counts >> shift) & ((1 << bits) - 1)
            step = jnp.int32(1) << shift
            if len(words) > 1:
                count, step = jnp.where(here, count, 0), jnp.where(here, step, 0)
            rank = rank + count
            words[k] = counts + step
        names.append(name)
        ranks.append(rank)
    return names, ranks


def pack_kernel(cap, query_ref, owner_ref, parent_ref, *refs):
    tables, (out_ref, *copies), meta_ref = refs[: len(refs) // 2 - 1], refs[len(refs) // 2 - 1 : -1], refs[-1]
    for table, copy in zip((owner_ref, *tables), copies):
        copy[...] = table[...]
    parent = parent_ref[...]
    count = query_ref.shape[0]
    head_span = cap * HEAD_ROWS
    out_ref[...] = jnp.zeros_like(out_ref)
    meta_ref[...] = jnp.zeros_like(meta_ref)
    names, ranks = slot_ranks(owner_ref, cap, out_ref.shape[0])
    for r in range(count):
        d, rank = names[r], ranks[r]
        for g in range(KV_HEADS):
            start = pl.multiple_of(g * head_span + rank * HEAD_ROWS, HEAD_ROWS)
            out_ref[d, pl.ds(start, HEAD_ROWS), :] = query_ref[r, pl.ds(g * HEAD_ROWS, HEAD_ROWS), :]
        meta_ref[d, pl.ds(rank, 1), :] = jnp.full((1, HEAD_DIM), parent[0, r].astype(jnp.float32))
    out_ref[:, pl.ds(KV_HEADS * head_span, 16), :] = meta_ref[...].astype(jnp.bfloat16)


def idle_kernel(*refs):
    tables, (out_ref, *copies) = refs[: len(refs) // 2], refs[len(refs) // 2 :]
    out_ref[...] = jnp.zeros_like(out_ref)
    for table, copy in zip(tables, copies):
        copy[...] = table[...]


def two_codes(values, steps):
    scaled = values * steps
    whole = jnp.floor(scaled)
    rest = jnp.minimum(jnp.floor((scaled - whole) * 65536.0 + 0.5), 65535.0) - 32768.0
    return whole, rest


def from_codes(whole, rest, steps):
    return (whole + (rest + 32768.0) * (1.0 / 65536.0)) * (1.0 / steps)


def parent_kernel(
    cap, chunk, pages_ref, len_ref, recv_ref, store_ref, out_hbm, out_ref, key_ref, value_ref, sems
):
    parents, page_count = pages_ref.shape
    pages, lengths = pages_ref[...], len_ref[...]
    sources = recv_ref.shape[0]
    head_span = cap * HEAD_ROWS
    tokens = page_count * PAGE
    heads = range(KV_HEADS)
    for p in range(parents):
        for i in range(page_count):
            start = pl.multiple_of(pages[p, i] * PAGE, PAGE)
            page = store_ref[pl.ds(start, PAGE), :]
            for g in heads:
                span = (g, pl.ds(i * PAGE, PAGE), pl.ds(p * HEAD_DIM, HEAD_DIM))
                key_ref[span] = page[:, g * HEAD_DIM : (g + 1) * HEAD_DIM]
                value_ref[span] = page[:, KEY_WIDTH + g * HEAD_DIM : KEY_WIDTH + (g + 1) * HEAD_DIM]

    rows = chunk * head_span
    lanes = iota((rows, HEAD_DIM), 1)
    positions = iota((rows, tokens), 1)

    def put(c, k):
        part = (pl.ds(c * chunk, chunk), pl.ds(k * head_span, head_span if k < KV_HEADS else STAT_ROWS))
        return pltpu.make_async_copy(out_ref.at[part], out_hbm.at[part], sems.at[c, k])

    def body(c, carry):
        part = pl.ds(c * chunk, chunk)
        meta = recv_ref[part, pl.ds(KV_HEADS * head_span, 16), :].astype(jnp.float32)
        picks = [
            jnp.broadcast_to(meta[:, s : s + 1, :], (chunk, HEAD_ROWS, HEAD_DIM)) for s in range(cap)
        ]
        parent = jnp.concatenate(picks, axis=1).reshape(rows, HEAD_DIM)
        limit = jnp.full((rows, HEAD_DIM), lengths[0, 0], jnp.int32)
        for p in range(1, parents):
            limit = jnp.where(parent == p, lengths[0, p], limit)
        bias = jnp.where(positions < limit[:, :1], 0.0, MASKED)
        parent_low = parent.astype(jnp.bfloat16)

        def scores_of(g):
            query = recv_ref[part, pl.ds(g * head_span, head_span), :].reshape(rows, HEAD_DIM)
            query = jnp.concatenate(
                [jnp.where(parent_low == p, query, jnp.zeros_like(query)) for p in range(parents)], axis=1
            )
            return lax.dot_general(query, key_ref[g], NT, preferred_element_type=jnp.float32)

        def softmax_of(scores):
            scores = scores + bias
            top = jnp.max(scores, axis=1, keepdims=True)
            terms = jnp.exp2((scores - top) * (SCALE * LOG2_E))
            return terms.astype(jnp.bfloat16), top, jnp.sum(terms, axis=1, keepdims=True)

        def blended_of(g, weights):
            both = jnp.dot(weights, value_ref[g], preferred_element_type=jnp.float32)
            blended = both[:, :HEAD_DIM]
            for p in range(1, parents):
                blended = jnp.where(parent == p, both[:, p * HEAD_DIM : (p + 1) * HEAD_DIM], blended)
            return blended

        scores = [scores_of(g) for g in heads]
        softmaxes = [softmax_of(scores[g]) for g in heads]
        blends = [blended_of(g, softmaxes[g][0]) for g in heads]
        stats = jnp.zeros((rows, HEAD_DIM), jnp.float32)
        for g in heads:
            reach = jnp.maximum(jnp.max(jnp.abs(blends[g]), axis=1, keepdims=True), 1e-30)
            inverse = pltpu.reciprocal(reach, approx=True) * CODE_TOP
            coded = jnp.round(blends[g] * inverse).astype(jnp.int32).astype(jnp.int16)
            out_ref[part, pl.ds(g * head_span, head_span), :] = coded.reshape(chunk, head_span, HEAD_DIM)
            put(c, g).start()
            for k, value in enumerate((softmaxes[g][1], softmaxes[g][2], inverse)):
                stats = jnp.where(lanes == k * KV_HEADS + g, value, stats)
        flat = stats.T
        top, total, inverse = (flat[k * KV_HEADS : (k + 1) * KV_HEADS, :] for k in range(3))
        codes = two_codes(top * SCALE + jnp.log(total), LOG_STEPS)
        codes += two_codes(-jnp.log2(inverse * total), SCALE_STEPS)
        flat = jnp.concatenate(codes, axis=0).astype(jnp.int32).astype(jnp.int16)
        for j in range(chunk):
            piece = flat[:, j * head_span : (j + 1) * head_span]
            if head_span < HEAD_DIM:
                piece = jnp.concatenate(
                    [piece, jnp.zeros((STAT_ROWS, HEAD_DIM - head_span), jnp.int16)], axis=1
                )
            out_ref[c * chunk + j, pl.ds(KV_HEADS * head_span, STAT_ROWS), :] = piece
        put(c, KV_HEADS).start()
        return carry

    lax.fori_loop(0, sources // chunk, body, 0, unroll=sources == chunk)
    for c in range(sources // chunk):
        for k in range(KV_HEADS + 1):
            put(c, k).wait()


def fill_suffix_bias(pages_ref, len_ref, bias_ref, last_of):
    page_count, count = pages_ref.shape
    pages, lengths = pages_ref[...], len_ref[...]
    row, lane = iota((PAGE, HEAD_DIM), 0), iota((PAGE, HEAD_DIM), 1)
    for r in range(count):
        for i in range(page_count):
            keep = (lane // 2 == r) & (row + i * PAGE <= last_of(lengths[0, r], lane % 2))
            start = pl.multiple_of(pages[i, r] * PAGE, PAGE)
            bias_ref[pl.ds(start, PAGE), :] = jnp.where(keep, 0.0, MASKED).astype(jnp.bfloat16)


def own_pick(count):
    rows = count * HEAD_ROWS
    row, lane = iota((rows, HEAD_DIM), 0), iota((rows, HEAD_DIM), 1)
    return jnp.where(lane == (row // HEAD_ROWS) * 2 + row % 2, 1.0, 0.0).astype(jnp.bfloat16)


def prefill_kernel(pages_ref, len_ref, query_ref, store_ref, out_ref, bias_ref):
    count = query_ref.shape[0]
    rows = count * HEAD_ROWS
    fill_suffix_bias(pages_ref, len_ref, bias_ref, lambda length, t: length - 2 + t)
    pick = own_pick(count)
    for g in range(KV_HEADS):
        query = query_ref[:, pl.ds(g * HEAD_ROWS, HEAD_ROWS), :].reshape(rows, HEAD_DIM)
        keys = store_ref[:, pl.ds(g * HEAD_DIM, HEAD_DIM)]
        values = store_ref[:, pl.ds(KEY_WIDTH + g * HEAD_DIM, HEAD_DIM)]
        scores = lax.dot_general(
            jnp.concatenate([query, pick], axis=1),
            jnp.concatenate([keys, bias_ref[...]], axis=1),
            NT,
            preferred_element_type=jnp.float32,
        ) * SCALE
        terms = jnp.exp(scores - jnp.max(scores, axis=1, keepdims=True))
        total = jnp.sum(terms, axis=1, keepdims=True)
        blended = jnp.dot(terms.astype(jnp.bfloat16), values, preferred_element_type=jnp.float32)
        out_ref[:, pl.ds(g * HEAD_ROWS, HEAD_ROWS), :] = (
            (blended / total).astype(jnp.bfloat16).reshape(count, HEAD_ROWS, HEAD_DIM)
        )


def local_kernel(pages_ref, len_ref, query_ref, store_ref, step_ref, out_ref, stat_ref, bias_ref):
    count = query_ref.shape[0]
    rows = count * HEAD_ROWS
    fill_suffix_bias(pages_ref, len_ref, bias_ref, lambda length, t: length - 1)
    steps = 2 * count
    step_pad = -steps % HEAD_DIM
    key_row, lane = iota((steps + step_pad, HEAD_DIM), 0), iota((steps + step_pad, HEAD_DIM), 1)
    seen = (key_row // 2 == lane // 2) & (key_row % 2 <= lane % 2) & (key_row < steps)
    step_bias = jnp.where(seen, 0.0, MASKED).astype(jnp.bfloat16)
    pad = jnp.zeros((step_pad, HEAD_DIM), jnp.bfloat16)

    def step_rows(c):
        return jnp.concatenate([step_ref[r, 2 * c : 2 * c + 2, :] for r in range(count)] + [pad], axis=0)

    pick = own_pick(count)
    lanes = iota((rows, HEAD_DIM), 1)
    stats = jnp.zeros((rows, HEAD_DIM), jnp.float32)
    for g in range(KV_HEADS):
        query = query_ref[:, pl.ds(g * HEAD_ROWS, HEAD_ROWS), :].reshape(rows, HEAD_DIM)
        query = jnp.concatenate([query, pick], axis=1)
        keys = jnp.concatenate([store_ref[:, pl.ds(g * HEAD_DIM, HEAD_DIM)], bias_ref[...]], axis=1)
        step_keys = jnp.concatenate([step_rows(g), step_bias], axis=1)
        values = store_ref[:, pl.ds(KEY_WIDTH + g * HEAD_DIM, HEAD_DIM)]
        step_values = step_rows(KV_HEADS + g)
        scores = lax.dot_general(query, keys, NT, preferred_element_type=jnp.float32) * SCALE
        step_scores = lax.dot_general(query, step_keys, NT, preferred_element_type=jnp.float32) * SCALE
        top = jnp.maximum(
            jnp.max(scores, axis=1, keepdims=True), jnp.max(step_scores, axis=1, keepdims=True)
        )
        terms = jnp.exp(scores - top)
        step_terms = jnp.exp(step_scores - top)
        total = jnp.sum(terms, axis=1, keepdims=True) + jnp.sum(step_terms, axis=1, keepdims=True)
        blended = jnp.dot(terms.astype(jnp.bfloat16), values, preferred_element_type=jnp.float32)
        blended = blended + jnp.dot(
            step_terms.astype(jnp.bfloat16), step_values, preferred_element_type=jnp.float32
        )
        out_ref[g] = blended
        stats = jnp.where(lanes == g, top, stats)
        stats = jnp.where(lanes == KV_HEADS + g, total, stats)
    stat_ref[...] = stats.T[: 2 * KV_HEADS, :]


def merge_kernel(cap, owner_ref, back_ref, own_ref, own_stat_ref, out_ref, decoded_ref):
    count = out_ref.shape[0]
    rows = count * HEAD_ROWS
    head_span = cap * HEAD_ROWS
    codes = back_ref[:, pl.ds(KV_HEADS * head_span, STAT_ROWS), :].astype(jnp.int32).astype(jnp.float32)
    codes = [codes[:, k * KV_HEADS : (k + 1) * KV_HEADS, :] for k in range(4)]
    log_total = from_codes(codes[0], codes[1], LOG_STEPS)
    unit = jnp.exp2(from_codes(codes[2], codes[3], SCALE_STEPS))
    decoded_ref[...] = jnp.concatenate([log_total, unit], axis=1)

    names, ranks = slot_ranks(owner_ref, cap, back_ref.shape[0])
    per_tile = HEAD_DIM // HEAD_ROWS
    place = iota((2 * KV_HEADS, HEAD_DIM), 1) // HEAD_ROWS
    tiles = []
    for first in range(0, count, per_tile):
        tile = jnp.zeros((2 * KV_HEADS, HEAD_DIM), jnp.float32)
        for r in range(first, min(first + per_tile, count)):
            shift = lax.rem((r - first) * HEAD_ROWS - ranks[r] * HEAD_ROWS + HEAD_DIM, HEAD_DIM)
            tile = jnp.where(place == r - first, pltpu.roll(decoded_ref[names[r]], shift, 1), tile)
        tiles.append(tile)
    flat = jnp.concatenate(tiles, axis=1)[:, :rows]
    part_top, unit = flat[:KV_HEADS], flat[KV_HEADS:]
    own_top, own_total = own_stat_ref[:KV_HEADS, :], own_stat_ref[KV_HEADS:, :]
    top = jnp.maximum(own_top, part_top)
    own_weight, part_weight = jnp.exp(own_top - top), jnp.exp(part_top - top)
    inverse = 1.0 / (own_weight * own_total + part_weight)
    weights = [own_weight * inverse, unit * part_weight * inverse]
    weights.append(jnp.zeros((HEAD_DIM - 2 * KV_HEADS, rows), jnp.float32))
    weights = jnp.concatenate(weights, axis=0).T
    for r in range(count):
        span = slice(r * HEAD_ROWS, (r + 1) * HEAD_ROWS)
        for g in range(KV_HEADS):
            start = pl.multiple_of(g * head_span + ranks[r] * HEAD_ROWS, HEAD_ROWS)
            part = back_ref[names[r], pl.ds(start, HEAD_ROWS), :].astype(jnp.int32).astype(jnp.float32)
            merged = own_ref[g, span, :] * weights[span, g : g + 1]
            merged = merged + part * weights[span, KV_HEADS + g : KV_HEADS + g + 1]
            out_ref[r, pl.ds(g * HEAD_ROWS, HEAD_ROWS), :] = merged.astype(jnp.bfloat16)


def call(kernel, out_shape, arrays, scratch, cost=None, out_space=pltpu.VMEM):
    vmem = pl.BlockSpec(memory_space=pltpu.VMEM)
    put = pl.BlockSpec(memory_space=out_space)
    return pl.pallas_call(
        kernel,
        out_shape=out_shape,
        in_specs=[vmem] * len(arrays),
        out_specs=jax.tree.map(lambda _: put, out_shape),
        cost_estimate=cost,
        scratch_shapes=scratch,
        compiler_params=pltpu.CompilerParams(vmem_limit_bytes=VMEM_BYTES),
    )(*arrays)


def head_rows(tokens):
    count, pair, width = tokens.shape
    blocks = tokens.reshape(count, pair, width // HEAD_DIM, HEAD_DIM)
    return blocks.transpose(0, 2, 1, 3).reshape(count, -1, HEAD_DIM)


def local(
    kv_store, queries, step_kv, suffix_pages, suffix_len, owner, parent_id, parent_pages, parent_len
):
    decoding = lax.axis_index("role") == 1
    seq_count = lax.axis_size("seq")
    store = kv_store[0]
    count, pair, width = queries.shape[1:]
    cap = max(2, 2 * count // seq_count)
    head_span = cap * HEAD_ROWS
    chunk = max(1, min(seq_count, 512 // head_span))
    query_rows = head_rows(queries[0])
    owner_row, parent_row = owner.reshape(1, -1), parent_id.reshape(1, -1)
    tables = (suffix_pages.T, suffix_len.reshape(1, -1), parent_pages, parent_len.reshape(1, -1))
    token_rows = store.shape[0]

    sent = jax.ShapeDtypeStruct((seq_count, KV_HEADS * head_span + 16, HEAD_DIM), jnp.bfloat16)
    answer = jax.ShapeDtypeStruct((seq_count, KV_HEADS * head_span + STAT_ROWS, HEAD_DIM), jnp.int16)
    result = jax.ShapeDtypeStruct(query_rows.shape, jnp.bfloat16)
    bias = pltpu.VMEM((token_rows, HEAD_DIM), jnp.bfloat16)
    rows = count * HEAD_ROWS
    part = (KV_HEADS, rows, HEAD_DIM)

    def exchange(block):
        return lax.all_to_all(block, "seq", split_axis=0, concat_axis=0, tiled=True)

    def tokens_of(rows):
        return rows.reshape(count, width // HEAD_DIM, pair, HEAD_DIM).transpose(0, 2, 1, 3).reshape(
            1, count, pair, width
        )

    handed = (sent, *(jax.ShapeDtypeStruct(t.shape, t.dtype) for t in (owner_row, *tables)))

    def send_queries(query_rows):
        packed, *copies = call(
            functools.partial(pack_kernel, cap),
            handed,
            (query_rows, owner_row, parent_row, *tables),
            [pltpu.VMEM((seq_count, 16, HEAD_DIM), jnp.float32)],
        )
        return exchange(packed), *copies

    def idle(query_rows):
        return call(idle_kernel, handed, (owner_row, *tables), [])

    received, owner_row, *tables = lax.cond(decoding, send_queries, idle, query_rows)
    store_after, received = lax.optimization_barrier((store, received))
    suffix_store = lax.ppermute(store_after, "role", [(0, 1), (1, 0)])

    def answer_queries(received):
        parents, page_count = parent_pages.shape
        beside = (KV_HEADS, page_count * PAGE, parents * HEAD_DIM)
        return call(
            functools.partial(parent_kernel, cap, chunk),
            answer,
            (*tables[2:], received, store),
            [
                pltpu.VMEM(answer.shape, jnp.int16),
                pltpu.VMEM(beside, jnp.bfloat16),
                pltpu.VMEM(beside, jnp.bfloat16),
                pltpu.SemaphoreType.DMA((seq_count // chunk, KV_HEADS + 1)),
            ],
            out_space=pl.ANY,
        )

    parts = lax.cond(decoding, answer_queries, lambda _: jnp.zeros(answer.shape, answer.dtype), received)

    def decode(parts, suffix_store, query_rows):
        back = exchange(parts)
        own, own_stats = call(
            local_kernel,
            (jax.ShapeDtypeStruct(part, jnp.float32), jax.ShapeDtypeStruct((2 * KV_HEADS, rows), jnp.float32)),
            (*tables[:2], query_rows, suffix_store, head_rows(step_kv)),
            [bias],
            pl.CostEstimate(flops=1 << 31, bytes_accessed=1 << 22, transcendentals=1 << 20),
        )
        return tokens_of(
            call(
                functools.partial(merge_kernel, cap),
                result,
                (owner_row, back, own, own_stats),
                [pltpu.VMEM((seq_count, 2 * KV_HEADS, HEAD_DIM), jnp.float32)],
            )
        )

    def prefill(parts, suffix_store, query_rows):
        return tokens_of(
            call(prefill_kernel, result, (*tables[:2], query_rows, store), [bias])
        )

    return lax.cond(decoding, decode, prefill, parts, suffix_store, query_rows)


def solution(mesh):
    in_specs = (
        P("role", ("groups", "seq"), None),
        P("role", ("groups", "seq"), None, None),
        P(("groups", "seq"), None, None),
        P(("groups", "seq"), None),
        P(("groups", "seq")),
        P(("groups", "seq"), None),
        P(("groups", "seq")),
        P(("groups", "seq"), None),
        P(("groups", "seq")),
    )
    out_specs = P("role", ("groups", "seq"), None, None)
    return jax.shard_map(local, mesh=mesh, in_specs=in_specs, out_specs=out_specs, check_vma=False)
```

```python
import functools

import jax
import jax.numpy as jnp
from jax import lax
from jax.experimental import pallas as pl
from jax.experimental.pallas import tpu as pltpu
from jax.sharding import PartitionSpec as P

HEAD_DIM = 128
KV_HEADS = 4
GROUP = 8
PAGE = 16
HEAD_ROWS = 2 * GROUP
KEY_WIDTH = KV_HEADS * HEAD_DIM
SCALE = HEAD_DIM ** (-0.5)
MASKED = -1e30
STAT_ROWS = 4 * KV_HEADS
LOG_STEPS = 4.0
SCALE_STEPS = 128.0
CODE_TOP = 32600.0
LOG2_E = 1.4426950408889634
VMEM_BYTES = 48 * 1024 * 1024

NT = (((1,), (1,)), ((), ()))


def iota(shape, dim):
    return lax.broadcasted_iota(jnp.int32, shape, dim)


def slot_ranks(owner_ref, cap, owners):
    owner = owner_ref[...]
    bits = cap.bit_length()
    per_word = 30 // bits
    words = [jnp.int32(0)] * -(-owners // per_word)
    names, ranks = [], []
    for r in range(owner.shape[1]):
        name = owner[0, r]
        word, rank = name // per_word if len(words) > 1 else 0, jnp.int32(0)
        shift = (name - word * per_word) * bits
        for k, counts in enumerate(words):
            here = (word == k) if len(words) > 1 else True
            count = (counts >> shift) & ((1 << bits) - 1)
            step = jnp.int32(1) << shift
            if len(words) > 1:
                count, step = jnp.where(here, count, 0), jnp.where(here, step, 0)
            rank = rank + count
            words[k] = counts + step
        names.append(name)
        ranks.append(rank)
    return names, ranks


def pack_kernel(cap, query_hbm, owner_hbm, parent_hbm, *refs):
    *refs, query_ref, parent_ref, meta_ref, sems = refs
    tables, (out_ref, owner_ref, *copies) = refs[: len(refs) // 2 - 1], refs[len(refs) // 2 - 1 :]
    moves = [(owner_hbm, owner_ref), (parent_hbm, parent_ref), (query_hbm, query_ref), *zip(tables, copies)]
    moves = [pltpu.make_async_copy(src, dst, sems.at[k]) for k, (src, dst) in enumerate(moves)]
    for move in moves:
        move.start()
    count = query_ref.shape[0]
    head_span = cap * HEAD_ROWS
    out_ref[...] = jnp.zeros_like(out_ref)
    meta_ref[...] = jnp.zeros_like(meta_ref)
    moves[0].wait()
    moves[1].wait()
    parent = parent_ref[...]
    names, ranks = slot_ranks(owner_ref, cap, out_ref.shape[0])
    for r in range(count):
        meta_ref[names[r], pl.ds(ranks[r], 1), :] = jnp.full((1, HEAD_DIM), parent[0, r].astype(jnp.float32))
    out_ref[:, pl.ds(KV_HEADS * head_span, 16), :] = meta_ref[...].astype(jnp.bfloat16)
    moves[2].wait()
    for r in range(count):
        d, rank = names[r], ranks[r]
        for g in range(KV_HEADS):
            start = pl.multiple_of(g * head_span + rank * HEAD_ROWS, HEAD_ROWS)
            out_ref[d, pl.ds(start, HEAD_ROWS), :] = query_ref[r, pl.ds(g * HEAD_ROWS, HEAD_ROWS), :]
    for move in moves[3:]:
        move.wait()


def idle_kernel(*refs):
    tables, (out_ref, *copies) = refs[: len(refs) // 2], refs[len(refs) // 2 :]
    out_ref[...] = jnp.zeros_like(out_ref)
    for table, copy in zip(tables, copies):
        copy[...] = table[...]


def two_codes(values, steps):
    scaled = values * steps
    whole = jnp.floor(scaled)
    rest = jnp.minimum(jnp.floor((scaled - whole) * 65536.0 + 0.5), 65535.0) - 32768.0
    return whole, rest


def from_codes(whole, rest, steps):
    return (whole + (rest + 32768.0) * (1.0 / 65536.0)) * (1.0 / steps)


def parent_kernel(
    cap, chunk, pages_ref, len_ref, recv_ref, store_ref, out_hbm, out_ref, key_ref, value_ref, sems
):
    parents, page_count = pages_ref.shape
    pages, lengths = pages_ref[...], len_ref[...]
    sources = recv_ref.shape[0]
    head_span = cap * HEAD_ROWS
    tokens = page_count * PAGE
    heads = range(KV_HEADS)
    for p in range(parents):
        for i in range(page_count):
            start = pl.multiple_of(pages[p, i] * PAGE, PAGE)
            page = store_ref[pl.ds(start, PAGE), :]
            for g in heads:
                span = (g, pl.ds(i * PAGE, PAGE), pl.ds(p * HEAD_DIM, HEAD_DIM))
                key_ref[span] = page[:, g * HEAD_DIM : (g + 1) * HEAD_DIM]
                value_ref[span] = page[:, KEY_WIDTH + g * HEAD_DIM : KEY_WIDTH + (g + 1) * HEAD_DIM]

    rows = chunk * head_span
    lanes = iota((rows, HEAD_DIM), 1)
    positions = iota((rows, tokens), 1)

    def put(c, k):
        part = (pl.ds(c * chunk, chunk), pl.ds(k * head_span, head_span if k < KV_HEADS else STAT_ROWS))
        return pltpu.make_async_copy(out_ref.at[part], out_hbm.at[part], sems.at[c, k])

    def body(c, carry):
        part = pl.ds(c * chunk, chunk)
        meta = recv_ref[part, pl.ds(KV_HEADS * head_span, 16), :].astype(jnp.float32)
        picks = [
            jnp.broadcast_to(meta[:, s : s + 1, :], (chunk, HEAD_ROWS, HEAD_DIM)) for s in range(cap)
        ]
        parent = jnp.concatenate(picks, axis=1).reshape(rows, HEAD_DIM)
        limit = jnp.full((rows, HEAD_DIM), lengths[0, 0], jnp.int32)
        for p in range(1, parents):
            limit = jnp.where(parent == p, lengths[0, p], limit)
        bias = jnp.where(positions < limit[:, :1], 0.0, MASKED)
        parent_low = parent.astype(jnp.bfloat16)

        def scores_of(g):
            query = recv_ref[part, pl.ds(g * head_span, head_span), :].reshape(rows, HEAD_DIM)
            query = jnp.concatenate(
                [jnp.where(parent_low == p, query, jnp.zeros_like(query)) for p in range(parents)], axis=1
            )
            return lax.dot_general(query, key_ref[g], NT, preferred_element_type=jnp.float32)

        def softmax_of(scores):
            scores = scores + bias
            top = jnp.max(scores, axis=1, keepdims=True)
            terms = jnp.exp2((scores - top) * (SCALE * LOG2_E))
            return terms.astype(jnp.bfloat16), top, jnp.sum(terms, axis=1, keepdims=True)

        def blended_of(g, weights):
            both = jnp.dot(weights, value_ref[g], preferred_element_type=jnp.float32)
            blended = both[:, :HEAD_DIM]
            for p in range(1, parents):
                blended = jnp.where(parent == p, both[:, p * HEAD_DIM : (p + 1) * HEAD_DIM], blended)
            return blended

        scores = [scores_of(g) for g in heads]
        softmaxes = [softmax_of(scores[g]) for g in heads]
        blends = [blended_of(g, softmaxes[g][0]) for g in heads]
        stats = jnp.zeros((rows, HEAD_DIM), jnp.float32)
        for g in heads:
            reach = jnp.maximum(jnp.max(jnp.abs(blends[g]), axis=1, keepdims=True), 1e-30)
            inverse = pltpu.reciprocal(reach, approx=True) * CODE_TOP
            coded = jnp.round(blends[g] * inverse).astype(jnp.int32).astype(jnp.int16)
            out_ref[part, pl.ds(g * head_span, head_span), :] = coded.reshape(chunk, head_span, HEAD_DIM)
            put(c, g).start()
            for k, value in enumerate((softmaxes[g][1], softmaxes[g][2], inverse)):
                stats = jnp.where(lanes == k * KV_HEADS + g, value, stats)
        flat = stats.T
        top, total, inverse = (flat[k * KV_HEADS : (k + 1) * KV_HEADS, :] for k in range(3))
        codes = two_codes(top * SCALE + jnp.log(total), LOG_STEPS)
        codes += two_codes(-jnp.log2(inverse * total), SCALE_STEPS)
        flat = jnp.concatenate(codes, axis=0).astype(jnp.int32).astype(jnp.int16)
        for j in range(chunk):
            piece = flat[:, j * head_span : (j + 1) * head_span]
            if head_span < HEAD_DIM:
                piece = jnp.concatenate(
                    [piece, jnp.zeros((STAT_ROWS, HEAD_DIM - head_span), jnp.int16)], axis=1
                )
            out_ref[c * chunk + j, pl.ds(KV_HEADS * head_span, STAT_ROWS), :] = piece
        put(c, KV_HEADS).start()
        return carry

    lax.fori_loop(0, sources // chunk, body, 0, unroll=sources == chunk)
    for c in range(sources // chunk):
        for k in range(KV_HEADS + 1):
            put(c, k).wait()


def fill_suffix_bias(pages_ref, len_ref, bias_ref, last_of):
    page_count, count = pages_ref.shape
    pages, lengths = pages_ref[...], len_ref[...]
    row, lane = iota((PAGE, HEAD_DIM), 0), iota((PAGE, HEAD_DIM), 1)
    for r in range(count):
        for i in range(page_count):
            keep = (lane // 2 == r) & (row + i * PAGE <= last_of(lengths[0, r], lane % 2))
            start = pl.multiple_of(pages[i, r] * PAGE, PAGE)
            bias_ref[pl.ds(start, PAGE), :] = jnp.where(keep, 0.0, MASKED).astype(jnp.bfloat16)


def own_pick(count):
    rows = count * HEAD_ROWS
    row, lane = iota((rows, HEAD_DIM), 0), iota((rows, HEAD_DIM), 1)
    return jnp.where(lane == (row // HEAD_ROWS) * 2 + row % 2, 1.0, 0.0).astype(jnp.bfloat16)


def prefill_kernel(pages_ref, len_ref, query_ref, store_ref, out_ref, bias_ref):
    count = query_ref.shape[0]
    rows = count * HEAD_ROWS
    fill_suffix_bias(pages_ref, len_ref, bias_ref, lambda length, t: length - 2 + t)
    pick = own_pick(count)
    for g in range(KV_HEADS):
        query = query_ref[:, pl.ds(g * HEAD_ROWS, HEAD_ROWS), :].reshape(rows, HEAD_DIM)
        keys = store_ref[:, pl.ds(g * HEAD_DIM, HEAD_DIM)]
        values = store_ref[:, pl.ds(KEY_WIDTH + g * HEAD_DIM, HEAD_DIM)]
        scores = lax.dot_general(
            jnp.concatenate([query, pick], axis=1),
            jnp.concatenate([keys, bias_ref[...]], axis=1),
            NT,
            preferred_element_type=jnp.float32,
        ) * SCALE
        terms = jnp.exp(scores - jnp.max(scores, axis=1, keepdims=True))
        total = jnp.sum(terms, axis=1, keepdims=True)
        blended = jnp.dot(terms.astype(jnp.bfloat16), values, preferred_element_type=jnp.float32)
        out_ref[:, pl.ds(g * HEAD_ROWS, HEAD_ROWS), :] = (
            (blended / total).astype(jnp.bfloat16).reshape(count, HEAD_ROWS, HEAD_DIM)
        )


def local_kernel(pages_ref, len_ref, query_ref, store_ref, step_ref, out_ref, stat_ref, bias_ref):
    count = query_ref.shape[0]
    rows = count * HEAD_ROWS
    fill_suffix_bias(pages_ref, len_ref, bias_ref, lambda length, t: length - 1)
    steps = 2 * count
    step_pad = -steps % HEAD_DIM
    key_row, lane = iota((steps + step_pad, HEAD_DIM), 0), iota((steps + step_pad, HEAD_DIM), 1)
    seen = (key_row // 2 == lane // 2) & (key_row % 2 <= lane % 2) & (key_row < steps)
    step_bias = jnp.where(seen, 0.0, MASKED).astype(jnp.bfloat16)
    pad = jnp.zeros((step_pad, HEAD_DIM), jnp.bfloat16)

    def step_rows(c):
        return jnp.concatenate([step_ref[r, 2 * c : 2 * c + 2, :] for r in range(count)] + [pad], axis=0)

    pick = own_pick(count)
    lanes = iota((rows, HEAD_DIM), 1)
    stats = jnp.zeros((rows, HEAD_DIM), jnp.float32)
    for g in range(KV_HEADS):
        query = query_ref[:, pl.ds(g * HEAD_ROWS, HEAD_ROWS), :].reshape(rows, HEAD_DIM)
        query = jnp.concatenate([query, pick], axis=1)
        keys = jnp.concatenate([store_ref[:, pl.ds(g * HEAD_DIM, HEAD_DIM)], bias_ref[...]], axis=1)
        step_keys = jnp.concatenate([step_rows(g), step_bias], axis=1)
        values = store_ref[:, pl.ds(KEY_WIDTH + g * HEAD_DIM, HEAD_DIM)]
        step_values = step_rows(KV_HEADS + g)
        scores = lax.dot_general(query, keys, NT, preferred_element_type=jnp.float32) * SCALE
        step_scores = lax.dot_general(query, step_keys, NT, preferred_element_type=jnp.float32) * SCALE
        top = jnp.maximum(
            jnp.max(scores, axis=1, keepdims=True), jnp.max(step_scores, axis=1, keepdims=True)
        )
        terms = jnp.exp(scores - top)
        step_terms = jnp.exp(step_scores - top)
        total = jnp.sum(terms, axis=1, keepdims=True) + jnp.sum(step_terms, axis=1, keepdims=True)
        blended = jnp.dot(terms.astype(jnp.bfloat16), values, preferred_element_type=jnp.float32)
        blended = blended + jnp.dot(
            step_terms.astype(jnp.bfloat16), step_values, preferred_element_type=jnp.float32
        )
        out_ref[g] = blended
        stats = jnp.where(lanes == g, top, stats)
        stats = jnp.where(lanes == KV_HEADS + g, total, stats)
    stat_ref[...] = stats.T[: 2 * KV_HEADS, :]


def merge_kernel(cap, owner_ref, back_ref, own_ref, own_stat_ref, out_ref, decoded_ref):
    count = out_ref.shape[0]
    rows = count * HEAD_ROWS
    head_span = cap * HEAD_ROWS
    codes = back_ref[:, pl.ds(KV_HEADS * head_span, STAT_ROWS), :].astype(jnp.int32).astype(jnp.float32)
    codes = [codes[:, k * KV_HEADS : (k + 1) * KV_HEADS, :] for k in range(4)]
    log_total = from_codes(codes[0], codes[1], LOG_STEPS)
    unit = jnp.exp2(from_codes(codes[2], codes[3], SCALE_STEPS))
    decoded_ref[...] = jnp.concatenate([log_total, unit], axis=1)

    names, ranks = slot_ranks(owner_ref, cap, back_ref.shape[0])
    per_tile = HEAD_DIM // HEAD_ROWS
    place = iota((2 * KV_HEADS, HEAD_DIM), 1) // HEAD_ROWS
    tiles = []
    for first in range(0, count, per_tile):
        tile = jnp.zeros((2 * KV_HEADS, HEAD_DIM), jnp.float32)
        for r in range(first, min(first + per_tile, count)):
            shift = lax.rem((r - first) * HEAD_ROWS - ranks[r] * HEAD_ROWS + HEAD_DIM, HEAD_DIM)
            tile = jnp.where(place == r - first, pltpu.roll(decoded_ref[names[r]], shift, 1), tile)
        tiles.append(tile)
    flat = jnp.concatenate(tiles, axis=1)[:, :rows]
    part_top, unit = flat[:KV_HEADS], flat[KV_HEADS:]
    own_top, own_total = own_stat_ref[:KV_HEADS, :], own_stat_ref[KV_HEADS:, :]
    top = jnp.maximum(own_top, part_top)
    own_weight, part_weight = jnp.exp(own_top - top), jnp.exp(part_top - top)
    inverse = 1.0 / (own_weight * own_total + part_weight)
    weights = [own_weight * inverse, unit * part_weight * inverse]
    weights.append(jnp.zeros((HEAD_DIM - 2 * KV_HEADS, rows), jnp.float32))
    weights = jnp.concatenate(weights, axis=0).T
    for r in range(count):
        span = slice(r * HEAD_ROWS, (r + 1) * HEAD_ROWS)
        for g in range(KV_HEADS):
            start = pl.multiple_of(g * head_span + ranks[r] * HEAD_ROWS, HEAD_ROWS)
            part = back_ref[names[r], pl.ds(start, HEAD_ROWS), :].astype(jnp.int32).astype(jnp.float32)
            merged = own_ref[g, span, :] * weights[span, g : g + 1]
            merged = merged + part * weights[span, KV_HEADS + g : KV_HEADS + g + 1]
            out_ref[r, pl.ds(g * HEAD_ROWS, HEAD_ROWS), :] = merged.astype(jnp.bfloat16)


def call(kernel, out_shape, arrays, scratch, cost=None, in_space=pltpu.VMEM, out_space=pltpu.VMEM):
    take = pl.BlockSpec(memory_space=in_space)
    put = pl.BlockSpec(memory_space=out_space)
    return pl.pallas_call(
        kernel,
        out_shape=out_shape,
        in_specs=[take] * len(arrays),
        out_specs=jax.tree.map(lambda _: put, out_shape),
        cost_estimate=cost,
        scratch_shapes=scratch,
        compiler_params=pltpu.CompilerParams(vmem_limit_bytes=VMEM_BYTES),
    )(*arrays)


def head_rows(tokens):
    count, pair, width = tokens.shape
    blocks = tokens.reshape(count, pair, width // HEAD_DIM, HEAD_DIM)
    return blocks.transpose(0, 2, 1, 3).reshape(count, -1, HEAD_DIM)


def local(
    kv_store, queries, step_kv, suffix_pages, suffix_len, owner, parent_id, parent_pages, parent_len
):
    decoding = lax.axis_index("role") == 1
    seq_count = lax.axis_size("seq")
    store = kv_store[0]
    count, pair, width = queries.shape[1:]
    cap = max(2, 2 * count // seq_count)
    head_span = cap * HEAD_ROWS
    chunk = max(1, min(seq_count, 512 // head_span))
    query_rows = head_rows(queries[0])
    owner_row, parent_row = owner.reshape(1, -1), parent_id.reshape(1, -1)
    tables = (suffix_pages.T, suffix_len.reshape(1, -1), parent_pages, parent_len.reshape(1, -1))
    token_rows = store.shape[0]

    sent = jax.ShapeDtypeStruct((seq_count, KV_HEADS * head_span + 16, HEAD_DIM), jnp.bfloat16)
    answer = jax.ShapeDtypeStruct((seq_count, KV_HEADS * head_span + STAT_ROWS, HEAD_DIM), jnp.int16)
    result = jax.ShapeDtypeStruct(query_rows.shape, jnp.bfloat16)
    bias = pltpu.VMEM((token_rows, HEAD_DIM), jnp.bfloat16)
    rows = count * HEAD_ROWS
    part = (KV_HEADS, rows, HEAD_DIM)

    def exchange(block):
        return lax.all_to_all(block, "seq", split_axis=0, concat_axis=0, tiled=True)

    def tokens_of(rows):
        return rows.reshape(count, width // HEAD_DIM, pair, HEAD_DIM).transpose(0, 2, 1, 3).reshape(
            1, count, pair, width
        )

    handed = (sent, *(jax.ShapeDtypeStruct(t.shape, t.dtype) for t in (owner_row, *tables)))

    def send_queries(query_rows):
        packed, *copies = call(
            functools.partial(pack_kernel, cap),
            handed,
            (query_rows, owner_row, parent_row, *tables),
            [
                pltpu.VMEM(query_rows.shape, jnp.bfloat16),
                pltpu.VMEM(parent_row.shape, jnp.int32),
                pltpu.VMEM((seq_count, 16, HEAD_DIM), jnp.float32),
                pltpu.SemaphoreType.DMA((3 + len(tables),)),
            ],
            in_space=pl.ANY,
        )
        return packed, *copies

    def idle(query_rows):
        return call(idle_kernel, handed, (owner_row, *tables), [])

    packed, owner_row, *tables = lax.cond(decoding, send_queries, idle, query_rows)
    store_after, packed = lax.optimization_barrier((store, packed))
    suffix_store = lax.ppermute(store_after, "role", [(0, 1), (1, 0)])
    received = lax.cond(decoding, exchange, lambda block: jnp.zeros_like(block), packed)

    def answer_queries(received):
        parents, page_count = parent_pages.shape
        beside = (KV_HEADS, page_count * PAGE, parents * HEAD_DIM)
        return call(
            functools.partial(parent_kernel, cap, chunk),
            answer,
            (*tables[2:], received, store),
            [
                pltpu.VMEM(answer.shape, jnp.int16),
                pltpu.VMEM(beside, jnp.bfloat16),
                pltpu.VMEM(beside, jnp.bfloat16),
                pltpu.SemaphoreType.DMA((seq_count // chunk, KV_HEADS + 1)),
            ],
            out_space=pl.ANY,
        )

    parts = lax.cond(decoding, answer_queries, lambda _: jnp.zeros(answer.shape, answer.dtype), received)

    def decode(parts, suffix_store, query_rows):
        back = exchange(parts)
        own, own_stats = call(
            local_kernel,
            (jax.ShapeDtypeStruct(part, jnp.float32), jax.ShapeDtypeStruct((2 * KV_HEADS, rows), jnp.float32)),
            (*tables[:2], query_rows, suffix_store, head_rows(step_kv)),
            [bias],
            pl.CostEstimate(flops=1 << 31, bytes_accessed=1 << 22, transcendentals=1 << 20),
        )
        return tokens_of(
            call(
                functools.partial(merge_kernel, cap),
                result,
                (owner_row, back, own, own_stats),
                [pltpu.VMEM((seq_count, 2 * KV_HEADS, HEAD_DIM), jnp.float32)],
            )
        )

    def prefill(parts, suffix_store, query_rows):
        return tokens_of(
            call(prefill_kernel, result, (*tables[:2], query_rows, store), [bias])
        )

    return lax.cond(decoding, decode, prefill, parts, suffix_store, query_rows)


def solution(mesh):
    in_specs = (
        P("role", ("groups", "seq"), None),
        P("role", ("groups", "seq"), None, None),
        P(("groups", "seq"), None, None),
        P(("groups", "seq"), None),
        P(("groups", "seq")),
        P(("groups", "seq"), None),
        P(("groups", "seq")),
        P(("groups", "seq"), None),
        P(("groups", "seq")),
    )
    out_specs = P("role", ("groups", "seq"), None, None)
    return jax.shard_map(local, mesh=mesh, in_specs=in_specs, out_specs=out_specs, check_vma=False)
```

```python
import functools

import jax
import jax.numpy as jnp
from jax import lax
from jax.experimental import pallas as pl
from jax.experimental.pallas import tpu as pltpu
from jax.sharding import PartitionSpec as P

HEAD_DIM = 128
KV_HEADS = 4
GROUP = 8
PAGE = 16
HEAD_ROWS = 2 * GROUP
KEY_WIDTH = KV_HEADS * HEAD_DIM
SCALE = HEAD_DIM ** (-0.5)
MASKED = -1e30
STAT_ROWS = 4 * KV_HEADS
LOG_STEPS = 4.0
SCALE_STEPS = 128.0
CODE_TOP = 32600.0
LOG2_E = 1.4426950408889634
VMEM_BYTES = 48 * 1024 * 1024

NT = (((1,), (1,)), ((), ()))


def iota(shape, dim):
    return lax.broadcasted_iota(jnp.int32, shape, dim)


def slot_ranks(owner_ref, cap, owners):
    owner = owner_ref[...]
    bits = cap.bit_length()
    per_word = 30 // bits
    words = [jnp.int32(0)] * -(-owners // per_word)
    names, ranks = [], []
    for r in range(owner.shape[1]):
        name = owner[0, r]
        word, rank = name // per_word if len(words) > 1 else 0, jnp.int32(0)
        shift = (name - word * per_word) * bits
        for k, counts in enumerate(words):
            here = (word == k) if len(words) > 1 else True
            count = (counts >> shift) & ((1 << bits) - 1)
            step = jnp.int32(1) << shift
            if len(words) > 1:
                count, step = jnp.where(here, count, 0), jnp.where(here, step, 0)
            rank = rank + count
            words[k] = counts + step
        names.append(name)
        ranks.append(rank)
    return names, ranks


def pack_kernel(cap, query_hbm, owner_hbm, parent_hbm, *refs):
    *refs, query_ref, parent_ref, meta_ref, sems = refs
    tables, (out_ref, owner_ref, *copies) = refs[: len(refs) // 2 - 1], refs[len(refs) // 2 - 1 :]
    moves = [(owner_hbm, owner_ref), (parent_hbm, parent_ref), (query_hbm, query_ref), *zip(tables, copies)]
    moves = [pltpu.make_async_copy(src, dst, sems.at[k]) for k, (src, dst) in enumerate(moves)]
    for move in moves:
        move.start()
    count = query_ref.shape[0]
    head_span = cap * HEAD_ROWS
    out_ref[...] = jnp.zeros_like(out_ref)
    meta_ref[...] = jnp.zeros_like(meta_ref)
    moves[0].wait()
    moves[1].wait()
    parent = parent_ref[...]
    names, ranks = slot_ranks(owner_ref, cap, out_ref.shape[0])
    for r in range(count):
        meta_ref[names[r], pl.ds(ranks[r], 1), :] = jnp.full((1, HEAD_DIM), parent[0, r].astype(jnp.float32))
    out_ref[:, pl.ds(KV_HEADS * head_span, 16), :] = meta_ref[...].astype(jnp.bfloat16)
    moves[2].wait()
    for r in range(count):
        d, rank = names[r], ranks[r]
        for g in range(KV_HEADS):
            start = pl.multiple_of(g * head_span + rank * HEAD_ROWS, HEAD_ROWS)
            out_ref[d, pl.ds(start, HEAD_ROWS), :] = query_ref[r, pl.ds(g * HEAD_ROWS, HEAD_ROWS), :]
    for move in moves[3:]:
        move.wait()


def idle_kernel(*refs):
    tables, (out_ref, *copies) = refs[: len(refs) // 2], refs[len(refs) // 2 :]
    out_ref[...] = jnp.zeros_like(out_ref)
    for table, copy in zip(tables, copies):
        copy[...] = table[...]


def two_codes(values, steps):
    scaled = values * steps
    whole = jnp.floor(scaled)
    rest = jnp.minimum(jnp.floor((scaled - whole) * 65536.0 + 0.5), 65535.0) - 32768.0
    return whole, rest


def from_codes(whole, rest, steps):
    return (whole + (rest + 32768.0) * (1.0 / 65536.0)) * (1.0 / steps)


def coded_rows(blended):
    reach = jnp.maximum(jnp.max(jnp.abs(blended), axis=1, keepdims=True), 1e-30)
    factor = pltpu.reciprocal(reach, approx=True) * CODE_TOP
    return jnp.round(blended * factor).astype(jnp.int32).astype(jnp.int16), factor


def coded_stats(stats):
    flat = stats.T
    top, total, factor = (flat[k * KV_HEADS : (k + 1) * KV_HEADS, :] for k in range(3))
    codes = two_codes(top * SCALE + jnp.log(total), LOG_STEPS)
    codes += two_codes(-jnp.log2(factor * total), SCALE_STEPS)
    return jnp.concatenate(codes, axis=0).astype(jnp.int32).astype(jnp.int16)


def decoded_stats(codes):
    codes = codes.astype(jnp.int32).astype(jnp.float32)
    codes = [codes[..., k * KV_HEADS : (k + 1) * KV_HEADS, :] for k in range(4)]
    log_total = from_codes(codes[0], codes[1], LOG_STEPS)
    return jnp.concatenate([log_total, jnp.exp2(from_codes(codes[2], codes[3], SCALE_STEPS))], axis=-2)


def parent_kernel(
    cap, chunk, pages_ref, len_ref, recv_ref, store_ref, out_ref, spare_hbm, spare_ref, key_ref, value_ref, sem
):
    spare_ref[...] = jnp.zeros_like(spare_ref)
    spare_copy = pltpu.make_async_copy(spare_ref, spare_hbm, sem)
    spare_copy.start()
    parents, page_count = pages_ref.shape
    pages, lengths = pages_ref[...], len_ref[...]
    sources = recv_ref.shape[0]
    head_span = cap * HEAD_ROWS
    tokens = page_count * PAGE
    heads = range(KV_HEADS)
    for p in range(parents):
        for i in range(page_count):
            start = pl.multiple_of(pages[p, i] * PAGE, PAGE)
            page = store_ref[pl.ds(start, PAGE), :]
            for g in heads:
                span = (g, pl.ds(i * PAGE, PAGE), pl.ds(p * HEAD_DIM, HEAD_DIM))
                key_ref[span] = page[:, g * HEAD_DIM : (g + 1) * HEAD_DIM]
                value_ref[span] = page[:, KEY_WIDTH + g * HEAD_DIM : KEY_WIDTH + (g + 1) * HEAD_DIM]

    rows = chunk * head_span
    lanes = iota((rows, HEAD_DIM), 1)
    positions = iota((rows, tokens), 1)

    def body(c, carry):
        part = pl.ds(c * chunk, chunk)
        meta = recv_ref[part, pl.ds(KV_HEADS * head_span, 16), :].astype(jnp.float32)
        picks = [
            jnp.broadcast_to(meta[:, s : s + 1, :], (chunk, HEAD_ROWS, HEAD_DIM)) for s in range(cap)
        ]
        parent = jnp.concatenate(picks, axis=1).reshape(rows, HEAD_DIM)
        limit = jnp.full((rows, HEAD_DIM), lengths[0, 0], jnp.int32)
        for p in range(1, parents):
            limit = jnp.where(parent == p, lengths[0, p], limit)
        bias = jnp.where(positions < limit[:, :1], 0.0, MASKED)
        parent_low = parent.astype(jnp.bfloat16)

        def scores_of(g):
            query = recv_ref[part, pl.ds(g * head_span, head_span), :].reshape(rows, HEAD_DIM)
            query = jnp.concatenate(
                [jnp.where(parent_low == p, query, jnp.zeros_like(query)) for p in range(parents)], axis=1
            )
            return lax.dot_general(query, key_ref[g], NT, preferred_element_type=jnp.float32)

        def softmax_of(scores):
            scores = scores + bias
            top = jnp.max(scores, axis=1, keepdims=True)
            terms = jnp.exp2((scores - top) * (SCALE * LOG2_E))
            return terms.astype(jnp.bfloat16), top, jnp.sum(terms, axis=1, keepdims=True)

        def blended_of(g, weights):
            both = jnp.dot(weights, value_ref[g], preferred_element_type=jnp.float32)
            blended = both[:, :HEAD_DIM]
            for p in range(1, parents):
                blended = jnp.where(parent == p, both[:, p * HEAD_DIM : (p + 1) * HEAD_DIM], blended)
            return blended

        scores = [scores_of(g) for g in heads]
        softmaxes = [softmax_of(scores[g]) for g in heads]
        blends = [blended_of(g, softmaxes[g][0]) for g in heads]
        stats = jnp.zeros((rows, HEAD_DIM), jnp.float32)
        for g in heads:
            coded, factor = coded_rows(blends[g])
            out_ref[part, pl.ds(g * head_span, head_span), :] = coded.reshape(chunk, head_span, HEAD_DIM)
            for k, value in enumerate((softmaxes[g][1], softmaxes[g][2], factor)):
                stats = jnp.where(lanes == k * KV_HEADS + g, value, stats)
        flat = coded_stats(stats)
        for j in range(chunk):
            piece = flat[:, j * head_span : (j + 1) * head_span]
            if head_span < HEAD_DIM:
                piece = jnp.concatenate(
                    [piece, jnp.zeros((STAT_ROWS, HEAD_DIM - head_span), jnp.int16)], axis=1
                )
            out_ref[c * chunk + j, pl.ds(KV_HEADS * head_span, STAT_ROWS), :] = piece
        return carry

    lax.fori_loop(0, sources // chunk, body, 0, unroll=sources == chunk)
    spare_copy.wait()


def fill_suffix_bias(pages_ref, len_ref, bias_ref, last_of):
    page_count, count = pages_ref.shape
    pages, lengths = pages_ref[...], len_ref[...]
    row, lane = iota((PAGE, HEAD_DIM), 0), iota((PAGE, HEAD_DIM), 1)
    for r in range(count):
        for i in range(page_count):
            keep = (lane // 2 == r) & (row + i * PAGE <= last_of(lengths[0, r], lane % 2))
            start = pl.multiple_of(pages[i, r] * PAGE, PAGE)
            bias_ref[pl.ds(start, PAGE), :] = jnp.where(keep, 0.0, MASKED).astype(jnp.bfloat16)


def own_pick(count):
    rows = count * HEAD_ROWS
    row, lane = iota((rows, HEAD_DIM), 0), iota((rows, HEAD_DIM), 1)
    return jnp.where(lane == (row // HEAD_ROWS) * 2 + row % 2, 1.0, 0.0).astype(jnp.bfloat16)


def prefill_kernel(pages_ref, len_ref, query_ref, store_ref, out_ref, bias_ref):
    count = query_ref.shape[0]
    rows = count * HEAD_ROWS
    fill_suffix_bias(pages_ref, len_ref, bias_ref, lambda length, t: length - 2 + t)
    pick = own_pick(count)
    for g in range(KV_HEADS):
        query = query_ref[:, pl.ds(g * HEAD_ROWS, HEAD_ROWS), :].reshape(rows, HEAD_DIM)
        keys = store_ref[:, pl.ds(g * HEAD_DIM, HEAD_DIM)]
        values = store_ref[:, pl.ds(KEY_WIDTH + g * HEAD_DIM, HEAD_DIM)]
        scores = lax.dot_general(
            jnp.concatenate([query, pick], axis=1),
            jnp.concatenate([keys, bias_ref[...]], axis=1),
            NT,
            preferred_element_type=jnp.float32,
        ) * SCALE
        terms = jnp.exp(scores - jnp.max(scores, axis=1, keepdims=True))
        total = jnp.sum(terms, axis=1, keepdims=True)
        blended = jnp.dot(terms.astype(jnp.bfloat16), values, preferred_element_type=jnp.float32)
        out_ref[:, pl.ds(g * HEAD_ROWS, HEAD_ROWS), :] = (
            (blended / total).astype(jnp.bfloat16).reshape(count, HEAD_ROWS, HEAD_DIM)
        )


def local_kernel(cap, pages_ref, len_ref, query_ref, store_ref, step_ref, spare_ref, out_ref, bias_ref):
    count = query_ref.shape[0]
    rows = count * HEAD_ROWS
    head_span = cap * HEAD_ROWS
    blocks = count // cap
    fill_suffix_bias(pages_ref, len_ref, bias_ref, lambda length, t: length - 1)
    steps = 2 * count
    step_pad = -steps % HEAD_DIM
    key_row, lane = iota((steps + step_pad, HEAD_DIM), 0), iota((steps + step_pad, HEAD_DIM), 1)
    seen = (key_row // 2 == lane // 2) & (key_row % 2 <= lane % 2) & (key_row < steps)
    step_bias = jnp.where(seen, 0.0, MASKED).astype(jnp.bfloat16)
    pad = jnp.zeros((step_pad, HEAD_DIM), jnp.bfloat16)

    def step_rows(c):
        return jnp.concatenate([step_ref[r, 2 * c : 2 * c + 2, :] for r in range(count)] + [pad], axis=0)

    pick = own_pick(count)
    lanes = iota((rows, HEAD_DIM), 1)
    stats = jnp.zeros((rows, HEAD_DIM), jnp.float32)
    for g in range(KV_HEADS):
        query = query_ref[:, pl.ds(g * HEAD_ROWS, HEAD_ROWS), :].reshape(rows, HEAD_DIM)
        query = jnp.concatenate([query, pick], axis=1)
        keys = jnp.concatenate([store_ref[:, pl.ds(g * HEAD_DIM, HEAD_DIM)], bias_ref[...]], axis=1)
        step_keys = jnp.concatenate([step_rows(g), step_bias], axis=1)
        values = store_ref[:, pl.ds(KEY_WIDTH + g * HEAD_DIM, HEAD_DIM)]
        step_values = step_rows(KV_HEADS + g)
        scores = lax.dot_general(query, keys, NT, preferred_element_type=jnp.float32)
        step_scores = lax.dot_general(query, step_keys, NT, preferred_element_type=jnp.float32)
        top = jnp.maximum(
            jnp.max(scores, axis=1, keepdims=True), jnp.max(step_scores, axis=1, keepdims=True)
        )
        terms = jnp.exp2((scores - top) * (SCALE * LOG2_E))
        step_terms = jnp.exp2((step_scores - top) * (SCALE * LOG2_E))
        total = jnp.sum(terms, axis=1, keepdims=True) + jnp.sum(step_terms, axis=1, keepdims=True)
        blended = jnp.dot(terms.astype(jnp.bfloat16), values, preferred_element_type=jnp.float32)
        blended = blended + jnp.dot(
            step_terms.astype(jnp.bfloat16), step_values, preferred_element_type=jnp.float32
        )
        coded, factor = coded_rows(blended)
        out_ref[:, pl.ds(g * head_span, head_span), :] = coded.reshape(blocks, head_span, HEAD_DIM)
        for k, value in enumerate((top, total, factor)):
            stats = jnp.where(lanes == k * KV_HEADS + g, value, stats)
    flat = coded_stats(stats)
    for j in range(rows // HEAD_DIM):
        out_ref[j, pl.ds(KV_HEADS * head_span, STAT_ROWS), :] = flat[:, j * HEAD_DIM : (j + 1) * HEAD_DIM]


def merge_kernel(cap, owner_ref, back_ref, own_ref, out_ref, decoded_ref):
    count = out_ref.shape[0]
    rows = count * HEAD_ROWS
    head_span = cap * HEAD_ROWS
    stat_span = pl.ds(KV_HEADS * head_span, STAT_ROWS)
    decoded_ref[...] = decoded_stats(back_ref[:, stat_span, :])
    own = jnp.concatenate([decoded_stats(own_ref[j, stat_span, :]) for j in range(rows // HEAD_DIM)], axis=1)

    names, ranks = slot_ranks(owner_ref, cap, back_ref.shape[0])
    per_tile = HEAD_DIM // HEAD_ROWS
    place = iota((2 * KV_HEADS, HEAD_DIM), 1) // HEAD_ROWS
    tiles = []
    for first in range(0, count, per_tile):
        tile = jnp.zeros((2 * KV_HEADS, HEAD_DIM), jnp.float32)
        for r in range(first, min(first + per_tile, count)):
            shift = lax.rem((r - first) * HEAD_ROWS - ranks[r] * HEAD_ROWS + HEAD_DIM, HEAD_DIM)
            tile = jnp.where(place == r - first, pltpu.roll(decoded_ref[names[r]], shift, 1), tile)
        tiles.append(tile)
    flat = jnp.concatenate(tiles, axis=1)[:, :rows]
    part_top, own_top = flat[:KV_HEADS], own[:KV_HEADS]
    top = jnp.maximum(own_top, part_top)
    own_weight, part_weight = jnp.exp(own_top - top), jnp.exp(part_top - top)
    inverse = 1.0 / (own_weight + part_weight)
    weights = [own[KV_HEADS:] * own_weight * inverse, flat[KV_HEADS:] * part_weight * inverse]
    weights.append(jnp.zeros((HEAD_DIM - 2 * KV_HEADS, rows), jnp.float32))
    weights = jnp.concatenate(weights, axis=0).T
    for r in range(count):
        span = slice(r * HEAD_ROWS, (r + 1) * HEAD_ROWS)
        for g in range(KV_HEADS):
            start = pl.multiple_of(g * head_span + ranks[r] * HEAD_ROWS, HEAD_ROWS)
            part = back_ref[names[r], pl.ds(start, HEAD_ROWS), :].astype(jnp.int32).astype(jnp.float32)
            own_start = g * head_span + r % cap * HEAD_ROWS
            own_part = own_ref[r // cap, pl.ds(own_start, HEAD_ROWS), :].astype(jnp.int32).astype(jnp.float32)
            merged = own_part * weights[span, g : g + 1]
            merged = merged + part * weights[span, KV_HEADS + g : KV_HEADS + g + 1]
            out_ref[r, pl.ds(g * HEAD_ROWS, HEAD_ROWS), :] = merged.astype(jnp.bfloat16)


def call(kernel, out_shape, arrays, scratch, cost=None, in_space=pltpu.VMEM, out_space=pltpu.VMEM):
    take = pl.BlockSpec(memory_space=in_space)
    if not isinstance(out_space, tuple):
        out_space = jax.tree.map(lambda _: out_space, out_shape)
    return pl.pallas_call(
        kernel,
        out_shape=out_shape,
        in_specs=[take] * len(arrays),
        out_specs=jax.tree.map(lambda space: pl.BlockSpec(memory_space=space), out_space),
        cost_estimate=cost,
        scratch_shapes=scratch,
        compiler_params=pltpu.CompilerParams(vmem_limit_bytes=VMEM_BYTES),
    )(*arrays)


def head_rows(tokens):
    count, pair, width = tokens.shape
    blocks = tokens.reshape(count, pair, width // HEAD_DIM, HEAD_DIM)
    return blocks.transpose(0, 2, 1, 3).reshape(count, -1, HEAD_DIM)


def local(
    kv_store, queries, step_kv, suffix_pages, suffix_len, owner, parent_id, parent_pages, parent_len
):
    decoding = lax.axis_index("role") == 1
    seq_count = lax.axis_size("seq")
    store = kv_store[0]
    count, pair, width = queries.shape[1:]
    cap = max(2, 2 * count // seq_count)
    head_span = cap * HEAD_ROWS
    chunk = max(1, min(seq_count, 512 // head_span))
    query_rows = head_rows(queries[0])
    owner_row, parent_row = owner.reshape(1, -1), parent_id.reshape(1, -1)
    tables = (suffix_pages.T, suffix_len.reshape(1, -1), parent_pages, parent_len.reshape(1, -1))
    token_rows = store.shape[0]

    sent = jax.ShapeDtypeStruct((seq_count, KV_HEADS * head_span + 16, HEAD_DIM), jnp.bfloat16)
    answer = jax.ShapeDtypeStruct((seq_count, KV_HEADS * head_span + STAT_ROWS, HEAD_DIM), jnp.int16)
    own_part = jax.ShapeDtypeStruct((count // cap, *answer.shape[1:]), answer.dtype)
    result = jax.ShapeDtypeStruct(query_rows.shape, jnp.bfloat16)
    bias = pltpu.VMEM((token_rows, HEAD_DIM), jnp.bfloat16)
    rows = count * HEAD_ROWS
    part = (KV_HEADS, rows, HEAD_DIM)

    def exchange(block):
        return lax.all_to_all(block, "seq", split_axis=0, concat_axis=0, tiled=True)

    def tokens_of(rows):
        return rows.reshape(count, width // HEAD_DIM, pair, HEAD_DIM).transpose(0, 2, 1, 3).reshape(
            1, count, pair, width
        )

    handed = (sent, *(jax.ShapeDtypeStruct(t.shape, t.dtype) for t in (owner_row, *tables)))

    def send_queries(query_rows):
        packed, *copies = call(
            functools.partial(pack_kernel, cap),
            handed,
            (query_rows, owner_row, parent_row, *tables),
            [
                pltpu.VMEM(query_rows.shape, jnp.bfloat16),
                pltpu.VMEM(parent_row.shape, jnp.int32),
                pltpu.VMEM((seq_count, 16, HEAD_DIM), jnp.float32),
                pltpu.SemaphoreType.DMA((3 + len(tables),)),
            ],
            in_space=pl.ANY,
        )
        return packed, *copies

    def idle(query_rows):
        return call(idle_kernel, handed, (owner_row, *tables), [])

    packed, owner_row, *tables = lax.cond(decoding, send_queries, idle, query_rows)
    query_after, packed = lax.optimization_barrier((query_rows, packed))
    decode_query = lax.ppermute(query_after, "role", [(0, 1), (1, 0)])
    received = lax.cond(decoding, exchange, lambda block: jnp.zeros_like(block), packed)

    def answer_queries(received, decode_query):
        parents, page_count = parent_pages.shape
        beside = (KV_HEADS, page_count * PAGE, parents * HEAD_DIM)
        return call(
            functools.partial(parent_kernel, cap, chunk),
            (answer, own_part),
            (*tables[2:], received, store),
            [
                pltpu.VMEM(own_part.shape, jnp.int16),
                pltpu.VMEM(beside, jnp.bfloat16),
                pltpu.VMEM(beside, jnp.bfloat16),
                pltpu.SemaphoreType.DMA,
            ],
            out_space=(pltpu.VMEM, pl.ANY),
        )

    def attend_own(received, decode_query):
        return call(
            functools.partial(local_kernel, cap),
            (answer, own_part),
            (*tables[:2], decode_query, store, head_rows(step_kv)),
            [bias],
        )

    parts, own = lax.cond(decoding, answer_queries, attend_own, received, decode_query)
    own = lax.ppermute(own, "role", [(0, 1), (1, 0)])
    back = lax.cond(decoding, exchange, lambda block: jnp.zeros_like(block), parts)

    def merge(back, own, query_rows):
        return tokens_of(
            call(
                functools.partial(merge_kernel, cap),
                result,
                (owner_row, back, own),
                [pltpu.VMEM((seq_count, 2 * KV_HEADS, HEAD_DIM), jnp.float32)],
            )
        )

    def prefill(back, own, query_rows):
        return tokens_of(call(prefill_kernel, result, (*tables[:2], query_rows, store), [bias]))

    return lax.cond(decoding, merge, prefill, back, own, query_rows)


def solution(mesh):
    in_specs = (
        P("role", ("groups", "seq"), None),
        P("role", ("groups", "seq"), None, None),
        P(("groups", "seq"), None, None),
        P(("groups", "seq"), None),
        P(("groups", "seq")),
        P(("groups", "seq"), None),
        P(("groups", "seq")),
        P(("groups", "seq"), None),
        P(("groups", "seq")),
    )
    out_specs = P("role", ("groups", "seq"), None, None)
    return jax.shard_map(local, mesh=mesh, in_specs=in_specs, out_specs=out_specs, check_vma=False)
```

```python
import functools

import jax
import jax.numpy as jnp
from jax import lax
from jax.experimental import pallas as pl
from jax.experimental.pallas import tpu as pltpu
from jax.sharding import PartitionSpec as P

HEAD_DIM = 128
KV_HEADS = 4
GROUP = 8
PAGE = 16
HEAD_ROWS = 2 * GROUP
KEY_WIDTH = KV_HEADS * HEAD_DIM
SCALE = HEAD_DIM ** (-0.5)
MASKED = -1e30
STAT_ROWS = 4 * KV_HEADS
LOG_STEPS = 4.0
SCALE_STEPS = 128.0
CODE_TOP = 32600.0
LOG2_E = 1.4426950408889634
VMEM_BYTES = 48 * 1024 * 1024

NT = (((1,), (1,)), ((), ()))


def iota(shape, dim):
    return lax.broadcasted_iota(jnp.int32, shape, dim)


def slot_ranks(owner_ref, cap, owners):
    owner = owner_ref[...]
    bits = cap.bit_length()
    per_word = 30 // bits
    words = [jnp.int32(0)] * -(-owners // per_word)
    names, ranks = [], []
    for r in range(owner.shape[1]):
        name = owner[0, r]
        word, rank = name // per_word if len(words) > 1 else 0, jnp.int32(0)
        shift = (name - word * per_word) * bits
        for k, counts in enumerate(words):
            here = (word == k) if len(words) > 1 else True
            count = (counts >> shift) & ((1 << bits) - 1)
            step = jnp.int32(1) << shift
            if len(words) > 1:
                count, step = jnp.where(here, count, 0), jnp.where(here, step, 0)
            rank = rank + count
            words[k] = counts + step
        names.append(name)
        ranks.append(rank)
    return names, ranks


def pack_kernel(cap, query_hbm, owner_hbm, parent_hbm, *refs):
    *refs, query_ref, parent_ref, meta_ref, sems = refs
    tables, (out_ref, owner_ref, *copies) = refs[: len(refs) // 2 - 1], refs[len(refs) // 2 - 1 :]
    moves = [(owner_hbm, owner_ref), (parent_hbm, parent_ref), (query_hbm, query_ref), *zip(tables, copies)]
    moves = [pltpu.make_async_copy(src, dst, sems.at[k]) for k, (src, dst) in enumerate(moves)]
    for move in moves:
        move.start()
    count = query_ref.shape[0]
    head_span = cap * HEAD_ROWS
    out_ref[...] = jnp.zeros_like(out_ref)
    meta_ref[...] = jnp.zeros_like(meta_ref)
    moves[0].wait()
    moves[1].wait()
    parent = parent_ref[...]
    names, ranks = slot_ranks(owner_ref, cap, out_ref.shape[0])
    for r in range(count):
        meta_ref[names[r], pl.ds(ranks[r], 1), :] = jnp.full((1, HEAD_DIM), parent[0, r].astype(jnp.float32))
    out_ref[:, pl.ds(KV_HEADS * head_span, 16), :] = meta_ref[...].astype(jnp.bfloat16)
    moves[2].wait()
    for r in range(count):
        d, rank = names[r], ranks[r]
        for g in range(KV_HEADS):
            start = pl.multiple_of(g * head_span + rank * HEAD_ROWS, HEAD_ROWS)
            out_ref[d, pl.ds(start, HEAD_ROWS), :] = query_ref[r, pl.ds(g * HEAD_ROWS, HEAD_ROWS), :]
    for move in moves[3:]:
        move.wait()


def zero_kernel(*refs):
    for ref in refs:
        ref[...] = jnp.zeros_like(ref)


def hand_kernel(*refs):
    half = len(refs) // 2
    for table, copy in zip(refs[:half], refs[half:]):
        copy[...] = table[...]


def two_codes(values, steps):
    scaled = values * steps
    whole = jnp.floor(scaled)
    rest = jnp.minimum(jnp.floor((scaled - whole) * 65536.0 + 0.5), 65535.0) - 32768.0
    return whole, rest


def from_codes(whole, rest, steps):
    return (whole + (rest + 32768.0) * (1.0 / 65536.0)) * (1.0 / steps)


def coded_rows(blended):
    reach = jnp.maximum(jnp.max(jnp.abs(blended), axis=1, keepdims=True), 1e-30)
    factor = pltpu.reciprocal(reach, approx=True) * CODE_TOP
    return jnp.round(blended * factor).astype(jnp.int32).astype(jnp.int16), factor


def coded_stats(stats):
    flat = stats.T
    top, total, factor = (flat[k * KV_HEADS : (k + 1) * KV_HEADS, :] for k in range(3))
    codes = two_codes(top * SCALE + jnp.log(total), LOG_STEPS)
    codes += two_codes(-jnp.log2(factor * total), SCALE_STEPS)
    return jnp.concatenate(codes, axis=0).astype(jnp.int32).astype(jnp.int16)


def decoded_stats(codes):
    codes = codes.astype(jnp.int32).astype(jnp.float32)
    codes = [codes[..., k * KV_HEADS : (k + 1) * KV_HEADS, :] for k in range(4)]
    log_total = from_codes(codes[0], codes[1], LOG_STEPS)
    return jnp.concatenate([log_total, jnp.exp2(from_codes(codes[2], codes[3], SCALE_STEPS))], axis=-2)


def parent_kernel(
    cap, chunk, pages_ref, len_ref, recv_ref, store_ref, out_ref, spare_hbm, spare_ref, key_ref, value_ref, sem
):
    spare_ref[...] = jnp.zeros_like(spare_ref)
    spare_copy = pltpu.make_async_copy(spare_ref, spare_hbm, sem)
    spare_copy.start()
    parents, page_count = pages_ref.shape
    pages, lengths = pages_ref[...], len_ref[...]
    sources = recv_ref.shape[0]
    head_span = cap * HEAD_ROWS
    tokens = page_count * PAGE
    heads = range(KV_HEADS)
    for p in range(parents):
        for i in range(page_count):
            start = pl.multiple_of(pages[p, i] * PAGE, PAGE)
            page = store_ref[pl.ds(start, PAGE), :]
            for g in heads:
                span = (g, pl.ds(i * PAGE, PAGE), pl.ds(p * HEAD_DIM, HEAD_DIM))
                key_ref[span] = page[:, g * HEAD_DIM : (g + 1) * HEAD_DIM]
                value_ref[span] = page[:, KEY_WIDTH + g * HEAD_DIM : KEY_WIDTH + (g + 1) * HEAD_DIM]

    rows = chunk * head_span
    lanes = iota((rows, HEAD_DIM), 1)
    positions = iota((rows, tokens), 1)

    def body(c, carry):
        part = pl.ds(c * chunk, chunk)
        meta = recv_ref[part, pl.ds(KV_HEADS * head_span, 16), :].astype(jnp.float32)
        picks = [
            jnp.broadcast_to(meta[:, s : s + 1, :], (chunk, HEAD_ROWS, HEAD_DIM)) for s in range(cap)
        ]
        parent = jnp.concatenate(picks, axis=1).reshape(rows, HEAD_DIM)
        limit = jnp.full((rows, HEAD_DIM), lengths[0, 0], jnp.int32)
        for p in range(1, parents):
            limit = jnp.where(parent == p, lengths[0, p], limit)
        bias = jnp.where(positions < limit[:, :1], 0.0, MASKED)
        parent_low = parent.astype(jnp.bfloat16)

        def scores_of(g):
            query = recv_ref[part, pl.ds(g * head_span, head_span), :].reshape(rows, HEAD_DIM)
            query = jnp.concatenate(
                [jnp.where(parent_low == p, query, jnp.zeros_like(query)) for p in range(parents)], axis=1
            )
            return lax.dot_general(query, key_ref[g], NT, preferred_element_type=jnp.float32)

        def softmax_of(scores):
            scores = scores + bias
            top = jnp.max(scores, axis=1, keepdims=True)
            terms = jnp.exp2((scores - top) * (SCALE * LOG2_E))
            return terms.astype(jnp.bfloat16), top, jnp.sum(terms, axis=1, keepdims=True)

        def blended_of(g, weights):
            both = jnp.dot(weights, value_ref[g], preferred_element_type=jnp.float32)
            blended = both[:, :HEAD_DIM]
            for p in range(1, parents):
                blended = jnp.where(parent == p, both[:, p * HEAD_DIM : (p + 1) * HEAD_DIM], blended)
            return blended

        scores = [scores_of(g) for g in heads]
        softmaxes = [softmax_of(scores[g]) for g in heads]
        blends = [blended_of(g, softmaxes[g][0]) for g in heads]
        stats = jnp.zeros((rows, HEAD_DIM), jnp.float32)
        for g in heads:
            coded, factor = coded_rows(blends[g])
            out_ref[part, pl.ds(g * head_span, head_span), :] = coded.reshape(chunk, head_span, HEAD_DIM)
            for k, value in enumerate((softmaxes[g][1], softmaxes[g][2], factor)):
                stats = jnp.where(lanes == k * KV_HEADS + g, value, stats)
        flat = coded_stats(stats)
        for j in range(chunk):
            piece = flat[:, j * head_span : (j + 1) * head_span]
            if head_span < HEAD_DIM:
                piece = jnp.concatenate(
                    [piece, jnp.zeros((STAT_ROWS, HEAD_DIM - head_span), jnp.int16)], axis=1
                )
            out_ref[c * chunk + j, pl.ds(KV_HEADS * head_span, STAT_ROWS), :] = piece
        return carry

    lax.fori_loop(0, sources // chunk, body, 0, unroll=sources == chunk)
    spare_copy.wait()


def fill_suffix_bias(pages_ref, len_ref, bias_ref, last_of):
    page_count, count = pages_ref.shape
    pages, lengths = pages_ref[...], len_ref[...]
    row, lane = iota((PAGE, HEAD_DIM), 0), iota((PAGE, HEAD_DIM), 1)
    for r in range(count):
        for i in range(page_count):
            keep = (lane // 2 == r) & (row + i * PAGE <= last_of(lengths[0, r], lane % 2))
            start = pl.multiple_of(pages[i, r] * PAGE, PAGE)
            bias_ref[pl.ds(start, PAGE), :] = jnp.where(keep, 0.0, MASKED).astype(jnp.bfloat16)


def own_pick(count):
    rows = count * HEAD_ROWS
    row, lane = iota((rows, HEAD_DIM), 0), iota((rows, HEAD_DIM), 1)
    return jnp.where(lane == (row // HEAD_ROWS) * 2 + row % 2, 1.0, 0.0).astype(jnp.bfloat16)


def prefill_kernel(pages_ref, len_ref, query_ref, store_ref, out_ref, bias_ref):
    count = query_ref.shape[0]
    rows = count * HEAD_ROWS
    fill_suffix_bias(pages_ref, len_ref, bias_ref, lambda length, t: length - 2 + t)
    pick = own_pick(count)
    for g in range(KV_HEADS):
        query = query_ref[:, pl.ds(g * HEAD_ROWS, HEAD_ROWS), :].reshape(rows, HEAD_DIM)
        keys = store_ref[:, pl.ds(g * HEAD_DIM, HEAD_DIM)]
        values = store_ref[:, pl.ds(KEY_WIDTH + g * HEAD_DIM, HEAD_DIM)]
        scores = lax.dot_general(
            jnp.concatenate([query, pick], axis=1),
            jnp.concatenate([keys, bias_ref[...]], axis=1),
            NT,
            preferred_element_type=jnp.float32,
        ) * SCALE
        terms = jnp.exp(scores - jnp.max(scores, axis=1, keepdims=True))
        total = jnp.sum(terms, axis=1, keepdims=True)
        blended = jnp.dot(terms.astype(jnp.bfloat16), values, preferred_element_type=jnp.float32)
        out_ref[:, pl.ds(g * HEAD_ROWS, HEAD_ROWS), :] = (
            (blended / total).astype(jnp.bfloat16).reshape(count, HEAD_ROWS, HEAD_DIM)
        )


def local_kernel(cap, pages_ref, len_ref, query_ref, store_ref, step_ref, spare_ref, out_ref, bias_ref):
    count = query_ref.shape[0]
    rows = count * HEAD_ROWS
    head_span = cap * HEAD_ROWS
    blocks = count // cap
    fill_suffix_bias(pages_ref, len_ref, bias_ref, lambda length, t: length - 1)
    steps = 2 * count
    step_pad = -steps % HEAD_DIM
    key_row, lane = iota((steps + step_pad, HEAD_DIM), 0), iota((steps + step_pad, HEAD_DIM), 1)
    seen = (key_row // 2 == lane // 2) & (key_row % 2 <= lane % 2) & (key_row < steps)
    step_bias = jnp.where(seen, 0.0, MASKED).astype(jnp.bfloat16)
    pad = jnp.zeros((step_pad, HEAD_DIM), jnp.bfloat16)

    def step_rows(c):
        return jnp.concatenate([step_ref[r, 2 * c : 2 * c + 2, :] for r in range(count)] + [pad], axis=0)

    pick = own_pick(count)
    lanes = iota((rows, HEAD_DIM), 1)
    stats = jnp.zeros((rows, HEAD_DIM), jnp.float32)
    for g in range(KV_HEADS):
        query = query_ref[:, pl.ds(g * HEAD_ROWS, HEAD_ROWS), :].reshape(rows, HEAD_DIM)
        query = jnp.concatenate([query, pick], axis=1)
        keys = jnp.concatenate([store_ref[:, pl.ds(g * HEAD_DIM, HEAD_DIM)], bias_ref[...]], axis=1)
        step_keys = jnp.concatenate([step_rows(g), step_bias], axis=1)
        values = store_ref[:, pl.ds(KEY_WIDTH + g * HEAD_DIM, HEAD_DIM)]
        step_values = step_rows(KV_HEADS + g)
        scores = lax.dot_general(query, keys, NT, preferred_element_type=jnp.float32)
        step_scores = lax.dot_general(query, step_keys, NT, preferred_element_type=jnp.float32)
        top = jnp.maximum(
            jnp.max(scores, axis=1, keepdims=True), jnp.max(step_scores, axis=1, keepdims=True)
        )
        terms = jnp.exp2((scores - top) * (SCALE * LOG2_E))
        step_terms = jnp.exp2((step_scores - top) * (SCALE * LOG2_E))
        total = jnp.sum(terms, axis=1, keepdims=True) + jnp.sum(step_terms, axis=1, keepdims=True)
        blended = jnp.dot(terms.astype(jnp.bfloat16), values, preferred_element_type=jnp.float32)
        blended = blended + jnp.dot(
            step_terms.astype(jnp.bfloat16), step_values, preferred_element_type=jnp.float32
        )
        coded, factor = coded_rows(blended)
        out_ref[:, pl.ds(g * head_span, head_span), :] = coded.reshape(blocks, head_span, HEAD_DIM)
        for k, value in enumerate((top, total, factor)):
            stats = jnp.where(lanes == k * KV_HEADS + g, value, stats)
    flat = coded_stats(stats)
    for j in range(rows // HEAD_DIM):
        out_ref[j, pl.ds(KV_HEADS * head_span, STAT_ROWS), :] = flat[:, j * HEAD_DIM : (j + 1) * HEAD_DIM]


def spread_rows(rows):
    high = rows.astype(jnp.bfloat16)
    rest = rows - high.astype(jnp.float32)
    middle = rest.astype(jnp.bfloat16)
    low = (rest - middle.astype(jnp.float32)).astype(jnp.bfloat16)
    count = rows.shape[0]
    shape = (3 * count, count * HEAD_DIM)
    chosen = iota(shape, 0) % count == iota(shape, 1) // HEAD_DIM
    return lax.dot_general(
        jnp.concatenate([high, middle, low], axis=0),
        jnp.where(chosen, 1.0, 0.0).astype(jnp.bfloat16),
        (((0,), (0,)), ((), ())),
        preferred_element_type=jnp.float32,
    )


def merge_kernel(cap, owner_ref, back_ref, own_ref, out_ref, decoded_ref):
    count = out_ref.shape[0]
    rows = count * HEAD_ROWS
    head_span = cap * HEAD_ROWS
    stat_span = pl.ds(KV_HEADS * head_span, STAT_ROWS)
    decoded_ref[...] = decoded_stats(back_ref[:, stat_span, :])
    own = jnp.concatenate([decoded_stats(own_ref[j, stat_span, :]) for j in range(rows // HEAD_DIM)], axis=1)

    names, ranks = slot_ranks(owner_ref, cap, back_ref.shape[0])
    per_tile = HEAD_DIM // HEAD_ROWS
    place = iota((2 * KV_HEADS, HEAD_DIM), 1) // HEAD_ROWS
    tiles = []
    for first in range(0, count, per_tile):
        tile = jnp.zeros((2 * KV_HEADS, HEAD_DIM), jnp.float32)
        for r in range(first, min(first + per_tile, count)):
            shift = lax.rem((r - first) * HEAD_ROWS - ranks[r] * HEAD_ROWS + HEAD_DIM, HEAD_DIM)
            tile = jnp.where(place == r - first, pltpu.roll(decoded_ref[names[r]], shift, 1), tile)
        tiles.append(tile)
    flat = jnp.concatenate(tiles, axis=1)[:, :rows]
    part_top, own_top = flat[:KV_HEADS], own[:KV_HEADS]
    top = jnp.maximum(own_top, part_top)
    own_weight, part_weight = jnp.exp(own_top - top), jnp.exp(part_top - top)
    inverse = 1.0 / (own_weight + part_weight)
    weights = [own[KV_HEADS:] * own_weight * inverse, flat[KV_HEADS:] * part_weight * inverse]
    weights = spread_rows(jnp.concatenate(weights, axis=0))
    for r in range(count):
        span = slice(r * HEAD_ROWS, (r + 1) * HEAD_ROWS)
        for g in range(KV_HEADS):
            start = pl.multiple_of(g * head_span + ranks[r] * HEAD_ROWS, HEAD_ROWS)
            part = back_ref[names[r], pl.ds(start, HEAD_ROWS), :].astype(jnp.int32).astype(jnp.float32)
            own_start = g * head_span + r % cap * HEAD_ROWS
            own_part = own_ref[r // cap, pl.ds(own_start, HEAD_ROWS), :].astype(jnp.int32).astype(jnp.float32)
            merged = own_part * weights[span, g * HEAD_DIM : (g + 1) * HEAD_DIM]
            k = KV_HEADS + g
            merged = merged + part * weights[span, k * HEAD_DIM : (k + 1) * HEAD_DIM]
            out_ref[r, pl.ds(g * HEAD_ROWS, HEAD_ROWS), :] = merged.astype(jnp.bfloat16)


def call(kernel, out_shape, arrays, scratch, cost=None, in_space=pltpu.VMEM, out_space=pltpu.VMEM):
    take = pl.BlockSpec(memory_space=in_space)
    if not isinstance(out_space, tuple):
        out_space = jax.tree.map(lambda _: out_space, out_shape)
    return pl.pallas_call(
        kernel,
        out_shape=out_shape,
        in_specs=[take] * len(arrays),
        out_specs=jax.tree.map(lambda space: pl.BlockSpec(memory_space=space), out_space),
        cost_estimate=cost,
        scratch_shapes=scratch,
        compiler_params=pltpu.CompilerParams(vmem_limit_bytes=VMEM_BYTES),
    )(*arrays)


def head_rows(tokens):
    count, pair, width = tokens.shape
    blocks = tokens.reshape(count, pair, width // HEAD_DIM, HEAD_DIM)
    return blocks.transpose(0, 2, 1, 3).reshape(count, -1, HEAD_DIM)


def local(
    kv_store, queries, step_kv, suffix_pages, suffix_len, owner, parent_id, parent_pages, parent_len
):
    decoding = lax.axis_index("role") == 1
    seq_count = lax.axis_size("seq")
    store = kv_store[0]
    count, pair, width = queries.shape[1:]
    cap = max(2, 2 * count // seq_count)
    head_span = cap * HEAD_ROWS
    chunk = max(1, min(seq_count, 512 // head_span))
    query_rows = head_rows(queries[0])
    owner_row, parent_row = owner.reshape(1, -1), parent_id.reshape(1, -1)
    parent_tables = (parent_pages, parent_len.reshape(1, -1))
    suffix_tables = (suffix_pages.T, suffix_len.reshape(1, -1))
    token_rows = store.shape[0]

    sent = jax.ShapeDtypeStruct((seq_count, KV_HEADS * head_span + 16, HEAD_DIM), jnp.bfloat16)
    answer = jax.ShapeDtypeStruct((seq_count, KV_HEADS * head_span + STAT_ROWS, HEAD_DIM), jnp.int16)
    own_part = jax.ShapeDtypeStruct((count // cap, *answer.shape[1:]), answer.dtype)
    result = jax.ShapeDtypeStruct(query_rows.shape, jnp.bfloat16)
    bias = pltpu.VMEM((token_rows, HEAD_DIM), jnp.bfloat16)
    rows = count * HEAD_ROWS
    part = (KV_HEADS, rows, HEAD_DIM)

    def exchange(block):
        return lax.all_to_all(block, "seq", split_axis=0, concat_axis=0, tiled=True)

    def tokens_of(rows):
        return rows.reshape(count, width // HEAD_DIM, pair, HEAD_DIM).transpose(0, 2, 1, 3).reshape(
            1, count, pair, width
        )

    def like(arrays):
        return tuple(jax.ShapeDtypeStruct(a.shape, a.dtype) for a in arrays)

    def zeros(shapes):
        return tuple(jnp.zeros(a.shape, a.dtype) for a in shapes)

    handed = (sent, *like((owner_row, *parent_tables)))

    def pack(query_rows):
        return call(
            functools.partial(pack_kernel, cap),
            handed,
            (query_rows, owner_row, parent_row, *parent_tables),
            [
                pltpu.VMEM(query_rows.shape, jnp.bfloat16),
                pltpu.VMEM(parent_row.shape, jnp.int32),
                pltpu.VMEM((seq_count, 16, HEAD_DIM), jnp.float32),
                pltpu.SemaphoreType.DMA((3 + len(parent_tables),)),
            ],
            in_space=pl.ANY,
        )

    packed, owner_row, *parent_tables = lax.cond(decoding, pack, lambda _: call(zero_kernel, handed, (), []), query_rows)
    query_after, packed = lax.optimization_barrier((query_rows, packed))
    decode_query = lax.ppermute(query_after, "role", [(0, 1), (1, 0)])

    def send(packed):
        return exchange(packed), *zeros(suffix_tables)

    def hand_on(packed):
        return jnp.zeros_like(packed), *call(hand_kernel, like(suffix_tables), suffix_tables, [])

    received, *suffix_tables = lax.cond(decoding, send, hand_on, packed)

    def answer_queries(received, decode_query):
        parents, page_count = parent_pages.shape
        beside = (KV_HEADS, page_count * PAGE, parents * HEAD_DIM)
        return call(
            functools.partial(parent_kernel, cap, chunk),
            (answer, own_part),
            (*parent_tables, received, store),
            [
                pltpu.VMEM(own_part.shape, jnp.int16),
                pltpu.VMEM(beside, jnp.bfloat16),
                pltpu.VMEM(beside, jnp.bfloat16),
                pltpu.SemaphoreType.DMA,
            ],
            out_space=(pltpu.VMEM, pl.ANY),
        )

    def attend_own(received, decode_query):
        return call(
            functools.partial(local_kernel, cap),
            (answer, own_part),
            (*suffix_tables, decode_query, store, head_rows(step_kv)),
            [bias],
        )

    parts, own = lax.cond(decoding, answer_queries, attend_own, received, decode_query)
    own = lax.ppermute(own, "role", [(0, 1), (1, 0)])
    back = lax.cond(decoding, exchange, lambda block: jnp.zeros_like(block), parts)

    def merge(back, own, query_rows):
        return tokens_of(
            call(
                functools.partial(merge_kernel, cap),
                result,
                (owner_row, back, own),
                [pltpu.VMEM((seq_count, 2 * KV_HEADS, HEAD_DIM), jnp.float32)],
            )
        )

    def prefill(back, own, query_rows):
        return tokens_of(call(prefill_kernel, result, (*suffix_tables, query_rows, store), [bias]))

    return lax.cond(decoding, merge, prefill, back, own, query_rows)


def solution(mesh):
    in_specs = (
        P("role", ("groups", "seq"), None),
        P("role", ("groups", "seq"), None, None),
        P(("groups", "seq"), None, None),
        P(("groups", "seq"), None),
        P(("groups", "seq")),
        P(("groups", "seq"), None),
        P(("groups", "seq")),
        P(("groups", "seq"), None),
        P(("groups", "seq")),
    )
    out_specs = P("role", ("groups", "seq"), None, None)
    return jax.shard_map(local, mesh=mesh, in_specs=in_specs, out_specs=out_specs, check_vma=False)
```

```python
import functools

import jax
import jax.numpy as jnp
from jax import lax
from jax.experimental import pallas as pl
from jax.experimental.pallas import tpu as pltpu
from jax.sharding import PartitionSpec as P

HEAD_DIM = 128
KV_HEADS = 4
GROUP = 8
PAGE = 16
HEAD_ROWS = 2 * GROUP
KEY_WIDTH = KV_HEADS * HEAD_DIM
SCALE = HEAD_DIM ** (-0.5)
MASKED = -1e30
STAT_ROWS = 4 * KV_HEADS
LOG_STEPS = 4.0
SCALE_STEPS = 128.0
CODE_TOP = 32600.0
LOG2_E = 1.4426950408889634
VMEM_BYTES = 48 * 1024 * 1024
PREFILL_VMEM_BYTES = (64 * 1024 - 1150) * 1024

NT = (((1,), (1,)), ((), ()))


def iota(shape, dim):
    return lax.broadcasted_iota(jnp.int32, shape, dim)


def slot_ranks(owner_ref, cap, owners):
    owner = owner_ref[...]
    bits = cap.bit_length()
    per_word = 30 // bits
    words = [jnp.int32(0)] * -(-owners // per_word)
    names, ranks = [], []
    for r in range(owner.shape[1]):
        name = owner[0, r]
        word, rank = name // per_word if len(words) > 1 else 0, jnp.int32(0)
        shift = (name - word * per_word) * bits
        for k, counts in enumerate(words):
            here = (word == k) if len(words) > 1 else True
            count = (counts >> shift) & ((1 << bits) - 1)
            step = jnp.int32(1) << shift
            if len(words) > 1:
                count, step = jnp.where(here, count, 0), jnp.where(here, step, 0)
            rank = rank + count
            words[k] = counts + step
        names.append(name)
        ranks.append(rank)
    return names, ranks


def pack_kernel(cap, query_hbm, owner_hbm, parent_hbm, *refs):
    *refs, query_ref, parent_ref, meta_ref, sems = refs
    tables, (out_ref, owner_ref, *copies) = refs[: len(refs) // 2 - 1], refs[len(refs) // 2 - 1 :]
    moves = [(owner_hbm, owner_ref), (parent_hbm, parent_ref), (query_hbm, query_ref), *zip(tables, copies)]
    moves = [pltpu.make_async_copy(src, dst, sems.at[k]) for k, (src, dst) in enumerate(moves)]
    for move in moves:
        move.start()
    count = query_ref.shape[0]
    head_span = cap * HEAD_ROWS
    out_ref[...] = jnp.zeros_like(out_ref)
    meta_ref[...] = jnp.zeros_like(meta_ref)
    moves[0].wait()
    moves[1].wait()
    parent = parent_ref[...]
    names, ranks = slot_ranks(owner_ref, cap, out_ref.shape[0])
    for r in range(count):
        meta_ref[names[r], pl.ds(ranks[r], 1), :] = jnp.full((1, HEAD_DIM), parent[0, r].astype(jnp.float32))
    out_ref[:, pl.ds(KV_HEADS * head_span, 16), :] = meta_ref[...].astype(jnp.bfloat16)
    moves[2].wait()
    for r in range(count):
        d, rank = names[r], ranks[r]
        for g in range(KV_HEADS):
            start = pl.multiple_of(g * head_span + rank * HEAD_ROWS, HEAD_ROWS)
            out_ref[d, pl.ds(start, HEAD_ROWS), :] = query_ref[r, pl.ds(g * HEAD_ROWS, HEAD_ROWS), :]
    for move in moves[3:]:
        move.wait()


def zero_kernel(*refs):
    for ref in refs:
        ref[...] = jnp.zeros_like(ref)


def hand_kernel(*refs):
    half = len(refs) // 2
    for table, copy in zip(refs[:half], refs[half:]):
        copy[...] = table[...]


def two_codes(values, steps):
    scaled = values * steps
    whole = jnp.floor(scaled)
    rest = jnp.minimum(jnp.floor((scaled - whole) * 65536.0 + 0.5), 65535.0) - 32768.0
    return whole, rest


def from_codes(whole, rest, steps):
    return (whole + (rest + 32768.0) * (1.0 / 65536.0)) * (1.0 / steps)


def coded_rows(blended):
    reach = jnp.maximum(jnp.max(jnp.abs(blended), axis=1, keepdims=True), 1e-30)
    factor = pltpu.reciprocal(reach, approx=True) * CODE_TOP
    return jnp.round(blended * factor).astype(jnp.int32).astype(jnp.int16), factor


def coded_stats(stats):
    flat = stats.T
    top, total, factor = (flat[k * KV_HEADS : (k + 1) * KV_HEADS, :] for k in range(3))
    codes = two_codes(top * SCALE + jnp.log(total), LOG_STEPS)
    codes += two_codes(-jnp.log2(factor * total), SCALE_STEPS)
    return jnp.concatenate(codes, axis=0).astype(jnp.int32).astype(jnp.int16)


def decoded_stats(codes):
    codes = codes.astype(jnp.int32).astype(jnp.float32)
    codes = [codes[..., k * KV_HEADS : (k + 1) * KV_HEADS, :] for k in range(4)]
    log_total = from_codes(codes[0], codes[1], LOG_STEPS)
    return jnp.concatenate([log_total, jnp.exp2(from_codes(codes[2], codes[3], SCALE_STEPS))], axis=-2)


def parent_kernel(
    cap, chunk, pages_ref, len_ref, recv_ref, store_ref, out_ref, spare_hbm, spare_ref, key_ref, value_ref, sem
):
    spare_ref[...] = jnp.zeros_like(spare_ref)
    spare_copy = pltpu.make_async_copy(spare_ref, spare_hbm, sem)
    spare_copy.start()
    parents, page_count = pages_ref.shape
    pages, lengths = pages_ref[...], len_ref[...]
    sources = recv_ref.shape[0]
    head_span = cap * HEAD_ROWS
    tokens = page_count * PAGE
    heads = range(KV_HEADS)
    for p in range(parents):
        for i in range(page_count):
            start = pl.multiple_of(pages[p, i] * PAGE, PAGE)
            page = store_ref[pl.ds(start, PAGE), :]
            for g in heads:
                span = (g, pl.ds(i * PAGE, PAGE), pl.ds(p * HEAD_DIM, HEAD_DIM))
                key_ref[span] = page[:, g * HEAD_DIM : (g + 1) * HEAD_DIM]
                value_ref[span] = page[:, KEY_WIDTH + g * HEAD_DIM : KEY_WIDTH + (g + 1) * HEAD_DIM]

    rows = chunk * head_span
    lanes = iota((rows, HEAD_DIM), 1)
    positions = iota((rows, tokens), 1)

    def body(c, carry):
        part = pl.ds(c * chunk, chunk)
        meta = recv_ref[part, pl.ds(KV_HEADS * head_span, 16), :].astype(jnp.float32)
        picks = [
            jnp.broadcast_to(meta[:, s : s + 1, :], (chunk, HEAD_ROWS, HEAD_DIM)) for s in range(cap)
        ]
        parent = jnp.concatenate(picks, axis=1).reshape(rows, HEAD_DIM)
        limit = jnp.full((rows, HEAD_DIM), lengths[0, 0], jnp.int32)
        for p in range(1, parents):
            limit = jnp.where(parent == p, lengths[0, p], limit)
        bias = jnp.where(positions < limit[:, :1], 0.0, MASKED)
        parent_low = parent.astype(jnp.bfloat16)

        def scores_of(g):
            query = recv_ref[part, pl.ds(g * head_span, head_span), :].reshape(rows, HEAD_DIM)
            query = jnp.concatenate(
                [jnp.where(parent_low == p, query, jnp.zeros_like(query)) for p in range(parents)], axis=1
            )
            return lax.dot_general(query, key_ref[g], NT, preferred_element_type=jnp.float32)

        def softmax_of(scores):
            scores = scores + bias
            top = jnp.max(scores, axis=1, keepdims=True)
            terms = jnp.exp2((scores - top) * (SCALE * LOG2_E))
            return terms.astype(jnp.bfloat16), top, jnp.sum(terms, axis=1, keepdims=True)

        def blended_of(g, weights):
            both = jnp.dot(weights, value_ref[g], preferred_element_type=jnp.float32)
            blended = both[:, :HEAD_DIM]
            for p in range(1, parents):
                blended = jnp.where(parent == p, both[:, p * HEAD_DIM : (p + 1) * HEAD_DIM], blended)
            return blended

        scores = [scores_of(g) for g in heads]
        softmaxes = [softmax_of(scores[g]) for g in heads]
        blends = [blended_of(g, softmaxes[g][0]) for g in heads]
        stats = jnp.zeros((rows, HEAD_DIM), jnp.float32)
        for g in heads:
            coded, factor = coded_rows(blends[g])
            out_ref[part, pl.ds(g * head_span, head_span), :] = coded.reshape(chunk, head_span, HEAD_DIM)
            for k, value in enumerate((softmaxes[g][1], softmaxes[g][2], factor)):
                stats = jnp.where(lanes == k * KV_HEADS + g, value, stats)
        flat = coded_stats(stats)
        for j in range(chunk):
            piece = flat[:, j * head_span : (j + 1) * head_span]
            if head_span < HEAD_DIM:
                piece = jnp.concatenate(
                    [piece, jnp.zeros((STAT_ROWS, HEAD_DIM - head_span), jnp.int16)], axis=1
                )
            out_ref[c * chunk + j, pl.ds(KV_HEADS * head_span, STAT_ROWS), :] = piece
        return carry

    lax.fori_loop(0, sources // chunk, body, 0, unroll=sources == chunk)
    spare_copy.wait()


def fill_suffix_bias(pages_ref, len_ref, bias_ref, last_of):
    page_count, count = pages_ref.shape
    pages, lengths = pages_ref[...], len_ref[...]
    row, lane = iota((PAGE, HEAD_DIM), 0), iota((PAGE, HEAD_DIM), 1)
    for r in range(count):
        for i in range(page_count):
            keep = (lane // 2 == r) & (row + i * PAGE <= last_of(lengths[0, r], lane % 2))
            start = pl.multiple_of(pages[i, r] * PAGE, PAGE)
            bias_ref[pl.ds(start, PAGE), :] = jnp.where(keep, 0.0, MASKED).astype(jnp.bfloat16)


def own_pick(count):
    rows = count * HEAD_ROWS
    row, lane = iota((rows, HEAD_DIM), 0), iota((rows, HEAD_DIM), 1)
    return jnp.where(lane == (row // HEAD_ROWS) * 2 + row % 2, 1.0, 0.0).astype(jnp.bfloat16)


def prefill_kernel(pages_ref, len_ref, query_ref, store_ref, out_ref, bias_ref):
    count = query_ref.shape[0]
    rows = count * HEAD_ROWS
    fill_suffix_bias(pages_ref, len_ref, bias_ref, lambda length, t: length - 2 + t)
    pick = own_pick(count)
    for g in range(KV_HEADS):
        query = query_ref[:, pl.ds(g * HEAD_ROWS, HEAD_ROWS), :].reshape(rows, HEAD_DIM)
        keys = store_ref[:, pl.ds(g * HEAD_DIM, HEAD_DIM)]
        values = store_ref[:, pl.ds(KEY_WIDTH + g * HEAD_DIM, HEAD_DIM)]
        scores = lax.dot_general(
            jnp.concatenate([query, pick], axis=1),
            jnp.concatenate([keys, bias_ref[...]], axis=1),
            NT,
            preferred_element_type=jnp.float32,
        ) * SCALE
        terms = jnp.exp(scores - jnp.max(scores, axis=1, keepdims=True))
        total = jnp.sum(terms, axis=1, keepdims=True)
        blended = jnp.dot(terms.astype(jnp.bfloat16), values, preferred_element_type=jnp.float32)
        out_ref[:, pl.ds(g * HEAD_ROWS, HEAD_ROWS), :] = (
            (blended / total).astype(jnp.bfloat16).reshape(count, HEAD_ROWS, HEAD_DIM)
        )


def local_kernel(cap, pages_ref, len_ref, query_ref, store_ref, step_ref, spare_ref, out_ref, bias_ref):
    count = query_ref.shape[0]
    rows = count * HEAD_ROWS
    head_span = cap * HEAD_ROWS
    blocks = count // cap
    fill_suffix_bias(pages_ref, len_ref, bias_ref, lambda length, t: length - 1)
    steps = 2 * count
    step_pad = -steps % HEAD_DIM
    key_row, lane = iota((steps + step_pad, HEAD_DIM), 0), iota((steps + step_pad, HEAD_DIM), 1)
    seen = (key_row // 2 == lane // 2) & (key_row % 2 <= lane % 2) & (key_row < steps)
    step_bias = jnp.where(seen, 0.0, MASKED).astype(jnp.bfloat16)
    pad = jnp.zeros((step_pad, HEAD_DIM), jnp.bfloat16)

    step_tiles = [step_ref[r] for r in range(count)]

    def step_rows(c):
        return jnp.concatenate([step[2 * c : 2 * c + 2, :] for step in step_tiles] + [pad], axis=0)

    pick = own_pick(count)
    lanes = iota((rows, HEAD_DIM), 1)
    stats = jnp.zeros((rows, HEAD_DIM), jnp.float32)
    for g in range(KV_HEADS):
        query = query_ref[:, pl.ds(g * HEAD_ROWS, HEAD_ROWS), :].reshape(rows, HEAD_DIM)
        query = jnp.concatenate([query, pick], axis=1)
        keys = jnp.concatenate([store_ref[:, pl.ds(g * HEAD_DIM, HEAD_DIM)], bias_ref[...]], axis=1)
        step_keys = jnp.concatenate([step_rows(g), step_bias], axis=1)
        values = store_ref[:, pl.ds(KEY_WIDTH + g * HEAD_DIM, HEAD_DIM)]
        step_values = step_rows(KV_HEADS + g)
        scores = lax.dot_general(query, keys, NT, preferred_element_type=jnp.float32)
        step_scores = lax.dot_general(query, step_keys, NT, preferred_element_type=jnp.float32)
        top = jnp.maximum(
            jnp.max(scores, axis=1, keepdims=True), jnp.max(step_scores, axis=1, keepdims=True)
        )
        terms = jnp.exp2((scores - top) * (SCALE * LOG2_E))
        step_terms = jnp.exp2((step_scores - top) * (SCALE * LOG2_E))
        total = jnp.sum(terms, axis=1, keepdims=True) + jnp.sum(step_terms, axis=1, keepdims=True)
        blended = jnp.dot(terms.astype(jnp.bfloat16), values, preferred_element_type=jnp.float32)
        blended = blended + jnp.dot(
            step_terms.astype(jnp.bfloat16), step_values, preferred_element_type=jnp.float32
        )
        coded, factor = coded_rows(blended)
        out_ref[:, pl.ds(g * head_span, head_span), :] = coded.reshape(blocks, head_span, HEAD_DIM)
        for k, value in enumerate((top, total, factor)):
            stats = jnp.where(lanes == k * KV_HEADS + g, value, stats)
    flat = coded_stats(stats)
    for j in range(rows // HEAD_DIM):
        out_ref[j, pl.ds(KV_HEADS * head_span, STAT_ROWS), :] = flat[:, j * HEAD_DIM : (j + 1) * HEAD_DIM]


def spread_rows(rows):
    high = rows.astype(jnp.bfloat16)
    rest = rows - high.astype(jnp.float32)
    middle = rest.astype(jnp.bfloat16)
    low = (rest - middle.astype(jnp.float32)).astype(jnp.bfloat16)
    count = rows.shape[0]
    shape = (3 * count, count * HEAD_DIM)
    chosen = iota(shape, 0) % count == iota(shape, 1) // HEAD_DIM
    return lax.dot_general(
        jnp.concatenate([high, middle, low], axis=0),
        jnp.where(chosen, 1.0, 0.0).astype(jnp.bfloat16),
        (((0,), (0,)), ((), ())),
        preferred_element_type=jnp.float32,
    )


def merge_kernel(cap, owner_ref, back_ref, own_ref, out_hbm, out_ref, decoded_ref, sems):
    count = out_ref.shape[0]
    step = count // sems.shape[0]

    def put(k):
        part = pl.ds(k * step, step)
        return pltpu.make_async_copy(out_ref.at[part], out_hbm.at[part], sems.at[k])

    rows = count * HEAD_ROWS
    head_span = cap * HEAD_ROWS
    stat_span = pl.ds(KV_HEADS * head_span, STAT_ROWS)
    decoded_ref[...] = decoded_stats(back_ref[:, stat_span, :])
    own = jnp.concatenate([decoded_stats(own_ref[j, stat_span, :]) for j in range(rows // HEAD_DIM)], axis=1)

    names, ranks = slot_ranks(owner_ref, cap, back_ref.shape[0])
    per_tile = HEAD_DIM // HEAD_ROWS
    place = iota((2 * KV_HEADS, HEAD_DIM), 1) // HEAD_ROWS
    tiles = []
    for first in range(0, count, per_tile):
        tile = jnp.zeros((2 * KV_HEADS, HEAD_DIM), jnp.float32)
        for r in range(first, min(first + per_tile, count)):
            shift = lax.rem((r - first) * HEAD_ROWS - ranks[r] * HEAD_ROWS + HEAD_DIM, HEAD_DIM)
            tile = jnp.where(place == r - first, pltpu.roll(decoded_ref[names[r]], shift, 1), tile)
        tiles.append(tile)
    flat = jnp.concatenate(tiles, axis=1)[:, :rows]
    part_top, own_top = flat[:KV_HEADS], own[:KV_HEADS]
    top = jnp.maximum(own_top, part_top)
    own_weight, part_weight = jnp.exp(own_top - top), jnp.exp(part_top - top)
    inverse = 1.0 / (own_weight + part_weight)
    weights = [own[KV_HEADS:] * own_weight * inverse, flat[KV_HEADS:] * part_weight * inverse]
    weights = spread_rows(jnp.concatenate(weights, axis=0))
    for r in range(count):
        span = slice(r * HEAD_ROWS, (r + 1) * HEAD_ROWS)
        for g in range(KV_HEADS):
            start = pl.multiple_of(g * head_span + ranks[r] * HEAD_ROWS, HEAD_ROWS)
            part = back_ref[names[r], pl.ds(start, HEAD_ROWS), :].astype(jnp.int32).astype(jnp.float32)
            own_start = g * head_span + r % cap * HEAD_ROWS
            own_part = own_ref[r // cap, pl.ds(own_start, HEAD_ROWS), :].astype(jnp.int32).astype(jnp.float32)
            merged = own_part * weights[span, g * HEAD_DIM : (g + 1) * HEAD_DIM]
            k = KV_HEADS + g
            merged = merged + part * weights[span, k * HEAD_DIM : (k + 1) * HEAD_DIM]
            out_ref[r, pl.ds(g * HEAD_ROWS, HEAD_ROWS), :] = merged.astype(jnp.bfloat16)
        if (r + 1) % step == 0:
            put(r // step).start()
    for k in range(count // step):
        put(k).wait()


def call(kernel, out_shape, arrays, scratch, cost=None, in_space=pltpu.VMEM, out_space=pltpu.VMEM, grant=VMEM_BYTES):
    take = pl.BlockSpec(memory_space=in_space)
    if not isinstance(out_space, tuple):
        out_space = jax.tree.map(lambda _: out_space, out_shape)
    return pl.pallas_call(
        kernel,
        out_shape=out_shape,
        in_specs=[take] * len(arrays),
        out_specs=jax.tree.map(lambda space: pl.BlockSpec(memory_space=space), out_space),
        cost_estimate=cost,
        scratch_shapes=scratch,
        compiler_params=pltpu.CompilerParams(vmem_limit_bytes=grant),
    )(*arrays)


def head_rows(tokens):
    count, pair, width = tokens.shape
    blocks = tokens.reshape(count, pair, width // HEAD_DIM, HEAD_DIM)
    return blocks.transpose(0, 2, 1, 3).reshape(count, -1, HEAD_DIM)


def local(
    kv_store, queries, step_kv, suffix_pages, suffix_len, owner, parent_id, parent_pages, parent_len
):
    decoding = lax.axis_index("role") == 1
    seq_count = lax.axis_size("seq")
    store = kv_store[0]
    count, pair, width = queries.shape[1:]
    cap = max(2, 2 * count // seq_count)
    head_span = cap * HEAD_ROWS
    chunk = max(1, min(seq_count, 512 // head_span))
    query_rows = head_rows(queries[0])
    owner_row, parent_row = owner.reshape(1, -1), parent_id.reshape(1, -1)
    parent_tables = (parent_pages, parent_len.reshape(1, -1))
    suffix_tables = (suffix_pages.T, suffix_len.reshape(1, -1))
    token_rows = store.shape[0]

    sent = jax.ShapeDtypeStruct((seq_count, KV_HEADS * head_span + 16, HEAD_DIM), jnp.bfloat16)
    answer = jax.ShapeDtypeStruct((seq_count, KV_HEADS * head_span + STAT_ROWS, HEAD_DIM), jnp.int16)
    own_part = jax.ShapeDtypeStruct((count // cap, *answer.shape[1:]), answer.dtype)
    result = jax.ShapeDtypeStruct(query_rows.shape, jnp.bfloat16)
    bias = pltpu.VMEM((token_rows, HEAD_DIM), jnp.bfloat16)
    rows = count * HEAD_ROWS
    part = (KV_HEADS, rows, HEAD_DIM)

    def exchange(block):
        return lax.all_to_all(block, "seq", split_axis=0, concat_axis=0, tiled=True)

    def tokens_of(rows):
        return rows.reshape(count, width // HEAD_DIM, pair, HEAD_DIM).transpose(0, 2, 1, 3).reshape(
            1, count, pair, width
        )

    def like(arrays):
        return tuple(jax.ShapeDtypeStruct(a.shape, a.dtype) for a in arrays)

    def zeros(shapes):
        return tuple(jnp.zeros(a.shape, a.dtype) for a in shapes)

    handed = (sent, *like((owner_row, *parent_tables)))

    def pack(query_rows):
        return call(
            functools.partial(pack_kernel, cap),
            handed,
            (query_rows, owner_row, parent_row, *parent_tables),
            [
                pltpu.VMEM(query_rows.shape, jnp.bfloat16),
                pltpu.VMEM(parent_row.shape, jnp.int32),
                pltpu.VMEM((seq_count, 16, HEAD_DIM), jnp.float32),
                pltpu.SemaphoreType.DMA((3 + len(parent_tables),)),
            ],
            in_space=pl.ANY,
        )

    packed, owner_row, *parent_tables = lax.cond(decoding, pack, lambda _: call(zero_kernel, handed, (), []), query_rows)
    query_after, packed = lax.optimization_barrier((query_rows, packed))
    decode_query = lax.ppermute(query_after, "role", [(0, 1), (1, 0)])

    def send(packed):
        return exchange(packed), *zeros(suffix_tables)

    def hand_on(packed):
        return jnp.zeros_like(packed), *call(hand_kernel, like(suffix_tables), suffix_tables, [])

    received, *suffix_tables = lax.cond(decoding, send, hand_on, packed)

    def answer_queries(received, decode_query):
        parents, page_count = parent_pages.shape
        beside = (KV_HEADS, page_count * PAGE, parents * HEAD_DIM)
        return call(
            functools.partial(parent_kernel, cap, chunk),
            (answer, own_part),
            (*parent_tables, received, store),
            [
                pltpu.VMEM(own_part.shape, jnp.int16),
                pltpu.VMEM(beside, jnp.bfloat16),
                pltpu.VMEM(beside, jnp.bfloat16),
                pltpu.SemaphoreType.DMA,
            ],
            out_space=(pltpu.VMEM, pl.ANY),
        )

    def attend_own(received, decode_query):
        return call(
            functools.partial(local_kernel, cap),
            (answer, own_part),
            (*suffix_tables, decode_query, store, head_rows(step_kv)),
            [bias],
        )

    parts, own = lax.cond(decoding, answer_queries, attend_own, received, decode_query)
    own = lax.ppermute(own, "role", [(0, 1), (1, 0)])
    back = lax.cond(decoding, exchange, lambda block: jnp.zeros_like(block), parts)

    def merge(back, own, query_rows):
        return tokens_of(
            call(
                functools.partial(merge_kernel, cap),
                result,
                (owner_row, back, own),
                [
                    pltpu.VMEM(result.shape, jnp.bfloat16),
                    pltpu.VMEM((seq_count, 2 * KV_HEADS, HEAD_DIM), jnp.float32),
                    pltpu.SemaphoreType.DMA((4 if count % 4 == 0 else 1,)),
                ],
                out_space=pl.ANY,
            )
        )

    def prefill(back, own, query_rows):
        return tokens_of(call(prefill_kernel, result, (*suffix_tables, query_rows, store), [bias], grant=PREFILL_VMEM_BYTES))

    return lax.cond(decoding, merge, prefill, back, own, query_rows)


def solution(mesh):
    in_specs = (
        P("role", ("groups", "seq"), None),
        P("role", ("groups", "seq"), None, None),
        P(("groups", "seq"), None, None),
        P(("groups", "seq"), None),
        P(("groups", "seq")),
        P(("groups", "seq"), None),
        P(("groups", "seq")),
        P(("groups", "seq"), None),
        P(("groups", "seq")),
    )
    out_specs = P("role", ("groups", "seq"), None, None)
    return jax.shard_map(local, mesh=mesh, in_specs=in_specs, out_specs=out_specs, check_vma=False)
```

```python
import functools

import jax
import jax.numpy as jnp
from jax import lax
from jax.experimental import pallas as pl
from jax.experimental.pallas import tpu as pltpu
from jax.sharding import PartitionSpec as P

HEAD_DIM = 128
KV_HEADS = 4
GROUP = 8
PAGE = 16
HEAD_ROWS = 2 * GROUP
KEY_WIDTH = KV_HEADS * HEAD_DIM
SCALE = HEAD_DIM ** (-0.5)
MASKED = -1e30
STAT_ROWS = 4 * KV_HEADS
LOG_STEPS = 4.0
SCALE_STEPS = 128.0
CODE_TOP = 32600.0
LOG2_E = 1.4426950408889634
VMEM_BYTES = 48 * 1024 * 1024
PREFILL_VMEM_BYTES = (64 * 1024 - 1150) * 1024

NT = (((1,), (1,)), ((), ()))


def iota(shape, dim):
    return lax.broadcasted_iota(jnp.int32, shape, dim)


def slot_ranks(owner_ref, cap, owners):
    owner = owner_ref[...]
    bits = cap.bit_length()
    per_word = 30 // bits
    words = [jnp.int32(0)] * -(-owners // per_word)
    names, ranks = [], []
    for r in range(owner.shape[1]):
        name = owner[0, r]
        word, rank = name // per_word if len(words) > 1 else 0, jnp.int32(0)
        shift = (name - word * per_word) * bits
        for k, counts in enumerate(words):
            here = (word == k) if len(words) > 1 else True
            count = (counts >> shift) & ((1 << bits) - 1)
            step = jnp.int32(1) << shift
            if len(words) > 1:
                count, step = jnp.where(here, count, 0), jnp.where(here, step, 0)
            rank = rank + count
            words[k] = counts + step
        names.append(name)
        ranks.append(rank)
    return names, ranks


def pack_kernel(cap, query_hbm, owner_hbm, parent_hbm, *refs):
    *refs, query_ref, parent_ref, meta_ref, sems = refs
    tables, (out_ref, owner_ref, *copies) = refs[: len(refs) // 2 - 1], refs[len(refs) // 2 - 1 :]
    moves = [(owner_hbm, owner_ref), (parent_hbm, parent_ref), (query_hbm, query_ref), *zip(tables, copies)]
    moves = [pltpu.make_async_copy(src, dst, sems.at[k]) for k, (src, dst) in enumerate(moves)]
    for move in moves:
        move.start()
    count = query_ref.shape[0]
    head_span = cap * HEAD_ROWS
    out_ref[...] = jnp.zeros_like(out_ref)
    meta_ref[...] = jnp.zeros_like(meta_ref)
    moves[0].wait()
    moves[1].wait()
    parent = parent_ref[...]
    names, ranks = slot_ranks(owner_ref, cap, out_ref.shape[0])
    for r in range(count):
        meta_ref[names[r], pl.ds(ranks[r], 1), :] = jnp.full((1, HEAD_DIM), parent[0, r].astype(jnp.float32))
    out_ref[:, pl.ds(KV_HEADS * head_span, 16), :] = meta_ref[...].astype(jnp.bfloat16)
    moves[2].wait()
    for r in range(count):
        d, rank = names[r], ranks[r]
        for g in range(KV_HEADS):
            start = pl.multiple_of(g * head_span + rank * HEAD_ROWS, HEAD_ROWS)
            out_ref[d, pl.ds(start, HEAD_ROWS), :] = query_ref[r, pl.ds(g * HEAD_ROWS, HEAD_ROWS), :]
    for move in moves[3:]:
        move.wait()


def zero_kernel(*refs):
    for ref in refs:
        ref[...] = jnp.zeros_like(ref)


def hand_kernel(*refs):
    half = len(refs) // 2
    for table, copy in zip(refs[:half], refs[half:]):
        copy[...] = table[...]


def two_codes(values, steps):
    scaled = values * steps
    whole = jnp.floor(scaled)
    rest = jnp.minimum(jnp.floor((scaled - whole) * 65536.0 + 0.5), 65535.0) - 32768.0
    return whole, rest


def from_codes(whole, rest, steps):
    return (whole + (rest + 32768.0) * (1.0 / 65536.0)) * (1.0 / steps)


def coded_rows(blended):
    reach = jnp.maximum(jnp.max(jnp.abs(blended), axis=1, keepdims=True), 1e-30)
    factor = pltpu.reciprocal(reach, approx=True) * CODE_TOP
    return jnp.round(blended * factor).astype(jnp.int32).astype(jnp.int16), factor


def coded_stats(stats):
    flat = stats.T
    top, total, factor = (flat[k * KV_HEADS : (k + 1) * KV_HEADS, :] for k in range(3))
    codes = two_codes(top * SCALE + jnp.log(total), LOG_STEPS)
    codes += two_codes(-jnp.log2(factor * total), SCALE_STEPS)
    return jnp.concatenate(codes, axis=0).astype(jnp.int32).astype(jnp.int16)


def decoded_stats(codes):
    codes = codes.astype(jnp.int32).astype(jnp.float32)
    codes = [codes[..., k * KV_HEADS : (k + 1) * KV_HEADS, :] for k in range(4)]
    log_total = from_codes(codes[0], codes[1], LOG_STEPS)
    return jnp.concatenate([log_total, jnp.exp2(from_codes(codes[2], codes[3], SCALE_STEPS))], axis=-2)


def parent_kernel(
    cap, chunk, pages_ref, len_ref, recv_ref, store_ref, out_ref, spare_hbm, spare_ref, key_ref, value_ref, sem
):
    spare_ref[...] = jnp.zeros_like(spare_ref)
    spare_copy = pltpu.make_async_copy(spare_ref, spare_hbm, sem)
    spare_copy.start()
    parents, page_count = pages_ref.shape
    pages, lengths = pages_ref[...], len_ref[...]
    sources = recv_ref.shape[0]
    head_span = cap * HEAD_ROWS
    tokens = page_count * PAGE
    heads = range(KV_HEADS)
    starts = [[pl.multiple_of(pages[p, i] * PAGE, PAGE) for i in range(page_count)] for p in range(parents)]

    def arrange(target_ref, g, column):
        for p in range(parents):
            for i in range(page_count):
                span = (g, pl.ds(i * PAGE, PAGE), pl.ds(p * HEAD_DIM, HEAD_DIM))
                target_ref[span] = store_ref[pl.ds(starts[p][i], PAGE), pl.ds(column, HEAD_DIM)]

    def arrange_keys(g):
        arrange(key_ref, g, g * HEAD_DIM)

    def arrange_values(g):
        arrange(value_ref, g, KEY_WIDTH + g * HEAD_DIM)

    at_once = sources == chunk
    if not at_once:
        for g in heads:
            arrange_keys(g)
            arrange_values(g)

    rows = chunk * head_span
    lanes = iota((rows, HEAD_DIM), 1)
    positions = iota((rows, tokens), 1)

    def body(c, carry):
        part = pl.ds(c * chunk, chunk)
        meta = recv_ref[part, pl.ds(KV_HEADS * head_span, 16), :].astype(jnp.float32)
        picks = [
            jnp.broadcast_to(meta[:, s : s + 1, :], (chunk, HEAD_ROWS, HEAD_DIM)) for s in range(cap)
        ]
        parent = jnp.concatenate(picks, axis=1).reshape(rows, HEAD_DIM)
        limit = jnp.full((rows, HEAD_DIM), lengths[0, 0], jnp.int32)
        for p in range(1, parents):
            limit = jnp.where(parent == p, lengths[0, p], limit)
        bias = jnp.where(positions < limit[:, :1], 0.0, MASKED)
        parent_low = parent.astype(jnp.bfloat16)

        def scores_of(g):
            if at_once:
                arrange_keys(g)
            query = recv_ref[part, pl.ds(g * head_span, head_span), :].reshape(rows, HEAD_DIM)
            query = jnp.concatenate(
                [jnp.where(parent_low == p, query, jnp.zeros_like(query)) for p in range(parents)], axis=1
            )
            return lax.dot_general(query, key_ref[g], NT, preferred_element_type=jnp.float32)

        def softmax_of(scores):
            scores = scores + bias
            top = jnp.max(scores, axis=1, keepdims=True)
            terms = jnp.exp2((scores - top) * (SCALE * LOG2_E))
            return terms.astype(jnp.bfloat16), top, jnp.sum(terms, axis=1, keepdims=True)

        def blended_of(g, weights):
            if at_once:
                arrange_values(g)
            both = jnp.dot(weights, value_ref[g], preferred_element_type=jnp.float32)
            blended = both[:, :HEAD_DIM]
            for p in range(1, parents):
                blended = jnp.where(parent == p, both[:, p * HEAD_DIM : (p + 1) * HEAD_DIM], blended)
            return blended

        scores, softmaxes, blends = {}, {}, {}
        for g in range(KV_HEADS + 2):
            if g < KV_HEADS:
                scores[g] = scores_of(g)
            if 0 <= g - 1 < KV_HEADS:
                softmaxes[g - 1] = softmax_of(scores[g - 1])
            if 0 <= g - 2 < KV_HEADS:
                blends[g - 2] = blended_of(g - 2, softmaxes[g - 2][0])
        stats = jnp.zeros((rows, HEAD_DIM), jnp.float32)
        for g in heads:
            coded, factor = coded_rows(blends[g])
            out_ref[part, pl.ds(g * head_span, head_span), :] = coded.reshape(chunk, head_span, HEAD_DIM)
            for k, value in enumerate((softmaxes[g][1], softmaxes[g][2], factor)):
                stats = jnp.where(lanes == k * KV_HEADS + g, value, stats)
        flat = coded_stats(stats)
        for j in range(chunk):
            first = j * head_span // HEAD_DIM * HEAD_DIM
            piece = flat[:, first : first + HEAD_DIM]
            out_ref[c * chunk + j, pl.ds(KV_HEADS * head_span, STAT_ROWS), :] = piece
        return carry

    lax.fori_loop(0, sources // chunk, body, 0, unroll=sources == chunk)
    spare_copy.wait()


def fill_suffix_bias(pages_ref, len_ref, bias_ref, last_of):
    page_count, count = pages_ref.shape
    pages, lengths = pages_ref[...], len_ref[...]
    row, lane = iota((PAGE, HEAD_DIM), 0), iota((PAGE, HEAD_DIM), 1)
    for r in range(count):
        for i in range(page_count):
            keep = (lane // 2 == r) & (row + i * PAGE <= last_of(lengths[0, r], lane % 2))
            start = pl.multiple_of(pages[i, r] * PAGE, PAGE)
            bias_ref[pl.ds(start, PAGE), :] = jnp.where(keep, 0.0, MASKED).astype(jnp.bfloat16)


def own_pick(count):
    rows = count * HEAD_ROWS
    row, lane = iota((rows, HEAD_DIM), 0), iota((rows, HEAD_DIM), 1)
    return jnp.where(lane == (row // HEAD_ROWS) * 2 + row % 2, 1.0, 0.0).astype(jnp.bfloat16)


def prefill_kernel(pages_ref, len_ref, query_ref, store_ref, out_ref, bias_ref):
    count = query_ref.shape[0]
    rows = count * HEAD_ROWS
    fill_suffix_bias(pages_ref, len_ref, bias_ref, lambda length, t: length - 2 + t)
    pick = own_pick(count)
    for g in range(KV_HEADS):
        query = query_ref[:, pl.ds(g * HEAD_ROWS, HEAD_ROWS), :].reshape(rows, HEAD_DIM)
        keys = store_ref[:, pl.ds(g * HEAD_DIM, HEAD_DIM)]
        values = store_ref[:, pl.ds(KEY_WIDTH + g * HEAD_DIM, HEAD_DIM)]
        scores = lax.dot_general(
            jnp.concatenate([query, pick], axis=1),
            jnp.concatenate([keys, bias_ref[...]], axis=1),
            NT,
            preferred_element_type=jnp.float32,
        ) * SCALE
        terms = jnp.exp(scores - jnp.max(scores, axis=1, keepdims=True))
        total = jnp.sum(terms, axis=1, keepdims=True)
        blended = jnp.dot(terms.astype(jnp.bfloat16), values, preferred_element_type=jnp.float32)
        out_ref[:, pl.ds(g * HEAD_ROWS, HEAD_ROWS), :] = (
            (blended / total).astype(jnp.bfloat16).reshape(count, HEAD_ROWS, HEAD_DIM)
        )


def local_kernel(cap, pages_ref, len_ref, query_ref, store_ref, step_ref, spare_ref, out_ref, bias_ref):
    count = query_ref.shape[0]
    rows = count * HEAD_ROWS
    head_span = cap * HEAD_ROWS
    blocks = count // cap
    fill_suffix_bias(pages_ref, len_ref, bias_ref, lambda length, t: length - 1)
    steps = 2 * count
    step_pad = -steps % HEAD_DIM
    key_row, lane = iota((steps + step_pad, HEAD_DIM), 0), iota((steps + step_pad, HEAD_DIM), 1)
    seen = (key_row // 2 == lane // 2) & (key_row % 2 <= lane % 2) & (key_row < steps)
    step_bias = jnp.where(seen, 0.0, MASKED).astype(jnp.bfloat16)
    pad = jnp.zeros((step_pad, HEAD_DIM), jnp.bfloat16)

    step_tiles = [step_ref[r] for r in range(count)]

    def step_rows(c):
        return jnp.concatenate([step[2 * c : 2 * c + 2, :] for step in step_tiles] + [pad], axis=0)

    pick = own_pick(count)
    lanes = iota((rows, HEAD_DIM), 1)
    stats = jnp.zeros((rows, HEAD_DIM), jnp.float32)
    for g in range(KV_HEADS):
        query = query_ref[:, pl.ds(g * HEAD_ROWS, HEAD_ROWS), :].reshape(rows, HEAD_DIM)
        query = jnp.concatenate([query, pick], axis=1)
        keys = jnp.concatenate([store_ref[:, pl.ds(g * HEAD_DIM, HEAD_DIM)], bias_ref[...]], axis=1)
        step_keys = jnp.concatenate([step_rows(g), step_bias], axis=1)
        values = store_ref[:, pl.ds(KEY_WIDTH + g * HEAD_DIM, HEAD_DIM)]
        step_values = step_rows(KV_HEADS + g)
        scores = lax.dot_general(query, keys, NT, preferred_element_type=jnp.float32)
        step_scores = lax.dot_general(query, step_keys, NT, preferred_element_type=jnp.float32)
        top = jnp.maximum(
            jnp.max(scores, axis=1, keepdims=True), jnp.max(step_scores, axis=1, keepdims=True)
        )
        terms = jnp.exp2((scores - top) * (SCALE * LOG2_E))
        step_terms = jnp.exp2((step_scores - top) * (SCALE * LOG2_E))
        total = jnp.sum(terms, axis=1, keepdims=True) + jnp.sum(step_terms, axis=1, keepdims=True)
        blended = jnp.dot(terms.astype(jnp.bfloat16), values, preferred_element_type=jnp.float32)
        blended = blended + jnp.dot(
            step_terms.astype(jnp.bfloat16), step_values, preferred_element_type=jnp.float32
        )
        coded, factor = coded_rows(blended)
        out_ref[:, pl.ds(g * head_span, head_span), :] = coded.reshape(blocks, head_span, HEAD_DIM)
        for k, value in enumerate((top, total, factor)):
            stats = jnp.where(lanes == k * KV_HEADS + g, value, stats)
    flat = coded_stats(stats)
    for j in range(rows // HEAD_DIM):
        out_ref[j, pl.ds(KV_HEADS * head_span, STAT_ROWS), :] = flat[:, j * HEAD_DIM : (j + 1) * HEAD_DIM]


def spread_rows(rows):
    high = rows.astype(jnp.bfloat16)
    rest = rows - high.astype(jnp.float32)
    middle = rest.astype(jnp.bfloat16)
    low = (rest - middle.astype(jnp.float32)).astype(jnp.bfloat16)
    count = rows.shape[0]
    shape = (3 * count, count * HEAD_DIM)
    chosen = iota(shape, 0) % count == iota(shape, 1) // HEAD_DIM
    return lax.dot_general(
        jnp.concatenate([high, middle, low], axis=0),
        jnp.where(chosen, 1.0, 0.0).astype(jnp.bfloat16),
        (((0,), (0,)), ((), ())),
        preferred_element_type=jnp.float32,
    )


def merge_kernel(cap, owner_ref, back_ref, own_ref, out_hbm, out_ref, decoded_ref, sems):
    count = out_ref.shape[0]
    step = count // sems.shape[0]

    def put(k):
        part = pl.ds(k * step, step)
        return pltpu.make_async_copy(out_ref.at[part], out_hbm.at[part], sems.at[k])

    rows = count * HEAD_ROWS
    head_span = cap * HEAD_ROWS
    stat_span = pl.ds(KV_HEADS * head_span, STAT_ROWS)
    decoded_ref[...] = decoded_stats(back_ref[:, stat_span, :])
    own = jnp.concatenate([decoded_stats(own_ref[j, stat_span, :]) for j in range(rows // HEAD_DIM)], axis=1)

    names, ranks = slot_ranks(owner_ref, cap, back_ref.shape[0])
    here = lax.rem(lax.axis_index("seq") * head_span, HEAD_DIM)
    per_tile = HEAD_DIM // HEAD_ROWS
    place = iota((2 * KV_HEADS, HEAD_DIM), 1) // HEAD_ROWS
    tiles = []
    for first in range(0, count, per_tile):
        tile = jnp.zeros((2 * KV_HEADS, HEAD_DIM), jnp.float32)
        for r in range(first, min(first + per_tile, count)):
            shift = lax.rem((r - first) * HEAD_ROWS - ranks[r] * HEAD_ROWS - here + 2 * HEAD_DIM, HEAD_DIM)
            tile = jnp.where(place == r - first, pltpu.roll(decoded_ref[names[r]], shift, 1), tile)
        tiles.append(tile)
    flat = jnp.concatenate(tiles, axis=1)[:, :rows]
    part_top, own_top = flat[:KV_HEADS], own[:KV_HEADS]
    top = jnp.maximum(own_top, part_top)
    own_weight, part_weight = jnp.exp(own_top - top), jnp.exp(part_top - top)
    inverse = 1.0 / (own_weight + part_weight)
    weights = [own[KV_HEADS:] * own_weight * inverse, flat[KV_HEADS:] * part_weight * inverse]
    weights = spread_rows(jnp.concatenate(weights, axis=0))
    for r in range(count):
        span = slice(r * HEAD_ROWS, (r + 1) * HEAD_ROWS)
        for g in range(KV_HEADS):
            start = pl.multiple_of(g * head_span + ranks[r] * HEAD_ROWS, HEAD_ROWS)
            part = back_ref[names[r], pl.ds(start, HEAD_ROWS), :].astype(jnp.int32).astype(jnp.float32)
            own_start = g * head_span + r % cap * HEAD_ROWS
            own_part = own_ref[r // cap, pl.ds(own_start, HEAD_ROWS), :].astype(jnp.int32).astype(jnp.float32)
            merged = own_part * weights[span, g * HEAD_DIM : (g + 1) * HEAD_DIM]
            k = KV_HEADS + g
            merged = merged + part * weights[span, k * HEAD_DIM : (k + 1) * HEAD_DIM]
            out_ref[r, pl.ds(g * HEAD_ROWS, HEAD_ROWS), :] = merged.astype(jnp.bfloat16)
        if (r + 1) % step == 0:
            put(r // step).start()
    for k in range(count // step):
        put(k).wait()


def call(kernel, out_shape, arrays, scratch, cost=None, in_space=pltpu.VMEM, out_space=pltpu.VMEM, grant=VMEM_BYTES):
    take = pl.BlockSpec(memory_space=in_space)
    if not isinstance(out_space, tuple):
        out_space = jax.tree.map(lambda _: out_space, out_shape)
    return pl.pallas_call(
        kernel,
        out_shape=out_shape,
        in_specs=[take] * len(arrays),
        out_specs=jax.tree.map(lambda space: pl.BlockSpec(memory_space=space), out_space),
        cost_estimate=cost,
        scratch_shapes=scratch,
        compiler_params=pltpu.CompilerParams(vmem_limit_bytes=grant),
    )(*arrays)


def head_rows(tokens):
    count, pair, width = tokens.shape
    blocks = tokens.reshape(count, pair, width // HEAD_DIM, HEAD_DIM)
    return blocks.transpose(0, 2, 1, 3).reshape(count, -1, HEAD_DIM)


def local(
    kv_store, queries, step_kv, suffix_pages, suffix_len, owner, parent_id, parent_pages, parent_len
):
    decoding = lax.axis_index("role") == 1
    seq_count = lax.axis_size("seq")
    store = kv_store[0]
    count, pair, width = queries.shape[1:]
    cap = max(2, 2 * count // seq_count)
    head_span = cap * HEAD_ROWS
    chunk = max(1, min(seq_count, 512 // head_span))
    query_rows = head_rows(queries[0])
    owner_row, parent_row = owner.reshape(1, -1), parent_id.reshape(1, -1)
    parent_tables = (parent_pages, parent_len.reshape(1, -1))
    suffix_tables = (suffix_pages.T, suffix_len.reshape(1, -1))
    token_rows = store.shape[0]

    sent = jax.ShapeDtypeStruct((seq_count, KV_HEADS * head_span + 16, HEAD_DIM), jnp.bfloat16)
    answer = jax.ShapeDtypeStruct((seq_count, KV_HEADS * head_span + STAT_ROWS, HEAD_DIM), jnp.int16)
    own_part = jax.ShapeDtypeStruct((count // cap, *answer.shape[1:]), answer.dtype)
    result = jax.ShapeDtypeStruct(query_rows.shape, jnp.bfloat16)
    bias = pltpu.VMEM((token_rows, HEAD_DIM), jnp.bfloat16)
    rows = count * HEAD_ROWS
    part = (KV_HEADS, rows, HEAD_DIM)

    def exchange(block):
        return lax.all_to_all(block, "seq", split_axis=0, concat_axis=0, tiled=True)

    def tokens_of(rows):
        return rows.reshape(count, width // HEAD_DIM, pair, HEAD_DIM).transpose(0, 2, 1, 3).reshape(
            1, count, pair, width
        )

    def like(arrays):
        return tuple(jax.ShapeDtypeStruct(a.shape, a.dtype) for a in arrays)

    def zeros(shapes):
        return tuple(jnp.zeros(a.shape, a.dtype) for a in shapes)

    handed = (sent, *like((owner_row, *parent_tables)))

    def pack(query_rows):
        return call(
            functools.partial(pack_kernel, cap),
            handed,
            (query_rows, owner_row, parent_row, *parent_tables),
            [
                pltpu.VMEM(query_rows.shape, jnp.bfloat16),
                pltpu.VMEM(parent_row.shape, jnp.int32),
                pltpu.VMEM((seq_count, 16, HEAD_DIM), jnp.float32),
                pltpu.SemaphoreType.DMA((3 + len(parent_tables),)),
            ],
            in_space=pl.ANY,
        )

    packed, owner_row, *parent_tables = lax.cond(decoding, pack, lambda _: call(zero_kernel, handed, (), []), query_rows)
    query_after, packed = lax.optimization_barrier((query_rows, packed))
    decode_query = lax.ppermute(query_after, "role", [(0, 1), (1, 0)])

    def send(packed):
        return exchange(packed), *zeros(suffix_tables)

    def hand_on(packed):
        return jnp.zeros_like(packed), *call(hand_kernel, like(suffix_tables), suffix_tables, [])

    received, *suffix_tables = lax.cond(decoding, send, hand_on, packed)

    def answer_queries(received, decode_query):
        parents, page_count = parent_pages.shape
        beside = (KV_HEADS, page_count * PAGE, parents * HEAD_DIM)
        return call(
            functools.partial(parent_kernel, cap, chunk),
            (answer, own_part),
            (*parent_tables, received, store),
            [
                pltpu.VMEM(own_part.shape, jnp.int16),
                pltpu.VMEM(beside, jnp.bfloat16),
                pltpu.VMEM(beside, jnp.bfloat16),
                pltpu.SemaphoreType.DMA,
            ],
            out_space=(pltpu.VMEM, pl.ANY),
        )

    def attend_own(received, decode_query):
        return call(
            functools.partial(local_kernel, cap),
            (answer, own_part),
            (*suffix_tables, decode_query, store, head_rows(step_kv)),
            [bias],
        )

    parts, own = lax.cond(decoding, answer_queries, attend_own, received, decode_query)
    own = lax.ppermute(own, "role", [(0, 1), (1, 0)])
    back = lax.cond(decoding, exchange, lambda block: jnp.zeros_like(block), parts)

    def merge(back, own, query_rows):
        return tokens_of(
            call(
                functools.partial(merge_kernel, cap),
                result,
                (owner_row, back, own),
                [
                    pltpu.VMEM(result.shape, jnp.bfloat16),
                    pltpu.VMEM((seq_count, 2 * KV_HEADS, HEAD_DIM), jnp.float32),
                    pltpu.SemaphoreType.DMA((4 if count % 4 == 0 else 1,)),
                ],
                out_space=pl.ANY,
            )
        )

    def prefill(back, own, query_rows):
        return tokens_of(call(prefill_kernel, result, (*suffix_tables, query_rows, store), [bias], grant=PREFILL_VMEM_BYTES))

    return lax.cond(decoding, merge, prefill, back, own, query_rows)


def solution(mesh):
    in_specs = (
        P("role", ("groups", "seq"), None),
        P("role", ("groups", "seq"), None, None),
        P(("groups", "seq"), None, None),
        P(("groups", "seq"), None),
        P(("groups", "seq")),
        P(("groups", "seq"), None),
        P(("groups", "seq")),
        P(("groups", "seq"), None),
        P(("groups", "seq")),
    )
    out_specs = P("role", ("groups", "seq"), None, None)
    return jax.shard_map(local, mesh=mesh, in_specs=in_specs, out_specs=out_specs, check_vma=False)
```

```python
import functools

import jax
import jax.numpy as jnp
from jax import lax
from jax.experimental import pallas as pl
from jax.experimental.pallas import tpu as pltpu
from jax.sharding import PartitionSpec as P

HEAD_DIM = 128
KV_HEADS = 4
GROUP = 8
PAGE = 16
HEAD_ROWS = 2 * GROUP
KEY_WIDTH = KV_HEADS * HEAD_DIM
SCALE = HEAD_DIM ** (-0.5)
MASKED = -1e30
STAT_ROWS = 4 * KV_HEADS
LOG_STEPS = 4.0
SCALE_STEPS = 128.0
CODE_TOP = 32600.0
LOG2_E = 1.4426950408889634
VMEM_BYTES = 48 * 1024 * 1024
PREFILL_VMEM_BYTES = (64 * 1024 - 1150) * 1024

NT = (((1,), (1,)), ((), ()))


def iota(shape, dim):
    return lax.broadcasted_iota(jnp.int32, shape, dim)


def slot_ranks(owner_ref, cap, owners):
    owner = owner_ref[...]
    bits = cap.bit_length()
    per_word = 30 // bits
    words = [jnp.int32(0)] * -(-owners // per_word)
    names, ranks = [], []
    for r in range(owner.shape[1]):
        name = owner[0, r]
        word, rank = name // per_word if len(words) > 1 else 0, jnp.int32(0)
        shift = (name - word * per_word) * bits
        for k, counts in enumerate(words):
            here = (word == k) if len(words) > 1 else True
            count = (counts >> shift) & ((1 << bits) - 1)
            step = jnp.int32(1) << shift
            if len(words) > 1:
                count, step = jnp.where(here, count, 0), jnp.where(here, step, 0)
            rank = rank + count
            words[k] = counts + step
        names.append(name)
        ranks.append(rank)
    return names, ranks


def pack_kernel(cap, query_hbm, owner_hbm, parent_hbm, *refs):
    *refs, query_ref, parent_ref, meta_ref, sems = refs
    half = (len(refs) - 3) // 2
    tables, (out_ref, owner_ref, rank_ref, *copies) = refs[:half], refs[half:]
    moves = [(owner_hbm, owner_ref), (parent_hbm, parent_ref), (query_hbm, query_ref), *zip(tables, copies)]
    moves = [pltpu.make_async_copy(src, dst, sems.at[k]) for k, (src, dst) in enumerate(moves)]
    for move in moves:
        move.start()
    count = query_ref.shape[0]
    head_span = cap * HEAD_ROWS
    out_ref[...] = jnp.zeros_like(out_ref)
    meta_ref[...] = jnp.zeros_like(meta_ref)
    moves[0].wait()
    moves[1].wait()
    parent = parent_ref[...]
    names, ranks = slot_ranks(owner_ref, cap, out_ref.shape[0])
    table = jnp.zeros(rank_ref.shape, jnp.int32)
    for r in range(count):
        table = jnp.where(iota(rank_ref.shape, 1) == r, ranks[r], table)
    rank_ref[...] = table
    for r in range(count):
        meta_ref[names[r], pl.ds(ranks[r], 1), :] = jnp.full((1, HEAD_DIM), parent[0, r].astype(jnp.float32))
    out_ref[:, pl.ds(KV_HEADS * head_span, 16), :] = meta_ref[...].astype(jnp.bfloat16)
    moves[2].wait()
    for r in range(count):
        d, rank = names[r], ranks[r]
        for g in range(KV_HEADS):
            start = pl.multiple_of(g * head_span + rank * HEAD_ROWS, HEAD_ROWS)
            out_ref[d, pl.ds(start, HEAD_ROWS), :] = query_ref[r, pl.ds(g * HEAD_ROWS, HEAD_ROWS), :]
    for move in moves[3:]:
        move.wait()


def zero_kernel(*refs):
    for ref in refs:
        ref[...] = jnp.zeros_like(ref)


def hand_kernel(*refs):
    half = len(refs) // 2
    for table, copy in zip(refs[:half], refs[half:]):
        copy[...] = table[...]


def two_codes(values, steps):
    scaled = values * steps
    whole = jnp.floor(scaled)
    rest = jnp.minimum(jnp.floor((scaled - whole) * 65536.0 + 0.5), 65535.0) - 32768.0
    return whole, rest


def from_codes(whole, rest, steps):
    return (whole + (rest + 32768.0) * (1.0 / 65536.0)) * (1.0 / steps)


def coded_rows(blended):
    reach = jnp.maximum(jnp.max(jnp.abs(blended), axis=1, keepdims=True), 1e-30)
    factor = pltpu.reciprocal(reach, approx=True) * CODE_TOP
    return jnp.round(blended * factor).astype(jnp.int32).astype(jnp.int16), factor


def coded_stats(stats):
    flat = stats.T
    top, total, factor = (flat[k * KV_HEADS : (k + 1) * KV_HEADS, :] for k in range(3))
    codes = two_codes(top * SCALE + jnp.log(total), LOG_STEPS)
    codes += two_codes(-jnp.log2(factor * total), SCALE_STEPS)
    return jnp.concatenate(codes, axis=0).astype(jnp.int32).astype(jnp.int16)


def decoded_stats(codes):
    codes = codes.astype(jnp.int32).astype(jnp.float32)
    codes = [codes[..., k * KV_HEADS : (k + 1) * KV_HEADS, :] for k in range(4)]
    log_total = from_codes(codes[0], codes[1], LOG_STEPS)
    return jnp.concatenate([log_total, jnp.exp2(from_codes(codes[2], codes[3], SCALE_STEPS))], axis=-2)


def parent_kernel(
    cap, chunk, pages_ref, len_ref, recv_ref, store_ref, out_ref, spare_hbm, spare_ref, key_ref, value_ref, sem
):
    spare_ref[...] = jnp.zeros_like(spare_ref)
    spare_copy = pltpu.make_async_copy(spare_ref, spare_hbm, sem)
    spare_copy.start()
    parents, page_count = pages_ref.shape
    pages, lengths = pages_ref[...], len_ref[...]
    sources = recv_ref.shape[0]
    head_span = cap * HEAD_ROWS
    tokens = page_count * PAGE
    heads = range(KV_HEADS)
    starts = [[pl.multiple_of(pages[p, i] * PAGE, PAGE) for i in range(page_count)] for p in range(parents)]

    def arrange(target_ref, g, column):
        for p in range(parents):
            for i in range(page_count):
                span = (g, pl.ds(i * PAGE, PAGE), pl.ds(p * HEAD_DIM, HEAD_DIM))
                target_ref[span] = store_ref[pl.ds(starts[p][i], PAGE), pl.ds(column, HEAD_DIM)]

    def arrange_keys(g):
        arrange(key_ref, g, g * HEAD_DIM)

    def arrange_values(g):
        arrange(value_ref, g, KEY_WIDTH + g * HEAD_DIM)

    at_once = sources == chunk
    if not at_once:
        for g in heads:
            arrange_keys(g)
            arrange_values(g)

    rows = chunk * head_span
    lanes = iota((rows, HEAD_DIM), 1)
    positions = iota((rows, tokens), 1)

    def body(c, carry):
        part = pl.ds(c * chunk, chunk)
        meta = recv_ref[part, pl.ds(KV_HEADS * head_span, 16), :].astype(jnp.float32)
        picks = [
            jnp.broadcast_to(meta[:, s : s + 1, :], (chunk, HEAD_ROWS, HEAD_DIM)) for s in range(cap)
        ]
        parent = jnp.concatenate(picks, axis=1).reshape(rows, HEAD_DIM)
        limit = jnp.full((rows, HEAD_DIM), lengths[0, 0], jnp.int32)
        for p in range(1, parents):
            limit = jnp.where(parent == p, lengths[0, p], limit)
        bias = jnp.where(positions < limit[:, :1], 0.0, MASKED)
        parent_low = parent.astype(jnp.bfloat16)

        def scores_of(g):
            if at_once:
                arrange_keys(g)
            query = recv_ref[part, pl.ds(g * head_span, head_span), :].reshape(rows, HEAD_DIM)
            query = jnp.concatenate(
                [jnp.where(parent_low == p, query, jnp.zeros_like(query)) for p in range(parents)], axis=1
            )
            return lax.dot_general(query, key_ref[g], NT, preferred_element_type=jnp.float32)

        def softmax_of(scores):
            scores = scores + bias
            top = jnp.max(scores, axis=1, keepdims=True)
            terms = jnp.exp2((scores - top) * (SCALE * LOG2_E))
            return terms.astype(jnp.bfloat16), top, jnp.sum(terms, axis=1, keepdims=True)

        def blended_of(g, weights):
            if at_once:
                arrange_values(g)
            both = jnp.dot(weights, value_ref[g], preferred_element_type=jnp.float32)
            blended = both[:, :HEAD_DIM]
            for p in range(1, parents):
                blended = jnp.where(parent == p, both[:, p * HEAD_DIM : (p + 1) * HEAD_DIM], blended)
            return blended

        scores, softmaxes, blends = {}, {}, {}
        for g in range(KV_HEADS + 2):
            if g < KV_HEADS:
                scores[g] = scores_of(g)
            if 0 <= g - 1 < KV_HEADS:
                softmaxes[g - 1] = softmax_of(scores[g - 1])
            if 0 <= g - 2 < KV_HEADS:
                blends[g - 2] = blended_of(g - 2, softmaxes[g - 2][0])
        stats = jnp.zeros((rows, HEAD_DIM), jnp.float32)
        for g in heads:
            coded, factor = coded_rows(blends[g])
            out_ref[part, pl.ds(g * head_span, head_span), :] = coded.reshape(chunk, head_span, HEAD_DIM)
            for k, value in enumerate((softmaxes[g][1], softmaxes[g][2], factor)):
                stats = jnp.where(lanes == k * KV_HEADS + g, value, stats)
        flat = coded_stats(stats)
        for j in range(chunk):
            first = j * head_span // HEAD_DIM * HEAD_DIM
            piece = flat[:, first : first + HEAD_DIM]
            out_ref[c * chunk + j, pl.ds(KV_HEADS * head_span, STAT_ROWS), :] = piece
        return carry

    lax.fori_loop(0, sources // chunk, body, 0, unroll=sources == chunk)
    spare_copy.wait()


def fill_suffix_bias(pages_ref, len_ref, bias_ref, last_of):
    page_count, count = pages_ref.shape
    pages, lengths = pages_ref[...], len_ref[...]
    row, lane = iota((PAGE, HEAD_DIM), 0), iota((PAGE, HEAD_DIM), 1)
    for r in range(count):
        for i in range(page_count):
            keep = (lane // 2 == r) & (row + i * PAGE <= last_of(lengths[0, r], lane % 2))
            start = pl.multiple_of(pages[i, r] * PAGE, PAGE)
            bias_ref[pl.ds(start, PAGE), :] = jnp.where(keep, 0.0, MASKED).astype(jnp.bfloat16)


def own_pick(count):
    rows = count * HEAD_ROWS
    row, lane = iota((rows, HEAD_DIM), 0), iota((rows, HEAD_DIM), 1)
    return jnp.where(lane == (row // HEAD_ROWS) * 2 + row % 2, 1.0, 0.0).astype(jnp.bfloat16)


def prefill_kernel(pages_ref, len_ref, query_ref, store_ref, out_ref, bias_ref):
    count = query_ref.shape[0]
    rows = count * HEAD_ROWS
    fill_suffix_bias(pages_ref, len_ref, bias_ref, lambda length, t: length - 2 + t)
    pick = own_pick(count)
    for g in range(KV_HEADS):
        query = query_ref[:, pl.ds(g * HEAD_ROWS, HEAD_ROWS), :].reshape(rows, HEAD_DIM)
        keys = store_ref[:, pl.ds(g * HEAD_DIM, HEAD_DIM)]
        values = store_ref[:, pl.ds(KEY_WIDTH + g * HEAD_DIM, HEAD_DIM)]
        scores = lax.dot_general(
            jnp.concatenate([query, pick], axis=1),
            jnp.concatenate([keys, bias_ref[...]], axis=1),
            NT,
            preferred_element_type=jnp.float32,
        ) * SCALE
        terms = jnp.exp(scores - jnp.max(scores, axis=1, keepdims=True))
        total = jnp.sum(terms, axis=1, keepdims=True)
        blended = jnp.dot(terms.astype(jnp.bfloat16), values, preferred_element_type=jnp.float32)
        out_ref[:, pl.ds(g * HEAD_ROWS, HEAD_ROWS), :] = (
            (blended / total).astype(jnp.bfloat16).reshape(count, HEAD_ROWS, HEAD_DIM)
        )


def local_kernel(cap, pages_ref, len_ref, query_ref, store_ref, step_ref, spare_ref, out_ref, bias_ref):
    count = query_ref.shape[0]
    rows = count * HEAD_ROWS
    head_span = cap * HEAD_ROWS
    blocks = count // cap
    fill_suffix_bias(pages_ref, len_ref, bias_ref, lambda length, t: length - 1)
    steps = 2 * count
    step_pad = -steps % HEAD_DIM
    key_row, lane = iota((steps + step_pad, HEAD_DIM), 0), iota((steps + step_pad, HEAD_DIM), 1)
    seen = (key_row // 2 == lane // 2) & (key_row % 2 <= lane % 2) & (key_row < steps)
    step_bias = jnp.where(seen, 0.0, MASKED).astype(jnp.bfloat16)
    pad = jnp.zeros((step_pad, HEAD_DIM), jnp.bfloat16)

    step_tiles = [step_ref[r] for r in range(count)]

    def step_rows(c):
        return jnp.concatenate([step[2 * c : 2 * c + 2, :] for step in step_tiles] + [pad], axis=0)

    pick = own_pick(count)
    lanes = iota((rows, HEAD_DIM), 1)
    stats = jnp.zeros((rows, HEAD_DIM), jnp.float32)
    for g in range(KV_HEADS):
        query = query_ref[:, pl.ds(g * HEAD_ROWS, HEAD_ROWS), :].reshape(rows, HEAD_DIM)
        query = jnp.concatenate([query, pick], axis=1)
        keys = jnp.concatenate([store_ref[:, pl.ds(g * HEAD_DIM, HEAD_DIM)], bias_ref[...]], axis=1)
        step_keys = jnp.concatenate([step_rows(g), step_bias], axis=1)
        values = store_ref[:, pl.ds(KEY_WIDTH + g * HEAD_DIM, HEAD_DIM)]
        step_values = step_rows(KV_HEADS + g)
        scores = lax.dot_general(query, keys, NT, preferred_element_type=jnp.float32)
        step_scores = lax.dot_general(query, step_keys, NT, preferred_element_type=jnp.float32)
        top = jnp.maximum(
            jnp.max(scores, axis=1, keepdims=True), jnp.max(step_scores, axis=1, keepdims=True)
        )
        terms = jnp.exp2((scores - top) * (SCALE * LOG2_E))
        step_terms = jnp.exp2((step_scores - top) * (SCALE * LOG2_E))
        total = jnp.sum(terms, axis=1, keepdims=True) + jnp.sum(step_terms, axis=1, keepdims=True)
        blended = jnp.dot(terms.astype(jnp.bfloat16), values, preferred_element_type=jnp.float32)
        blended = blended + jnp.dot(
            step_terms.astype(jnp.bfloat16), step_values, preferred_element_type=jnp.float32
        )
        coded, factor = coded_rows(blended)
        out_ref[:, pl.ds(g * head_span, head_span), :] = coded.reshape(blocks, head_span, HEAD_DIM)
        for k, value in enumerate((top, total, factor)):
            stats = jnp.where(lanes == k * KV_HEADS + g, value, stats)
    flat = coded_stats(stats)
    for j in range(rows // HEAD_DIM):
        out_ref[j, pl.ds(KV_HEADS * head_span, STAT_ROWS), :] = flat[:, j * HEAD_DIM : (j + 1) * HEAD_DIM]


def spread_rows(rows):
    high = rows.astype(jnp.bfloat16)
    rest = rows - high.astype(jnp.float32)
    middle = rest.astype(jnp.bfloat16)
    low = (rest - middle.astype(jnp.float32)).astype(jnp.bfloat16)
    count = rows.shape[0]
    shape = (3 * count, count * HEAD_DIM)
    chosen = iota(shape, 0) % count == iota(shape, 1) // HEAD_DIM
    return lax.dot_general(
        jnp.concatenate([high, middle, low], axis=0),
        jnp.where(chosen, 1.0, 0.0).astype(jnp.bfloat16),
        (((0,), (0,)), ((), ())),
        preferred_element_type=jnp.float32,
    )


def merge_kernel(cap, owner_ref, rank_ref, back_ref, own_ref, out_hbm, out_ref, decoded_ref, sems):
    count = out_ref.shape[0]
    step = count // sems.shape[0]

    def put(k):
        part = pl.ds(k * step, step)
        return pltpu.make_async_copy(out_ref.at[part], out_hbm.at[part], sems.at[k])

    rows = count * HEAD_ROWS
    head_span = cap * HEAD_ROWS
    stat_span = pl.ds(KV_HEADS * head_span, STAT_ROWS)
    decoded_ref[...] = decoded_stats(back_ref[:, stat_span, :])
    own = jnp.concatenate([decoded_stats(own_ref[j, stat_span, :]) for j in range(rows // HEAD_DIM)], axis=1)

    names, ranks = owner_ref[...], rank_ref[...]
    names, ranks = [names[0, r] for r in range(count)], [ranks[0, r] for r in range(count)]
    here = lax.rem(lax.axis_index("seq") * head_span, HEAD_DIM)
    per_tile = HEAD_DIM // HEAD_ROWS
    place = iota((2 * KV_HEADS, HEAD_DIM), 1) // HEAD_ROWS
    tiles = []
    for first in range(0, count, per_tile):
        tile = jnp.zeros((2 * KV_HEADS, HEAD_DIM), jnp.float32)
        for r in range(first, min(first + per_tile, count)):
            shift = lax.rem((r - first) * HEAD_ROWS - ranks[r] * HEAD_ROWS - here + 2 * HEAD_DIM, HEAD_DIM)
            tile = jnp.where(place == r - first, pltpu.roll(decoded_ref[names[r]], shift, 1), tile)
        tiles.append(tile)
    flat = jnp.concatenate(tiles, axis=1)[:, :rows]
    part_top, own_top = flat[:KV_HEADS], own[:KV_HEADS]
    top = jnp.maximum(own_top, part_top)
    own_weight, part_weight = jnp.exp(own_top - top), jnp.exp(part_top - top)
    inverse = 1.0 / (own_weight + part_weight)
    weights = [own[KV_HEADS:] * own_weight * inverse, flat[KV_HEADS:] * part_weight * inverse]
    weights = spread_rows(jnp.concatenate(weights, axis=0))
    for r in range(count):
        span = slice(r * HEAD_ROWS, (r + 1) * HEAD_ROWS)
        for g in range(KV_HEADS):
            start = pl.multiple_of(g * head_span + ranks[r] * HEAD_ROWS, HEAD_ROWS)
            part = back_ref[names[r], pl.ds(start, HEAD_ROWS), :].astype(jnp.int32).astype(jnp.float32)
            own_start = g * head_span + r % cap * HEAD_ROWS
            own_part = own_ref[r // cap, pl.ds(own_start, HEAD_ROWS), :].astype(jnp.int32).astype(jnp.float32)
            merged = own_part * weights[span, g * HEAD_DIM : (g + 1) * HEAD_DIM]
            k = KV_HEADS + g
            merged = merged + part * weights[span, k * HEAD_DIM : (k + 1) * HEAD_DIM]
            out_ref[r, pl.ds(g * HEAD_ROWS, HEAD_ROWS), :] = merged.astype(jnp.bfloat16)
        if (r + 1) % step == 0:
            put(r // step).start()
    for k in range(count // step):
        put(k).wait()


def call(kernel, out_shape, arrays, scratch, cost=None, in_space=pltpu.VMEM, out_space=pltpu.VMEM, grant=VMEM_BYTES):
    take = pl.BlockSpec(memory_space=in_space)
    if not isinstance(out_space, tuple):
        out_space = jax.tree.map(lambda _: out_space, out_shape)
    return pl.pallas_call(
        kernel,
        out_shape=out_shape,
        in_specs=[take] * len(arrays),
        out_specs=jax.tree.map(lambda space: pl.BlockSpec(memory_space=space), out_space),
        cost_estimate=cost,
        scratch_shapes=scratch,
        compiler_params=pltpu.CompilerParams(vmem_limit_bytes=grant),
    )(*arrays)


def head_rows(tokens):
    count, pair, width = tokens.shape
    blocks = tokens.reshape(count, pair, width // HEAD_DIM, HEAD_DIM)
    return blocks.transpose(0, 2, 1, 3).reshape(count, -1, HEAD_DIM)


def local(
    kv_store, queries, step_kv, suffix_pages, suffix_len, owner, parent_id, parent_pages, parent_len
):
    decoding = lax.axis_index("role") == 1
    seq_count = lax.axis_size("seq")
    store = kv_store[0]
    count, pair, width = queries.shape[1:]
    cap = max(2, 2 * count // seq_count)
    head_span = cap * HEAD_ROWS
    chunk = max(1, min(seq_count, 512 // head_span))
    query_rows = head_rows(queries[0])
    owner_row, parent_row = owner.reshape(1, -1), parent_id.reshape(1, -1)
    parent_tables = (parent_pages, parent_len.reshape(1, -1))
    suffix_tables = (suffix_pages.T, suffix_len.reshape(1, -1))
    token_rows = store.shape[0]

    sent = jax.ShapeDtypeStruct((seq_count, KV_HEADS * head_span + 16, HEAD_DIM), jnp.bfloat16)
    answer = jax.ShapeDtypeStruct((seq_count, KV_HEADS * head_span + STAT_ROWS, HEAD_DIM), jnp.int16)
    own_part = jax.ShapeDtypeStruct((count // cap, *answer.shape[1:]), answer.dtype)
    result = jax.ShapeDtypeStruct(query_rows.shape, jnp.bfloat16)
    bias = pltpu.VMEM((token_rows, HEAD_DIM), jnp.bfloat16)
    rows = count * HEAD_ROWS
    part = (KV_HEADS, rows, HEAD_DIM)

    def exchange(block):
        return lax.all_to_all(block, "seq", split_axis=0, concat_axis=0, tiled=True)

    def tokens_of(rows):
        return rows.reshape(count, width // HEAD_DIM, pair, HEAD_DIM).transpose(0, 2, 1, 3).reshape(
            1, count, pair, width
        )

    def like(arrays):
        return tuple(jax.ShapeDtypeStruct(a.shape, a.dtype) for a in arrays)

    def zeros(shapes):
        return tuple(jnp.zeros(a.shape, a.dtype) for a in shapes)

    handed = (sent, *like((owner_row, owner_row, *parent_tables)))

    def pack(query_rows):
        return call(
            functools.partial(pack_kernel, cap),
            handed,
            (query_rows, owner_row, parent_row, *parent_tables),
            [
                pltpu.VMEM(query_rows.shape, jnp.bfloat16),
                pltpu.VMEM(parent_row.shape, jnp.int32),
                pltpu.VMEM((seq_count, 16, HEAD_DIM), jnp.float32),
                pltpu.SemaphoreType.DMA((3 + len(parent_tables),)),
            ],
            in_space=pl.ANY,
        )

    packed, owner_row, rank_row, *parent_tables = lax.cond(decoding, pack, lambda _: call(zero_kernel, handed, (), []), query_rows)
    query_after, packed = lax.optimization_barrier((query_rows, packed))
    decode_query = lax.ppermute(query_after, "role", [(0, 1), (1, 0)])

    def send(packed):
        return exchange(packed), *zeros(suffix_tables)

    def hand_on(packed):
        return jnp.zeros_like(packed), *call(hand_kernel, like(suffix_tables), suffix_tables, [])

    received, *suffix_tables = lax.cond(decoding, send, hand_on, packed)

    def answer_queries(received, decode_query):
        parents, page_count = parent_pages.shape
        beside = (KV_HEADS, page_count * PAGE, parents * HEAD_DIM)
        return call(
            functools.partial(parent_kernel, cap, chunk),
            (answer, own_part),
            (*parent_tables, received, store),
            [
                pltpu.VMEM(own_part.shape, jnp.int16),
                pltpu.VMEM(beside, jnp.bfloat16),
                pltpu.VMEM(beside, jnp.bfloat16),
                pltpu.SemaphoreType.DMA,
            ],
            out_space=(pltpu.VMEM, pl.ANY),
        )

    def attend_own(received, decode_query):
        return call(
            functools.partial(local_kernel, cap),
            (answer, own_part),
            (*suffix_tables, decode_query, store, head_rows(step_kv)),
            [bias],
        )

    parts, own = lax.cond(decoding, answer_queries, attend_own, received, decode_query)
    own = lax.ppermute(own, "role", [(0, 1), (1, 0)])
    back = lax.cond(decoding, exchange, lambda block: jnp.zeros_like(block), parts)

    def merge(back, own, query_rows):
        return tokens_of(
            call(
                functools.partial(merge_kernel, cap),
                result,
                (owner_row, rank_row, back, own),
                [
                    pltpu.VMEM(result.shape, jnp.bfloat16),
                    pltpu.VMEM((seq_count, 2 * KV_HEADS, HEAD_DIM), jnp.float32),
                    pltpu.SemaphoreType.DMA((4 if count % 4 == 0 else 1,)),
                ],
                out_space=pl.ANY,
            )
        )

    def prefill(back, own, query_rows):
        return tokens_of(call(prefill_kernel, result, (*suffix_tables, query_rows, store), [bias], grant=PREFILL_VMEM_BYTES))

    return lax.cond(decoding, merge, prefill, back, own, query_rows)


def solution(mesh):
    in_specs = (
        P("role", ("groups", "seq"), None),
        P("role", ("groups", "seq"), None, None),
        P(("groups", "seq"), None, None),
        P(("groups", "seq"), None),
        P(("groups", "seq")),
        P(("groups", "seq"), None),
        P(("groups", "seq")),
        P(("groups", "seq"), None),
        P(("groups", "seq")),
    )
    out_specs = P("role", ("groups", "seq"), None, None)
    return jax.shard_map(local, mesh=mesh, in_specs=in_specs, out_specs=out_specs, check_vma=False)
```

```python
import functools

import jax
import jax.numpy as jnp
from jax import lax
from jax.experimental import pallas as pl
from jax.experimental.pallas import tpu as pltpu
from jax.sharding import PartitionSpec as P

HEAD_DIM = 128
KV_HEADS = 4
GROUP = 8
PAGE = 16
HEAD_ROWS = 2 * GROUP
KEY_WIDTH = KV_HEADS * HEAD_DIM
SCALE = HEAD_DIM ** (-0.5)
MASKED = -1e30
STAT_ROWS = 4 * KV_HEADS
LOG_STEPS = 4.0
SCALE_STEPS = 128.0
CODE_TOP = 32600.0
LOG2_E = 1.4426950408889634
VMEM_BYTES = 48 * 1024 * 1024
PREFILL_VMEM_BYTES = (64 * 1024 - 1150) * 1024

NT = (((1,), (1,)), ((), ()))


def iota(shape, dim):
    return lax.broadcasted_iota(jnp.int32, shape, dim)


def slot_ranks(owner_ref, cap, owners):
    owner = owner_ref[...]
    bits = cap.bit_length()
    per_word = 30 // bits
    words = [jnp.int32(0)] * -(-owners // per_word)
    names, ranks = [], []
    for r in range(owner.shape[1]):
        name = owner[0, r]
        word, rank = name // per_word if len(words) > 1 else 0, jnp.int32(0)
        shift = (name - word * per_word) * bits
        for k, counts in enumerate(words):
            here = (word == k) if len(words) > 1 else True
            count = (counts >> shift) & ((1 << bits) - 1)
            step = jnp.int32(1) << shift
            if len(words) > 1:
                count, step = jnp.where(here, count, 0), jnp.where(here, step, 0)
            rank = rank + count
            words[k] = counts + step
        names.append(name)
        ranks.append(rank)
    return names, ranks


def pack_kernel(cap, query_hbm, owner_hbm, parent_hbm, *refs):
    *refs, query_ref, parent_ref, meta_ref, sems = refs
    tables, (out_ref, owner_ref, *copies) = refs[: len(refs) // 2 - 1], refs[len(refs) // 2 - 1 :]
    moves = [(owner_hbm, owner_ref), (parent_hbm, parent_ref), (query_hbm, query_ref), *zip(tables, copies)]
    moves = [pltpu.make_async_copy(src, dst, sems.at[k]) for k, (src, dst) in enumerate(moves)]
    for move in moves:
        move.start()
    count = query_ref.shape[0]
    head_span = cap * HEAD_ROWS
    out_ref[...] = jnp.zeros_like(out_ref)
    meta_ref[...] = jnp.zeros_like(meta_ref)
    moves[0].wait()
    moves[1].wait()
    parent = parent_ref[...]
    names, ranks = slot_ranks(owner_ref, cap, out_ref.shape[0])
    for r in range(count):
        meta_ref[names[r], pl.ds(ranks[r], 1), :] = jnp.full((1, HEAD_DIM), parent[0, r].astype(jnp.float32))
    out_ref[:, pl.ds(KV_HEADS * head_span, 16), :] = meta_ref[...].astype(jnp.bfloat16)
    moves[2].wait()
    for r in range(count):
        d, rank = names[r], ranks[r]
        for g in range(KV_HEADS):
            start = pl.multiple_of(g * head_span + rank * HEAD_ROWS, HEAD_ROWS)
            out_ref[d, pl.ds(start, HEAD_ROWS), :] = query_ref[r, pl.ds(g * HEAD_ROWS, HEAD_ROWS), :]
    for move in moves[3:]:
        move.wait()


def zero_kernel(*refs):
    for ref in refs:
        ref[...] = jnp.zeros_like(ref)


def hand_kernel(*refs):
    half = len(refs) // 2
    for table, copy in zip(refs[:half], refs[half:]):
        copy[...] = table[...]


def two_codes(values, steps):
    scaled = values * steps
    whole = jnp.floor(scaled)
    rest = jnp.minimum(jnp.floor((scaled - whole) * 65536.0 + 0.5), 65535.0) - 32768.0
    return whole, rest


def from_codes(whole, rest, steps):
    return (whole + (rest + 32768.0) * (1.0 / 65536.0)) * (1.0 / steps)


def coded_rows(blended):
    reach = jnp.maximum(jnp.max(jnp.abs(blended), axis=1, keepdims=True), 1e-30)
    factor = pltpu.reciprocal(reach, approx=True) * CODE_TOP
    return jnp.round(blended * factor).astype(jnp.int32).astype(jnp.int16), factor


def coded_stats(stats):
    flat = stats.T
    top, total, factor = (flat[k * KV_HEADS : (k + 1) * KV_HEADS, :] for k in range(3))
    codes = two_codes(top * SCALE + jnp.log(total), LOG_STEPS)
    codes += two_codes(-jnp.log2(factor * total), SCALE_STEPS)
    return jnp.concatenate(codes, axis=0).astype(jnp.int32).astype(jnp.int16)


def decoded_stats(codes):
    codes = codes.astype(jnp.int32).astype(jnp.float32)
    codes = [codes[..., k * KV_HEADS : (k + 1) * KV_HEADS, :] for k in range(4)]
    log_total = from_codes(codes[0], codes[1], LOG_STEPS)
    return jnp.concatenate([log_total, jnp.exp2(from_codes(codes[2], codes[3], SCALE_STEPS))], axis=-2)


def parent_kernel(
    cap, chunk, pages_ref, len_ref, recv_ref, store_ref, out_ref, spare_hbm, spare_ref, key_ref, value_ref, sem
):
    spare_ref[...] = jnp.zeros_like(spare_ref)
    spare_copy = pltpu.make_async_copy(spare_ref, spare_hbm, sem)
    spare_copy.start()
    parents, page_count = pages_ref.shape
    pages, lengths = pages_ref[...], len_ref[...]
    sources = recv_ref.shape[0]
    head_span = cap * HEAD_ROWS
    tokens = page_count * PAGE
    heads = range(KV_HEADS)
    starts = [[pl.multiple_of(pages[p, i] * PAGE, PAGE) for i in range(page_count)] for p in range(parents)]

    def arrange(target_ref, g, column):
        for p in range(parents):
            for i in range(page_count):
                span = (g, pl.ds(i * PAGE, PAGE), pl.ds(p * HEAD_DIM, HEAD_DIM))
                target_ref[span] = store_ref[pl.ds(starts[p][i], PAGE), pl.ds(column, HEAD_DIM)]

    def arrange_keys(g):
        arrange(key_ref, g, g * HEAD_DIM)

    def arrange_values(g):
        arrange(value_ref, g, KEY_WIDTH + g * HEAD_DIM)

    at_once = sources == chunk
    if not at_once:
        for g in heads:
            arrange_keys(g)
            arrange_values(g)

    rows = chunk * head_span
    lanes = iota((rows, HEAD_DIM), 1)
    positions = iota((rows, tokens), 1)

    def body(c, carry):
        part = pl.ds(c * chunk, chunk)
        meta = recv_ref[part, pl.ds(KV_HEADS * head_span, 16), :].astype(jnp.float32)
        picks = [
            jnp.broadcast_to(meta[:, s : s + 1, :], (chunk, HEAD_ROWS, HEAD_DIM)) for s in range(cap)
        ]
        parent = jnp.concatenate(picks, axis=1).reshape(rows, HEAD_DIM)
        limit = jnp.full((rows, HEAD_DIM), lengths[0, 0], jnp.int32)
        for p in range(1, parents):
            limit = jnp.where(parent == p, lengths[0, p], limit)
        bias = jnp.where(positions < limit[:, :1], 0.0, MASKED)
        parent_low = parent.astype(jnp.bfloat16)

        def scores_of(g):
            if at_once:
                arrange_keys(g)
            query = recv_ref[part, pl.ds(g * head_span, head_span), :].reshape(rows, HEAD_DIM)
            query = jnp.concatenate(
                [jnp.where(parent_low == p, query, jnp.zeros_like(query)) for p in range(parents)], axis=1
            )
            return lax.dot_general(query, key_ref[g], NT, preferred_element_type=jnp.float32)

        def softmax_of(scores):
            scores = scores + bias
            top = jnp.max(scores, axis=1, keepdims=True)
            terms = jnp.exp2((scores - top) * (SCALE * LOG2_E))
            return terms.astype(jnp.bfloat16), top, jnp.sum(terms, axis=1, keepdims=True)

        def blended_of(g, weights):
            if at_once:
                arrange_values(g)
            both = jnp.dot(weights, value_ref[g], preferred_element_type=jnp.float32)
            blended = both[:, :HEAD_DIM]
            for p in range(1, parents):
                blended = jnp.where(parent == p, both[:, p * HEAD_DIM : (p + 1) * HEAD_DIM], blended)
            return blended

        scores, softmaxes, blends = {}, {}, {}
        for g in heads:
            scores[g] = scores_of(g)
        for g in heads:
            softmaxes[g] = softmax_of(scores[g])
        for g in heads:
            blends[g] = blended_of(g, softmaxes[g][0])
        stats = jnp.zeros((rows, HEAD_DIM), jnp.float32)
        for g in heads:
            coded, factor = coded_rows(blends[g])
            out_ref[part, pl.ds(g * head_span, head_span), :] = coded.reshape(chunk, head_span, HEAD_DIM)
            for k, value in enumerate((softmaxes[g][1], softmaxes[g][2], factor)):
                stats = jnp.where(lanes == k * KV_HEADS + g, value, stats)
        flat = coded_stats(stats)
        for j in range(chunk):
            first = j * head_span // HEAD_DIM * HEAD_DIM
            piece = flat[:, first : first + HEAD_DIM]
            out_ref[c * chunk + j, pl.ds(KV_HEADS * head_span, STAT_ROWS), :] = piece
        return carry

    lax.fori_loop(0, sources // chunk, body, 0, unroll=sources == chunk)
    spare_copy.wait()


def fill_suffix_bias(pages_ref, len_ref, bias_ref, last_of):
    page_count, count = pages_ref.shape
    pages, lengths = pages_ref[...], len_ref[...]
    row, lane = iota((PAGE, HEAD_DIM), 0), iota((PAGE, HEAD_DIM), 1)
    for r in range(count):
        for i in range(page_count):
            keep = (lane // 2 == r) & (row + i * PAGE <= last_of(lengths[0, r], lane % 2))
            start = pl.multiple_of(pages[i, r] * PAGE, PAGE)
            bias_ref[pl.ds(start, PAGE), :] = jnp.where(keep, 0.0, MASKED).astype(jnp.bfloat16)


def own_pick(count):
    rows = count * HEAD_ROWS
    row, lane = iota((rows, HEAD_DIM), 0), iota((rows, HEAD_DIM), 1)
    return jnp.where(lane == (row // HEAD_ROWS) * 2 + row % 2, 1.0, 0.0).astype(jnp.bfloat16)


def prefill_kernel(pages_ref, len_ref, query_ref, store_ref, out_ref, bias_ref):
    count = query_ref.shape[0]
    rows = count * HEAD_ROWS
    fill_suffix_bias(pages_ref, len_ref, bias_ref, lambda length, t: length - 2 + t)
    pick = own_pick(count)
    for g in range(KV_HEADS):
        query = query_ref[:, pl.ds(g * HEAD_ROWS, HEAD_ROWS), :].reshape(rows, HEAD_DIM)
        keys = store_ref[:, pl.ds(g * HEAD_DIM, HEAD_DIM)]
        values = store_ref[:, pl.ds(KEY_WIDTH + g * HEAD_DIM, HEAD_DIM)]
        scores = lax.dot_general(
            jnp.concatenate([query, pick], axis=1),
            jnp.concatenate([keys, bias_ref[...]], axis=1),
            NT,
            preferred_element_type=jnp.float32,
        ) * SCALE
        terms = jnp.exp(scores - jnp.max(scores, axis=1, keepdims=True))
        total = jnp.sum(terms, axis=1, keepdims=True)
        blended = jnp.dot(terms.astype(jnp.bfloat16), values, preferred_element_type=jnp.float32)
        out_ref[:, pl.ds(g * HEAD_ROWS, HEAD_ROWS), :] = (
            (blended / total).astype(jnp.bfloat16).reshape(count, HEAD_ROWS, HEAD_DIM)
        )


def local_kernel(cap, pages_ref, len_ref, query_ref, store_ref, step_ref, spare_ref, out_ref, bias_ref):
    count = query_ref.shape[0]
    rows = count * HEAD_ROWS
    head_span = cap * HEAD_ROWS
    blocks = count // cap
    fill_suffix_bias(pages_ref, len_ref, bias_ref, lambda length, t: length - 1)
    steps = 2 * count
    step_pad = -steps % HEAD_DIM
    key_row, lane = iota((steps + step_pad, HEAD_DIM), 0), iota((steps + step_pad, HEAD_DIM), 1)
    seen = (key_row // 2 == lane // 2) & (key_row % 2 <= lane % 2) & (key_row < steps)
    step_bias = jnp.where(seen, 0.0, MASKED).astype(jnp.bfloat16)
    pad = jnp.zeros((step_pad, HEAD_DIM), jnp.bfloat16)

    step_tiles = [step_ref[r] for r in range(count)]

    def step_rows(c):
        return jnp.concatenate([step[2 * c : 2 * c + 2, :] for step in step_tiles] + [pad], axis=0)

    pick = own_pick(count)
    lanes = iota((rows, HEAD_DIM), 1)
    stats = jnp.zeros((rows, HEAD_DIM), jnp.float32)
    for g in range(KV_HEADS):
        query = query_ref[:, pl.ds(g * HEAD_ROWS, HEAD_ROWS), :].reshape(rows, HEAD_DIM)
        query = jnp.concatenate([query, pick], axis=1)
        keys = jnp.concatenate([store_ref[:, pl.ds(g * HEAD_DIM, HEAD_DIM)], bias_ref[...]], axis=1)
        step_keys = jnp.concatenate([step_rows(g), step_bias], axis=1)
        values = store_ref[:, pl.ds(KEY_WIDTH + g * HEAD_DIM, HEAD_DIM)]
        step_values = step_rows(KV_HEADS + g)
        scores = lax.dot_general(query, keys, NT, preferred_element_type=jnp.float32)
        step_scores = lax.dot_general(query, step_keys, NT, preferred_element_type=jnp.float32)
        top = jnp.maximum(
            jnp.max(scores, axis=1, keepdims=True), jnp.max(step_scores, axis=1, keepdims=True)
        )
        terms = jnp.exp2((scores - top) * (SCALE * LOG2_E))
        step_terms = jnp.exp2((step_scores - top) * (SCALE * LOG2_E))
        total = jnp.sum(terms, axis=1, keepdims=True) + jnp.sum(step_terms, axis=1, keepdims=True)
        blended = jnp.dot(terms.astype(jnp.bfloat16), values, preferred_element_type=jnp.float32)
        blended = blended + jnp.dot(
            step_terms.astype(jnp.bfloat16), step_values, preferred_element_type=jnp.float32
        )
        coded, factor = coded_rows(blended)
        out_ref[:, pl.ds(g * head_span, head_span), :] = coded.reshape(blocks, head_span, HEAD_DIM)
        for k, value in enumerate((top, total, factor)):
            stats = jnp.where(lanes == k * KV_HEADS + g, value, stats)
    flat = coded_stats(stats)
    for j in range(rows // HEAD_DIM):
        out_ref[j, pl.ds(KV_HEADS * head_span, STAT_ROWS), :] = flat[:, j * HEAD_DIM : (j + 1) * HEAD_DIM]


def spread_rows(rows):
    high = rows.astype(jnp.bfloat16)
    rest = rows - high.astype(jnp.float32)
    middle = rest.astype(jnp.bfloat16)
    low = (rest - middle.astype(jnp.float32)).astype(jnp.bfloat16)
    count = rows.shape[0]
    shape = (3 * count, count * HEAD_DIM)
    chosen = iota(shape, 0) % count == iota(shape, 1) // HEAD_DIM
    return lax.dot_general(
        jnp.concatenate([high, middle, low], axis=0),
        jnp.where(chosen, 1.0, 0.0).astype(jnp.bfloat16),
        (((0,), (0,)), ((), ())),
        preferred_element_type=jnp.float32,
    )


def merge_kernel(cap, owner_ref, back_ref, own_ref, out_hbm, out_ref, decoded_ref, sems):
    count = out_ref.shape[0]
    step = count // sems.shape[0]

    def put(k):
        part = pl.ds(k * step, step)
        return pltpu.make_async_copy(out_ref.at[part], out_hbm.at[part], sems.at[k])

    rows = count * HEAD_ROWS
    head_span = cap * HEAD_ROWS
    stat_span = pl.ds(KV_HEADS * head_span, STAT_ROWS)
    decoded_ref[...] = decoded_stats(back_ref[:, stat_span, :])
    own = jnp.concatenate([decoded_stats(own_ref[j, stat_span, :]) for j in range(rows // HEAD_DIM)], axis=1)

    names, ranks = slot_ranks(owner_ref, cap, back_ref.shape[0])
    here = lax.rem(lax.axis_index("seq") * head_span, HEAD_DIM)
    per_tile = HEAD_DIM // HEAD_ROWS
    place = iota((2 * KV_HEADS, HEAD_DIM), 1) // HEAD_ROWS
    tiles = []
    for first in range(0, count, per_tile):
        tile = jnp.zeros((2 * KV_HEADS, HEAD_DIM), jnp.float32)
        for r in range(first, min(first + per_tile, count)):
            shift = lax.rem((r - first) * HEAD_ROWS - ranks[r] * HEAD_ROWS - here + 2 * HEAD_DIM, HEAD_DIM)
            tile = jnp.where(place == r - first, pltpu.roll(decoded_ref[names[r]], shift, 1), tile)
        tiles.append(tile)
    flat = jnp.concatenate(tiles, axis=1)[:, :rows]
    part_top, own_top = flat[:KV_HEADS], own[:KV_HEADS]
    top = jnp.maximum(own_top, part_top)
    own_weight, part_weight = jnp.exp(own_top - top), jnp.exp(part_top - top)
    inverse = 1.0 / (own_weight + part_weight)
    weights = [own[KV_HEADS:] * own_weight * inverse, flat[KV_HEADS:] * part_weight * inverse]
    weights = spread_rows(jnp.concatenate(weights, axis=0))
    for r in range(count):
        span = slice(r * HEAD_ROWS, (r + 1) * HEAD_ROWS)
        for g in range(KV_HEADS):
            start = pl.multiple_of(g * head_span + ranks[r] * HEAD_ROWS, HEAD_ROWS)
            part = back_ref[names[r], pl.ds(start, HEAD_ROWS), :].astype(jnp.int32).astype(jnp.float32)
            own_start = g * head_span + r % cap * HEAD_ROWS
            own_part = own_ref[r // cap, pl.ds(own_start, HEAD_ROWS), :].astype(jnp.int32).astype(jnp.float32)
            merged = own_part * weights[span, g * HEAD_DIM : (g + 1) * HEAD_DIM]
            k = KV_HEADS + g
            merged = merged + part * weights[span, k * HEAD_DIM : (k + 1) * HEAD_DIM]
            out_ref[r, pl.ds(g * HEAD_ROWS, HEAD_ROWS), :] = merged.astype(jnp.bfloat16)
        if (r + 1) % step == 0:
            put(r // step).start()
    for k in range(count // step):
        put(k).wait()


def call(kernel, out_shape, arrays, scratch, cost=None, in_space=pltpu.VMEM, out_space=pltpu.VMEM, grant=VMEM_BYTES):
    take = pl.BlockSpec(memory_space=in_space)
    if not isinstance(out_space, tuple):
        out_space = jax.tree.map(lambda _: out_space, out_shape)
    return pl.pallas_call(
        kernel,
        out_shape=out_shape,
        in_specs=[take] * len(arrays),
        out_specs=jax.tree.map(lambda space: pl.BlockSpec(memory_space=space), out_space),
        cost_estimate=cost,
        scratch_shapes=scratch,
        compiler_params=pltpu.CompilerParams(vmem_limit_bytes=grant),
    )(*arrays)


def head_rows(tokens):
    count, pair, width = tokens.shape
    blocks = tokens.reshape(count, pair, width // HEAD_DIM, HEAD_DIM)
    return blocks.transpose(0, 2, 1, 3).reshape(count, -1, HEAD_DIM)


def local(
    kv_store, queries, step_kv, suffix_pages, suffix_len, owner, parent_id, parent_pages, parent_len
):
    decoding = lax.axis_index("role") == 1
    seq_count = lax.axis_size("seq")
    store = kv_store[0]
    count, pair, width = queries.shape[1:]
    cap = max(2, 2 * count // seq_count)
    head_span = cap * HEAD_ROWS
    chunk = max(1, min(seq_count, 512 // head_span))
    query_rows = head_rows(queries[0])
    owner_row, parent_row = owner.reshape(1, -1), parent_id.reshape(1, -1)
    parent_tables = (parent_pages, parent_len.reshape(1, -1))
    suffix_tables = (suffix_pages.T, suffix_len.reshape(1, -1))
    token_rows = store.shape[0]

    sent = jax.ShapeDtypeStruct((seq_count, KV_HEADS * head_span + 16, HEAD_DIM), jnp.bfloat16)
    answer = jax.ShapeDtypeStruct((seq_count, KV_HEADS * head_span + STAT_ROWS, HEAD_DIM), jnp.int16)
    own_part = jax.ShapeDtypeStruct((count // cap, *answer.shape[1:]), answer.dtype)
    result = jax.ShapeDtypeStruct(query_rows.shape, jnp.bfloat16)
    bias = pltpu.VMEM((token_rows, HEAD_DIM), jnp.bfloat16)
    rows = count * HEAD_ROWS
    part = (KV_HEADS, rows, HEAD_DIM)

    def exchange(block):
        return lax.all_to_all(block, "seq", split_axis=0, concat_axis=0, tiled=True)

    def tokens_of(rows):
        return rows.reshape(count, width // HEAD_DIM, pair, HEAD_DIM).transpose(0, 2, 1, 3).reshape(
            1, count, pair, width
        )

    def like(arrays):
        return tuple(jax.ShapeDtypeStruct(a.shape, a.dtype) for a in arrays)

    def zeros(shapes):
        return tuple(jnp.zeros(a.shape, a.dtype) for a in shapes)

    handed = (sent, *like((owner_row, *parent_tables)))

    def pack(query_rows):
        return call(
            functools.partial(pack_kernel, cap),
            handed,
            (query_rows, owner_row, parent_row, *parent_tables),
            [
                pltpu.VMEM(query_rows.shape, jnp.bfloat16),
                pltpu.VMEM(parent_row.shape, jnp.int32),
                pltpu.VMEM((seq_count, 16, HEAD_DIM), jnp.float32),
                pltpu.SemaphoreType.DMA((3 + len(parent_tables),)),
            ],
            in_space=pl.ANY,
        )

    packed, owner_row, *parent_tables = lax.cond(decoding, pack, lambda _: call(zero_kernel, handed, (), []), query_rows)
    query_after, packed = lax.optimization_barrier((query_rows, packed))
    decode_query = lax.ppermute(query_after, "role", [(0, 1), (1, 0)])

    def send(packed):
        return exchange(packed), *zeros(suffix_tables)

    def hand_on(packed):
        return jnp.zeros_like(packed), *call(hand_kernel, like(suffix_tables), suffix_tables, [])

    received, *suffix_tables = lax.cond(decoding, send, hand_on, packed)

    def answer_queries(received, decode_query):
        parents, page_count = parent_pages.shape
        beside = (KV_HEADS, page_count * PAGE, parents * HEAD_DIM)
        return call(
            functools.partial(parent_kernel, cap, chunk),
            (answer, own_part),
            (*parent_tables, received, store),
            [
                pltpu.VMEM(own_part.shape, jnp.int16),
                pltpu.VMEM(beside, jnp.bfloat16),
                pltpu.VMEM(beside, jnp.bfloat16),
                pltpu.SemaphoreType.DMA,
            ],
            out_space=(pltpu.VMEM, pl.ANY),
        )

    def attend_own(received, decode_query):
        return call(
            functools.partial(local_kernel, cap),
            (answer, own_part),
            (*suffix_tables, decode_query, store, head_rows(step_kv)),
            [bias],
        )

    parts, own = lax.cond(decoding, answer_queries, attend_own, received, decode_query)
    own = lax.ppermute(own, "role", [(0, 1), (1, 0)])
    back = lax.cond(decoding, exchange, lambda block: jnp.zeros_like(block), parts)

    def merge(back, own, query_rows):
        return tokens_of(
            call(
                functools.partial(merge_kernel, cap),
                result,
                (owner_row, back, own),
                [
                    pltpu.VMEM(result.shape, jnp.bfloat16),
                    pltpu.VMEM((seq_count, 2 * KV_HEADS, HEAD_DIM), jnp.float32),
                    pltpu.SemaphoreType.DMA((4 if count % 4 == 0 else 1,)),
                ],
                out_space=pl.ANY,
            )
        )

    def prefill(back, own, query_rows):
        return tokens_of(call(prefill_kernel, result, (*suffix_tables, query_rows, store), [bias], grant=PREFILL_VMEM_BYTES))

    return lax.cond(decoding, merge, prefill, back, own, query_rows)


def solution(mesh):
    in_specs = (
        P("role", ("groups", "seq"), None),
        P("role", ("groups", "seq"), None, None),
        P(("groups", "seq"), None, None),
        P(("groups", "seq"), None),
        P(("groups", "seq")),
        P(("groups", "seq"), None),
        P(("groups", "seq")),
        P(("groups", "seq"), None),
        P(("groups", "seq")),
    )
    out_specs = P("role", ("groups", "seq"), None, None)
    return jax.shard_map(local, mesh=mesh, in_specs=in_specs, out_specs=out_specs, check_vma=False)
```
